32 devices in a mesh: axial: 4 (over y, x), azim: 8 (over z, core).
Axes of the slice: x: 2, y: 2, z: 4, core: 2. Of those that a mesh axis runs over, the one named last changes fastest.
Arguments:
- density: float32 [64, 64, 512], P(None, 'azim', 'axial'), may hold values from 0.5 to 2
- velocity: float32 [3, 64, 64, 512], P(None, None, 'azim', 'axial'), may hold values from -3 to 3
- pressure: float32 [64, 64, 512], P(None, 'azim', 'axial'), may hold values from 0.4 to 1.5
- axial_metric: float32 [3, 64, 64, 512], P(None, None, 'azim', 'axial'), may hold values from -4 to 4
- azim_metric: float32 [3, 64, 64, 512], P(None, None, 'azim', 'axial'), may hold values from -4 to 4
- volume: float32 [64, 64, 512], P(None, 'azim', 'axial'), may hold values from 0.5 to 2
- radial_term: float32 [5, 64, 64, 512], P(None, None, 'azim', 'axial'), may hold values from -6 to 6
- panel_area: float32 [64, 512], P('azim', 'axial'), may hold values from 0.5 to 2
- observer_ids: int32 [4, 64, 512], P(None, 'azim', 'axial'), may hold values from 0 to 511
- bin_ids: int32 [4, 64, 512], P(None, 'azim', 'axial'), may hold values from 0 to 127
- weight_ids: int32 [4, 64, 512], P(None, 'azim', 'axial'), may hold values from 0 to 255
- bin_weights: float32 [256], replicated, may hold values from 0.2 to 1
Outputs:
- new_state: float32 [5, 64, 64, 512], P(None, None, 'azim', 'axial')
- signals: float32 [512, 128], P(('axial', 'azim'))
The draws below stay inside these ranges and needn't reach their ends.
All inputs are finite; a program needn't handle non-finite values.
Results may differ from the reference program's by a relative error of at most 0.0003.
Values sent between devices are 32-bit elements; how exact they have to be, the bound alone decides.
No kernel may reach another device: no remote copies, remote signals or barrier semaphores. Data moves between devices by JAX's collectives and lax.ppermute only.
A program may use at most 128 MiB of HBM per device.

```python
import math
import jax
import jax.numpy as jnp
from jax import lax

PLANES = 64
OBSERVERS = 512
TIME_BINS = 128
ENTRIES = 4
TABLE = 256
NA = 512
NAZ = 64


def place_ends(array, stream_key, least, largest):
    shape = array.shape
    place = [jax.random.randint(jax.random.fold_in(stream_key, axis), (), 0, shape[axis]) for axis in range(len(shape))]
    array = array.at[tuple(place)].set(least)
    longest = shape.index(max(shape))
    place[longest] = (place[longest] + 1) % shape[longest]
    return array.at[tuple(place)].set(largest)


def levels(rng, shape, cuts, smallest, high):
    factor_of, own = 1.0, jax.random.fold_in(rng, 6)
    for dim, parts in cuts:
        steps = jnp.exp(jax.random.uniform(jax.random.fold_in(own, dim), (parts,), jnp.float32, smallest / len(cuts), high / len(cuts)))
        factor_of = factor_of * jnp.repeat(steps, shape[dim] // parts).reshape([-1 if axis == dim else 1 for axis in range(len(shape))])
    return factor_of


def noise(key, shape, spread, reach, shards=(), kind=jnp.bfloat16):
    values = jax.random.normal(key, shape, jnp.float32) * spread
    if len(shards) > 0:
        values = levels(key, shape, shards, -0.22, 0.18) * values
    return jnp.clip(values, min=-reach, max=reach).astype(kind)


def setup_inputs(seed: int = 0) -> dict:
    key_list = jax.random.split(jax.random.key(seed), 13)
    density = jnp.clip(jnp.exp(math.log(2.0) - 1.3862944 * jax.random.uniform(key_list[0], (PLANES, NAZ, NA), jnp.float32) ** levels(key_list[0], (PLANES, NAZ, NA), ((1, 8), (2, 4)), -0.2, 0.2)), 0.5, 2.0)
    velocity = noise(key_list[1], (3, PLANES, NAZ, NA), 0.5, 3.0, ((2, 8), (3, 4)), jnp.float32)
    pressure = jnp.clip(jnp.exp(math.log(1.5) - 1.3217558 * jax.random.uniform(key_list[2], (PLANES, NAZ, NA), jnp.float32) ** levels(key_list[2], (PLANES, NAZ, NA), ((1, 8), (2, 4)), -0.2, 0.2)), 0.4, 1.5)
    axial_metric = noise(key_list[3], (3, PLANES, NAZ, NA), 1.0, 4.0, ((2, 8), (3, 4)), jnp.float32)
    azim_metric = noise(key_list[4], (3, PLANES, NAZ, NA), 1.0, 4.0, ((2, 8), (3, 4)), jnp.float32)
    volume = jnp.clip(jnp.exp(math.log(2.0) - 1.3862944 * jax.random.uniform(key_list[5], (PLANES, NAZ, NA), jnp.float32) ** levels(key_list[5], (PLANES, NAZ, NA), ((1, 8), (2, 4)), -0.2, 0.2)), 0.5, 2.0)
    radial_term = noise(key_list[6], (5, PLANES, NAZ, NA), 1.0, 6.0, ((2, 8), (3, 4)), jnp.float32)
    panel_area = jnp.clip(jnp.exp(math.log(2.0) - 1.3862944 * jax.random.uniform(key_list[7], (NAZ, NA), jnp.float32) ** levels(key_list[7], (NAZ, NA), ((0, 8), (1, 4)), -0.2, 0.2)), 0.5, 2.0)
    observer_ids = place_ends(jax.random.randint(key_list[8], (ENTRIES, NAZ, NA), 0, OBSERVERS), jax.random.fold_in(key_list[8], 1), 0, OBSERVERS - 1).astype(jnp.int32)
    bin_ids = place_ends(jax.random.randint(key_list[9], (ENTRIES, NAZ, NA), 0, TIME_BINS), jax.random.fold_in(key_list[9], 1), 0, TIME_BINS - 1).astype(jnp.int32)
    weight_ids = place_ends(jax.random.randint(key_list[10], (ENTRIES, NAZ, NA), 0, TABLE), jax.random.fold_in(key_list[10], 1), 0, TABLE - 1).astype(jnp.int32)
    bin_weights = jnp.clip(jax.random.uniform(key_list[11], (TABLE,), jnp.float32, 0.2, 1.0), 0.2, 1.0)
    return dict(density=density, velocity=velocity, pressure=pressure, axial_metric=axial_metric, azim_metric=azim_metric, volume=volume, radial_term=radial_term, panel_area=panel_area, observer_ids=observer_ids, bin_ids=bin_ids, weight_ids=weight_ids, bin_weights=bin_weights)


GAMMA = 1.4
SECTION = 0.25
DERIV_ALPHA = 1.0 / 3.0
FILTER_ALPHA = 0.499
DERIV_A = 14.0 / 9.0
DERIV_B = 1.0 / 9.0

def decay_root(alpha):
    return (-1.0 + math.sqrt(1.0 - 4.0 * alpha * alpha)) / (2.0 * alpha)

def signed_power(base, exponent):
    exponent = jnp.asarray(exponent).astype(jnp.int32)
    parity = jnp.where(exponent % 2 == 0, 1.0, -1.0)
    return parity * jnp.exp(exponent.astype(jnp.float32) * math.log(-base))

def deriv_side(extended, dim):
    length = extended.shape[dim] - 6

    def cells(offset):
        return lax.slice_in_dim(extended, 3 + offset, 3 + offset + length, axis=dim)
    return 0.5 * DERIV_A * (cells(1) - cells(-1)) + 0.25 * DERIV_B * (cells(2) - cells(-2))

def filter_side(extended, dim):
    length = extended.shape[dim] - 6

    def cells(offset):
        return lax.slice_in_dim(extended, 3 + offset, 3 + offset + length, axis=dim)
    beta = FILTER_ALPHA
    coeffs = [(11.0 + 10.0 * beta) / 16.0, (15.0 + 34.0 * beta) / 32.0, (-3.0 + 6.0 * beta) / 16.0, (1.0 - 2.0 * beta) / 32.0]
    total = coeffs[0] * cells(0)
    for shift in range(1, 4):
        total = total + 0.5 * coeffs[shift] * (cells(shift) + cells(-shift))
    return total

def fluxes(density, velocity, pressure, energy, metric, volume):
    contra = metric[0] * velocity[0] + metric[1] * velocity[1] + metric[2] * velocity[2]
    mass_flow = density * contra
    pieces = [volume * mass_flow]
    for comp in range(3):
        pieces.append(volume * (mass_flow * velocity[comp] + metric[comp] * pressure))
    pieces.append(volume * (energy + pressure) * contra)
    return jnp.stack(pieces)

def pad_open(field):
    return jnp.pad(field, ((0, 0), (0, 0), (0, 0), (3, 3)))

def pad_cycle(field):
    return jnp.concatenate([field[:, :, -3:], field, field[:, :, :3]], axis=2)

def open_line(rhs, alpha):
    base = decay_root(alpha)
    factor_g = -alpha / base
    lines = jnp.moveaxis(rhs, 3, 0)

    def forward(carry, row):
        fresh = row + base * carry
        return (fresh, fresh)

    def backward(carry, row):
        fresh = row / factor_g + base * carry
        return (fresh, fresh)
    ignored, upward = lax.scan(forward, jnp.zeros_like(lines[0]), lines)
    ignored, result = lax.scan(backward, jnp.zeros_like(lines[0]), upward, reverse=True)
    return jnp.moveaxis(result, 0, 3)

def cycle_line(rhs, alpha):
    base = decay_root(alpha)
    factor_g = -alpha / base
    lines = jnp.moveaxis(rhs, 2, 0)
    length = lines.shape[0]
    wrap = 1.0 / (1.0 - base ** length)

    def forward(carry, row):
        fresh = row + base * carry
        return (fresh, fresh)
    ignored, upward_zero = lax.scan(forward, jnp.zeros_like(lines[0]), lines)
    steps_ahead = jnp.arange(length, dtype=jnp.int32)
    upward = upward_zero + signed_power(base, steps_ahead + 1)[:, None, None, None] * (upward_zero[-1] * wrap)[None]
    ignored, down_zero = lax.scan(forward, jnp.zeros_like(lines[0]), upward, reverse=True)
    downward = down_zero + signed_power(base, length - steps_ahead)[:, None, None, None] * (down_zero[0] * wrap)[None]
    return jnp.moveaxis(downward / factor_g, 0, 2)

def reference(density, velocity, pressure, axial_metric, azim_metric, volume, radial_term, panel_area, observer_ids, bin_ids, weight_ids, bin_weights):
    energy = pressure / (GAMMA - 1.0) + 0.5 * density * (velocity[0] ** 2 + velocity[1] ** 2 + velocity[2] ** 2)
    state = jnp.concatenate([density[None], density[None] * velocity, energy[None]], axis=0)
    axial_flux = fluxes(density, velocity, pressure, energy, axial_metric, volume)
    azim_flux = fluxes(density, velocity, pressure, energy, azim_metric, volume)
    axial_deriv = open_line(deriv_side(pad_open(axial_flux), 3), DERIV_ALPHA)
    azim_deriv = cycle_line(deriv_side(pad_cycle(azim_flux), 2), DERIV_ALPHA)
    sectioned = state + SECTION * (radial_term - (axial_deriv + azim_deriv) / volume)
    smoothed = open_line(filter_side(pad_open(sectioned), 3), FILTER_ALPHA)
    new_state = cycle_line(filter_side(pad_cycle(smoothed), 2), FILTER_ALPHA)
    surface = new_state[:, 0]
    source = panel_area * (surface[2] + surface[0] - 1.0)
    values = bin_weights[weight_ids] * source[None]
    bucket = observer_ids * TIME_BINS + bin_ids
    signals = jax.ops.segment_sum(values.reshape(-1), bucket.reshape(-1), num_segments=OBSERVERS * TIME_BINS)
    return (new_state, signals.reshape(OBSERVERS, TIME_BINS))
```

```python
import functools
import math

import jax
import jax.numpy as jnp
import numpy as np
from jax import lax
from jax.experimental import pallas as pl
from jax.experimental.pallas import tpu as pltpu
from jax.sharding import PartitionSpec as P

OBSERVERS = 512
TIME_BINS = 128

GAMMA = 1.4
SECTION = 0.25
DERIV_ALPHA = 1.0 / 3.0
FILTER_ALPHA = 0.499
FIELDS = 5
CHUNK = 16
BASIS = 8
VMEM_LIMIT = 48 * 1024 * 1024


def decay_root(alpha):
    return (-1.0 + math.sqrt(1.0 - 4.0 * alpha * alpha)) / (2.0 * alpha)


DERIV_ROOT = decay_root(DERIV_ALPHA)
FILTER_ROOT = decay_root(FILTER_ALPHA)

DERIV_NEAR = 1.0 / 12.0
DERIV_FAR = (
    (25.0 / 36.0) * (DERIV_ROOT - 1.0 / DERIV_ROOT) / (1.0 + 2.0 * DERIV_ALPHA * DERIV_ROOT)
)

_B = FILTER_ALPHA
_EDGE = (1.0 - 2.0 * _B) / 64.0
_Q2 = 1.0 / _B
_Q1 = (-6.0 - _Q2) / _B
_Q0 = (12.0 - _Q1) / _B
_RHO = -8.0 - _Q0
FILTER_MID = _EDGE * (_Q0 + 2.0 * _Q2)
FILTER_ONE = _EDGE * _Q1
FILTER_TWO = _EDGE * _Q2
FILTER_FAR = _EDGE * _RHO / (1.0 + 2.0 * _B * FILTER_ROOT)


def open_operator(length, alpha, side):
    base = decay_root(alpha)
    tri = np.eye(length) + alpha * (np.eye(length, k=1) + np.eye(length, k=-1))
    tri[0, 0] = -alpha / base
    return np.linalg.solve(tri, side)


def deriv_matrix(length):
    return (7.0 / 9.0) * (np.eye(length, k=1) - np.eye(length, k=-1)) + (1.0 / 36.0) * (
        np.eye(length, k=2) - np.eye(length, k=-2)
    )


def filter_matrix(length):
    beta = FILTER_ALPHA
    coeffs = [
        (11.0 + 10.0 * beta) / 16.0,
        (15.0 + 34.0 * beta) / 32.0,
        (-3.0 + 6.0 * beta) / 16.0,
        (1.0 - 2.0 * beta) / 32.0,
    ]
    total = coeffs[0] * np.eye(length)
    for shift in range(1, 4):
        total = total + 0.5 * coeffs[shift] * (np.eye(length, k=shift) + np.eye(length, k=-shift))
    return total


def axial_tables(count, width, alpha, kind):
    length = count * width
    side = deriv_matrix(length) if kind == "deriv" else filter_matrix(length)
    whole = open_operator(length, alpha, side)
    base = decay_root(alpha)
    basis = np.zeros((BASIS, width))
    for edge in range(3):
        basis[edge, edge] = 1.0
        basis[3 + edge, width - 3 + edge] = 1.0
    basis[6] = base ** np.arange(width - 1, -1, -1, dtype=np.float64)
    basis[7] = base ** np.arange(width, dtype=np.float64)
    inverse = np.linalg.pinv(basis)
    own = np.zeros((count, width, width))
    far = np.zeros((count, max(count - 1, 1) * BASIS, width))
    for here in range(count):
        rows = whole[here * width : (here + 1) * width]
        own[here] = rows[:, here * width : (here + 1) * width].T
        if kind == "filter":
            own[here] -= np.eye(width)
        for shift in range(1, count):
            there = (here - shift) % count
            block = rows[:, there * width : (there + 1) * width]
            far[here, (shift - 1) * BASIS : shift * BASIS] = (block @ inverse).T
    return own, basis, far


def halves(table):
    high = np.asarray(table, np.float32).astype(jnp.bfloat16)
    low = (np.asarray(table, np.float64) - high.astype(np.float64)).astype(jnp.bfloat16)
    return np.stack([high, low], axis=-3)


def split(values):
    high = values.astype(jnp.bfloat16)
    return high, (values - high.astype(jnp.float32)).astype(jnp.bfloat16)


def dots(left, right, dims):
    out = None
    for a, b in ((0, 0), (1, 0), (0, 1)):
        part = lax.dot_general(
            left[a], right[b], (dims, ((), ())), preferred_element_type=jnp.float32
        )
        out = part if out is None else out + part
    return out


def outgoing(basis_ref, lines):
    return dots((basis_ref[0], basis_ref[1]), split(lines), ((1,), (1,)))


def incoming(parts, far_ref):
    return dots(split(jnp.concatenate(parts, axis=0)), (far_ref[0], far_ref[1]), ((0,), (0,)))


def own_block(lines, own_ref):
    return dots(split(lines), (own_ref[0], own_ref[1]), ((1,), (0,)))


def tile_state(density, velocity, pressure):
    energy = pressure * (1.0 / (GAMMA - 1.0)) + 0.5 * density * (
        velocity[0] * velocity[0] + velocity[1] * velocity[1] + velocity[2] * velocity[2]
    )
    return energy


def tile_flux(density, velocity, pressure, energy, metric, volume):
    contra = metric[0] * velocity[0] + metric[1] * velocity[1] + metric[2] * velocity[2]
    volume_contra = volume * contra
    mass = density * volume_contra
    push = volume * pressure
    pieces = [mass]
    for comp in range(3):
        pieces.append(mass * velocity[comp] + metric[comp] * push)
    pieces.append((energy + pressure) * volume_contra)
    return pieces


def flux_send_kernel(
    core_ref, density, velocity, pressure, axial_metric, azim_metric, volume, basis, edge, pair, odd, flux
):
    rows = density.shape[1]
    first_core = core_ref[0] == 0
    head = [None] * FIELDS
    tail = [None] * FIELDS
    for row in range(rows):
        rho = density[:, row, :]
        vel = [velocity[c, :, row, :] for c in range(3)]
        pres = pressure[:, row, :]
        vol = volume[:, row, :]
        energy = tile_state(rho, vel, pres)
        axial = tile_flux(rho, vel, pres, energy, [axial_metric[c, :, row, :] for c in range(3)], vol)
        azim = tile_flux(rho, vel, pres, energy, [azim_metric[c, :, row, :] for c in range(3)], vol)
        for f in range(FIELDS):
            flux[f, row] = axial[f]
            if row == 0:
                head[f] = azim[f]
                tail[f] = azim[f]
                start = azim[f]
                pair[0, 2, f] = start
                odd[0, f] = start
            else:
                head[f] = azim[f] + DERIV_ROOT * head[f]
                tail[f] = tail[f] + (DERIV_ROOT**row) * azim[f]
            if row == rows - 1:
                start = pair[0, 2, f]
                pair[0, 2, f] = jnp.where(first_core, azim[f], start)
                odd[0, f] = jnp.where(first_core, start, azim[f])
    for f in range(FIELDS):
        pair[0, 0, f] = head[f]
        pair[0, 1, f] = tail[f]
    edge[...] = outgoing(basis, flux[...].reshape(-1, flux.shape[-1]))


def section_local_kernel(
    density,
    velocity,
    pressure,
    axial_metric,
    azim_metric,
    volume,
    radial,
    own,
    base_out,
    scale_out,
    axial_flux,
    azim_flux,
):
    rows = density.shape[1]
    lanes = density.shape[2]
    for row in range(rows):
        rho = density[:, row, :]
        vel = [velocity[c, :, row, :] for c in range(3)]
        pres = pressure[:, row, :]
        vol = volume[:, row, :]
        energy = tile_state(rho, vel, pres)
        axial = tile_flux(rho, vel, pres, energy, [axial_metric[c, :, row, :] for c in range(3)], vol)
        azim = tile_flux(rho, vel, pres, energy, [azim_metric[c, :, row, :] for c in range(3)], vol)
        state = [rho, rho * vel[0], rho * vel[1], rho * vel[2], energy]
        scale_out[0, row] = SECTION / vol
        for f in range(FIELDS):
            axial_flux[f, row] = axial[f]
            azim_flux[f, row] = azim[f]
            base_out[0, f, row] = state[f] + SECTION * radial[f, :, row, :]
    deriv = own_block(axial_flux[...].reshape(-1, lanes), own)
    axial_flux[...] = deriv.reshape(axial_flux.shape)
    for f in range(FIELDS):
        down = [None] * rows
        down[rows - 1] = azim_flux[f, rows - 1]
        for row in range(rows - 2, -1, -1):
            down[row] = azim_flux[f, row] + DERIV_ROOT * down[row + 1]
        up = None
        for row in range(rows):
            here = azim_flux[f, row]
            up = here if row == 0 else here + DERIV_ROOT * up
            total = axial_flux[f, row] + DERIV_FAR * (up - down[row])
            if row > 0:
                total = total - DERIV_NEAR * azim_flux[f, row - 1]
            if row < rows - 1:
                total = total + DERIV_NEAR * azim_flux[f, row + 1]
            base_out[0, f, row] = base_out[0, f, row] - scale_out[0, row] * total


def pick(core, zero, one):
    return jnp.where(core == 0, jnp.float32(zero), jnp.float32(one))


def ring_sums(core, mine, chunk, own_sums, sib_sums, sib_pair, root, rows):
    half = own_sums.shape[0]
    local = lax.rem(chunk, half)
    left = jnp.where(mine, own_sums[local, 0], sib_sums[local, 0])
    right = jnp.where(mine, own_sums[local, 1], sib_sums[local, 1])
    decay = root**rows
    left = pick(core, 1.0, decay) * left + pick(core, 0.0, 1.0) * sib_pair[0, 0]
    right = pick(core, decay, 1.0) * right + pick(core, 1.0, 0.0) * sib_pair[0, 1]
    return left, right


def section_join_kernel(
    count, core_ref, base, scale, own_sums, sib_sums, sib_pair, odd, far, basis, *rest
):
    edges, (out, edge_out) = rest[:count], rest[count:]
    rows = scale.shape[1]
    lanes = scale.shape[3]
    core = core_ref[0]
    chunk = pl.program_id(0)
    mine = (chunk // own_sums.shape[0]) == core
    left, right = ring_sums(core, mine, chunk, own_sums, sib_sums, sib_pair, DERIV_ROOT, rows)
    facing = sib_pair[0, 2]
    before = jnp.where(core == 0, odd[0], facing)
    after = jnp.where(core == 0, facing, odd[0])
    if count:
        axial = incoming([ref[...] for ref in edges], far).reshape(out.shape[1:])
    else:
        axial = jnp.zeros(out.shape[1:], jnp.float32)
    for row in range(rows):
        azim = (DERIV_FAR * DERIV_ROOT ** (row + 1)) * left - (
            DERIV_FAR * DERIV_ROOT ** (rows - row)
        ) * right
        if row == 0:
            azim = azim - DERIV_NEAR * before
        if row == rows - 1:
            azim = azim + DERIV_NEAR * after
        out[0, :, row] = base[0, :, row] - scale[0, row][None] * (axial[:, row] + azim)
    edge_out[...] = outgoing(basis, out[0].reshape(-1, lanes))


def axial_local_kernel(values, own, out):
    lines = values[0].reshape(-1, values.shape[-1])
    out[0] = (lines + own_block(lines, own)).reshape(out.shape[1:])


def axial_join_kernel(count, core_ref, local, far, *rest):
    edges, (out, pair, odd) = rest[:count], rest[count:]
    rows = local.shape[2]
    core = core_ref[0]
    if count:
        out[0] = local[0] + incoming([ref[...] for ref in edges], far).reshape(out.shape[1:])
    else:
        out[0] = local[0]
    first = core == 0
    for f in range(FIELDS):
        head = out[0, f, 0]
        tail = out[0, f, 0]
        for row in range(1, rows):
            head = out[0, f, row] + FILTER_ROOT * head
            tail = tail + (FILTER_ROOT**row) * out[0, f, row]
        pair[0, 0, f] = head
        pair[0, 1, f] = tail
        for near in range(2):
            low, high = out[0, f, near], out[0, f, rows - 2 + near]
            pair[0, 2 + near, f] = jnp.where(first, high, low)
            odd[0, near, f] = jnp.where(first, low, high)


def azim_local_kernel(values, out):
    rows = values.shape[2]
    for f in range(FIELDS):
        down = [None] * rows
        down[rows - 1] = values[0, f, rows - 1]
        for row in range(rows - 2, -1, -1):
            down[row] = values[0, f, row] + FILTER_ROOT * down[row + 1]
        up = None
        for row in range(rows):
            here = values[0, f, row]
            up = here if row == 0 else here + FILTER_ROOT * up
            total = (1.0 + FILTER_MID - FILTER_FAR) * here + FILTER_FAR * (up + down[row])
            for step, weight in ((1, FILTER_ONE), (2, FILTER_TWO)):
                if row >= step:
                    total = total + weight * values[0, f, row - step]
                if row + step < rows:
                    total = total + weight * values[0, f, row + step]
            out[0, f, row] = total


def azim_join_kernel(core_ref, local, own_sums, sib_sums, sib_pair, odd, out, surface):
    rows = local.shape[2]
    core = core_ref[0]
    chunk = pl.program_id(0)
    mine = (chunk // own_sums.shape[0]) == core
    left, right = ring_sums(core, mine, chunk, own_sums, sib_sums, sib_pair, FILTER_ROOT, rows)
    for row in range(rows):
        total = (
            local[0, :, row]
            + (FILTER_FAR * FILTER_ROOT ** (row + 1)) * left
            + (FILTER_FAR * FILTER_ROOT ** (rows - row)) * right
        )
        if row < 2:
            before = [jnp.where(core == 0, odd[0, n], sib_pair[0, 2 + n]) for n in range(2)]
            total = total + FILTER_TWO * before[row]
            if row == 0:
                total = total + FILTER_ONE * before[1]
        if row >= rows - 2:
            after = [jnp.where(core == 0, sib_pair[0, 2 + n], odd[0, n]) for n in range(2)]
            total = total + FILTER_TWO * after[row - (rows - 2)]
            if row == rows - 1:
                total = total + FILTER_ONE * after[0]
        out[:, :, row, :] = total

    @pl.when(chunk == 0)
    def _():
        surface[...] = out[2, 0] + out[0, 0] - 1.0


def weights_kernel(table, ids, area, out):
    entries = ids.shape[0]
    for entry in range(entries):
        chosen = ids[entry]
        found = jnp.zeros(chosen.shape, jnp.float32)
        for t in range(table.shape[0]):
            found = jnp.where(chosen == t, table[t], found)
        out[entry] = found * area[...]


def signals_kernel(weights, surface, observers, bins, out):
    entries, rows, lanes = weights.shape
    observer_rows = lax.broadcasted_iota(jnp.int32, (out.shape[0], lanes), 0)
    bin_rows = lax.broadcasted_iota(jnp.int32, (out.shape[1], lanes), 0)
    out[...] = jnp.zeros_like(out)
    for row in range(rows):
        left, right = [], []
        for entry in range(entries):
            value = weights[entry, row : row + 1, :] * surface[row : row + 1, :]
            hit = observer_rows == observers[entry, row : row + 1, :]
            left.append(jnp.where(hit, 1.0, 0.0).astype(jnp.bfloat16))
            right.append(jnp.where(bin_rows == bins[entry, row : row + 1, :], value, 0.0))
        one_hot = jnp.concatenate(left, axis=1)
        high, low = split(jnp.concatenate(right, axis=1))
        for part in (high, low):
            out[...] += lax.dot_general(
                one_hot, part, (((1,), (1,)), ((), ())), preferred_element_type=jnp.float32
            )


def params():
    return pltpu.CompilerParams(vmem_limit_bytes=VMEM_LIMIT)


def cost(flops, moved):
    return pl.CostEstimate(flops=int(flops), bytes_accessed=int(moved), transcendentals=0)


def rotate(values, axis, count, shift):
    return lax.ppermute(values, axis, [(i, (i + shift) % count) for i in range(count)])


def azim_exchange(pair, odd, core, count, root, rows):
    sib = lax.ppermute(pair, "azim", [(i, i ^ 1) for i in range(count)])
    odd_in = lax.ppermute(
        odd, "azim", [(i, (i + 1) % count if i % 2 else (i - 1) % count) for i in range(count)]
    )
    chips = count // 2
    half = pair.shape[0] // 2
    decay = root**rows
    mine = lax.dynamic_slice_in_dim(pair[:, :2], core * half, half, axis=0)
    other = lax.dynamic_slice_in_dim(sib[:, :2], core * half, half, axis=0)
    first = core == 0
    low = jnp.where(first, mine, other)
    high = jnp.where(first, other, mine)
    chip = jnp.stack([high[:, 0] + decay * low[:, 0], low[:, 1] + decay * high[:, 1]], axis=1)
    wide = root ** (2 * rows)
    close = 1.0 / (1.0 - root ** (rows * count))
    left = wide ** (chips - 1) * chip[:, 0]
    right = wide ** (chips - 1) * chip[:, 1]
    for shift in range(1, chips):
        there = rotate(chip, "azim", count, 2 * shift)
        left = left + wide ** (shift - 1) * there[:, 0]
        right = right + wide ** (chips - shift - 1) * there[:, 1]
    sums = close * jnp.stack([left, right], axis=1)
    sib_sums = lax.ppermute(sums, "azim", [(i, i ^ 1) for i in range(count)])
    return sib, odd_in, sums, sib_sums


def per_device(
    density,
    velocity,
    pressure,
    axial_metric,
    azim_metric,
    volume,
    radial_term,
    panel_area,
    observer_ids,
    bin_ids,
    weight_ids,
    bin_weights,
):
    planes, rows, lanes = density.shape
    along = lax.axis_size("axial")
    around = lax.axis_size("azim")
    steps = planes // CHUNK
    lines = FIELDS * rows * CHUNK
    place = lax.axis_index("axial")
    core = lax.axis_index("azim") % 2
    core_ref = core.astype(jnp.int32).reshape(1)
    f32 = jnp.float32

    tables = {}
    for kind, alpha in (("deriv", DERIV_ALPHA), ("filter", FILTER_ALPHA)):
        own, basis, far = axial_tables(along, lanes, alpha, kind)
        tables[kind] = (
            jnp.asarray(halves(own))[place],
            jnp.asarray(halves(basis)),
            jnp.asarray(halves(far))[place],
        )

    smem = pl.BlockSpec(memory_space=pltpu.SMEM)
    field = pl.BlockSpec((CHUNK, rows, lanes), lambda k: (k, 0, 0))
    vector = pl.BlockSpec((3, CHUNK, rows, lanes), lambda k: (0, k, 0, 0))
    wide_in = pl.BlockSpec((FIELDS, CHUNK, rows, lanes), lambda k: (0, k, 0, 0))
    inner = pl.BlockSpec((1, FIELDS, rows, CHUNK, lanes), lambda k: (k, 0, 0, 0, 0))
    inner_one = pl.BlockSpec((1, rows, CHUNK, lanes), lambda k: (k, 0, 0, 0))
    edge = pl.BlockSpec((BASIS, lines), lambda k: (0, k))

    def fixed(shape):
        return pl.BlockSpec(shape, lambda k: (0,) * len(shape))

    def packed(*lead):
        return pl.BlockSpec(
            (1,) + lead + (FIELDS, CHUNK, lanes), lambda k: (k,) + (0,) * (len(lead) + 3)
        )

    def packed_shape(*lead):
        return jax.ShapeDtypeStruct((steps,) + lead + (FIELDS, CHUNK, lanes), f32)

    inner_shape = jax.ShapeDtypeStruct((steps, FIELDS, rows, CHUNK, lanes), f32)
    one_shape = jax.ShapeDtypeStruct((steps, rows, CHUNK, lanes), f32)
    edge_shape = jax.ShapeDtypeStruct((BASIS, steps * lines), f32)
    flux_scratch = pltpu.VMEM((FIELDS, rows, CHUNK, lanes), f32)
    block = planes * rows * lanes
    sums_shape = (steps // 2, 2, FIELDS, CHUNK, lanes)

    own_d, basis_d, far_d = tables["deriv"]
    own_f, basis_f, far_f = tables["filter"]

    edge_d, pair_d, odd_d = pl.pallas_call(
        flux_send_kernel,
        grid=(steps,),
        in_specs=[smem, field, vector, field, vector, vector, field, fixed(basis_d.shape)],
        out_specs=[edge, packed(3), packed()],
        out_shape=[edge_shape, packed_shape(3), packed_shape()],
        scratch_shapes=[flux_scratch],
        compiler_params=params(),
        cost_estimate=cost(200 * block, 52 * block),
        name="flux_send",
    )(core_ref, density, velocity, pressure, axial_metric, azim_metric, volume, basis_d)

    weights = pl.pallas_call(
        weights_kernel,
        in_specs=[smem] + [pl.BlockSpec(memory_space=pltpu.VMEM)] * 2,
        out_specs=pl.BlockSpec(memory_space=pltpu.VMEM),
        out_shape=jax.ShapeDtypeStruct(weight_ids.shape, f32),
        compiler_params=params(),
        name="entry_weights",
    )(bin_weights, weight_ids, panel_area)

    edges_d = [rotate(edge_d, "axial", along, s) for s in range(1, along)]
    sib_d, odd_d, sums_d, sib_sums_d = azim_exchange(pair_d, odd_d, core, around, DERIV_ROOT, rows)

    base, scale = pl.pallas_call(
        section_local_kernel,
        grid=(steps,),
        in_specs=[field, vector, field, vector, vector, field, wide_in, fixed(own_d.shape)],
        out_specs=[inner, inner_one],
        out_shape=[inner_shape, one_shape],
        scratch_shapes=[flux_scratch, flux_scratch],
        compiler_params=params(),
        cost_estimate=cost(4000 * block, 100 * block),
        name="section_local",
    )(density, velocity, pressure, axial_metric, azim_metric, volume, radial_term, own_d)

    sectioned, edge_f = pl.pallas_call(
        functools.partial(section_join_kernel, along - 1),
        grid=(steps,),
        in_specs=[
            smem,
            inner,
            inner_one,
            fixed(sums_shape),
            fixed(sums_shape),
            packed(3),
            packed(),
            fixed(far_d.shape),
            fixed(basis_f.shape),
        ]
        + [edge] * (along - 1),
        out_specs=[inner, edge],
        out_shape=[inner_shape, edge_shape],
        compiler_params=params(),
        cost_estimate=cost(500 * block, 48 * block),
        name="section_join",
    )(core_ref, base, scale, sums_d, sib_sums_d, sib_d, odd_d, far_d, basis_f, *edges_d)

    edges_f = [rotate(edge_f, "axial", along, s) for s in range(1, along)]

    axial_local = pl.pallas_call(
        axial_local_kernel,
        grid=(steps,),
        in_specs=[inner, fixed(own_f.shape)],
        out_specs=inner,
        out_shape=inner_shape,
        compiler_params=params(),
        cost_estimate=cost(4000 * block, 40 * block),
        name="axial_local",
    )(sectioned, own_f)

    smoothed, pair_f, odd_f = pl.pallas_call(
        functools.partial(axial_join_kernel, along - 1),
        grid=(steps,),
        in_specs=[smem, inner, fixed(far_f.shape)] + [edge] * (along - 1),
        out_specs=[inner, packed(4), packed(2)],
        out_shape=[inner_shape, packed_shape(4), packed_shape(2)],
        compiler_params=params(),
        cost_estimate=cost(500 * block, 48 * block),
        name="axial_join",
    )(core_ref, axial_local, far_f, *edges_f)

    sib_f, odd_f, sums_f, sib_sums_f = azim_exchange(pair_f, odd_f, core, around, FILTER_ROOT, rows)

    azim_local = pl.pallas_call(
        azim_local_kernel,
        grid=(steps,),
        in_specs=[inner],
        out_specs=inner,
        out_shape=inner_shape,
        compiler_params=params(),
        cost_estimate=cost(100 * block, 40 * block),
        name="azim_local",
    )(smoothed)

    new_state, surface = pl.pallas_call(
        azim_join_kernel,
        grid=(steps,),
        in_specs=[smem, inner, fixed(sums_shape), fixed(sums_shape), packed(4), packed(2)],
        out_specs=[wide_in, fixed((rows, lanes))],
        out_shape=[
            jax.ShapeDtypeStruct((FIELDS, planes, rows, lanes), f32),
            jax.ShapeDtypeStruct((rows, lanes), f32),
        ],
        compiler_params=params(),
        cost_estimate=cost(100 * block, 48 * block),
        name="azim_join",
    )(core_ref, azim_local, sums_f, sib_sums_f, sib_f, odd_f)

    partial = pl.pallas_call(
        signals_kernel,
        out_shape=jax.ShapeDtypeStruct((OBSERVERS, TIME_BINS), f32),
        compiler_params=params(),
        name="signals",
    )(weights, surface, observer_ids, bin_ids)
    devices = along * around
    shares = lax.all_to_all(
        partial.reshape(devices, OBSERVERS // devices, TIME_BINS),
        ("axial", "azim"),
        0,
        0,
        tiled=True,
    )
    return (new_state, jnp.sum(shares, axis=0))


def solution(mesh):
    placed = (
        P(None, "azim", "axial"),
        P(None, None, "azim", "axial"),
        P(None, "azim", "axial"),
        P(None, None, "azim", "axial"),
        P(None, None, "azim", "axial"),
        P(None, "azim", "axial"),
        P(None, None, "azim", "axial"),
        P("azim", "axial"),
        P(None, "azim", "axial"),
        P(None, "azim", "axial"),
        P(None, "azim", "axial"),
        P(),
    )
    return jax.shard_map(
        per_device,
        mesh=mesh,
        in_specs=placed,
        out_specs=(P(None, None, "azim", "axial"), P(("axial", "azim"), None)),
        check_vma=False,
    )
```

```python
import functools
import math

import jax
import jax.numpy as jnp
import numpy as np
from jax import lax
from jax.experimental import pallas as pl
from jax.experimental.pallas import tpu as pltpu
from jax.sharding import PartitionSpec as P

OBSERVERS = 512
TIME_BINS = 128

GAMMA = 1.4
SECTION = 0.25
DERIV_ALPHA = 1.0 / 3.0
FILTER_ALPHA = 0.499
FIELDS = 5
CHUNK = 16
BASIS = 8
VMEM_LIMIT = 32 * 1024 * 1024
INPUT_LIMIT = 60 * 1024 * 1024


def decay_root(alpha):
    return (-1.0 + math.sqrt(1.0 - 4.0 * alpha * alpha)) / (2.0 * alpha)


DERIV_ROOT = decay_root(DERIV_ALPHA)
FILTER_ROOT = decay_root(FILTER_ALPHA)

DERIV_NEAR = 1.0 / 12.0
DERIV_FAR = (
    (25.0 / 36.0) * (DERIV_ROOT - 1.0 / DERIV_ROOT) / (1.0 + 2.0 * DERIV_ALPHA * DERIV_ROOT)
)

_B = FILTER_ALPHA
_EDGE = (1.0 - 2.0 * _B) / 64.0
_Q2 = 1.0 / _B
_Q1 = (-6.0 - _Q2) / _B
_Q0 = (12.0 - _Q1) / _B
_RHO = -8.0 - _Q0
FILTER_MID = _EDGE * (_Q0 + 2.0 * _Q2)
FILTER_ONE = _EDGE * _Q1
FILTER_TWO = _EDGE * _Q2
FILTER_FAR = _EDGE * _RHO / (1.0 + 2.0 * _B * FILTER_ROOT)


def open_operator(length, alpha, side):
    base = decay_root(alpha)
    tri = np.eye(length) + alpha * (np.eye(length, k=1) + np.eye(length, k=-1))
    tri[0, 0] = -alpha / base
    return np.linalg.solve(tri, side)


def deriv_matrix(length):
    return (7.0 / 9.0) * (np.eye(length, k=1) - np.eye(length, k=-1)) + (1.0 / 36.0) * (
        np.eye(length, k=2) - np.eye(length, k=-2)
    )


def filter_matrix(length):
    beta = FILTER_ALPHA
    coeffs = [
        (11.0 + 10.0 * beta) / 16.0,
        (15.0 + 34.0 * beta) / 32.0,
        (-3.0 + 6.0 * beta) / 16.0,
        (1.0 - 2.0 * beta) / 32.0,
    ]
    total = coeffs[0] * np.eye(length)
    for shift in range(1, 4):
        total = total + 0.5 * coeffs[shift] * (np.eye(length, k=shift) + np.eye(length, k=-shift))
    return total


def axial_tables(count, width, alpha, kind):
    length = count * width
    side = deriv_matrix(length) if kind == "deriv" else filter_matrix(length)
    whole = open_operator(length, alpha, side)
    base = decay_root(alpha)
    basis = np.zeros((BASIS, width))
    for edge in range(3):
        basis[edge, edge] = 1.0
        basis[3 + edge, width - 3 + edge] = 1.0
    basis[6] = base ** np.arange(width - 1, -1, -1, dtype=np.float64)
    basis[7] = base ** np.arange(width, dtype=np.float64)
    inverse = np.linalg.pinv(basis)
    own = np.zeros((count, width, width))
    far = np.zeros((count, max(count - 1, 1) * BASIS, width))
    for here in range(count):
        rows = whole[here * width : (here + 1) * width]
        own[here] = rows[:, here * width : (here + 1) * width].T
        if kind == "filter":
            own[here] -= np.eye(width)
        for shift in range(1, count):
            there = (here - shift) % count
            block = rows[:, there * width : (there + 1) * width]
            far[here, (shift - 1) * BASIS : shift * BASIS] = (block @ inverse).T
    return own, basis, far


def surface_tables(along, width, around, rows):
    axial = open_operator(along * width, FILTER_ALPHA, filter_matrix(along * width))
    axial = axial.reshape(along, width, along * width).transpose(0, 2, 1)
    length = around * rows
    turn = np.roll(np.eye(length), 1, axis=1)
    beta = FILTER_ALPHA
    side = (11.0 + 10.0 * beta) / 16.0 * np.eye(length)
    coeffs = [(15.0 + 34.0 * beta) / 32.0, (-3.0 + 6.0 * beta) / 16.0, (1.0 - 2.0 * beta) / 32.0]
    for shift in range(1, 4):
        step = np.linalg.matrix_power(turn, shift)
        side = side + 0.5 * coeffs[shift - 1] * (step + step.T)
    cycle = np.linalg.solve(np.eye(length) + beta * (turn + turn.T), side)
    return axial.astype(np.float32), cycle.reshape(around, rows, length).astype(np.float32)


def halves(table):
    high = np.asarray(table, np.float32).astype(jnp.bfloat16)
    low = (np.asarray(table, np.float64) - high.astype(np.float64)).astype(jnp.bfloat16)
    return np.stack([high, low], axis=-3)


def split(values):
    high = values.astype(jnp.bfloat16)
    return high, (values - high.astype(jnp.float32)).astype(jnp.bfloat16)


def dots(left, right, dims):
    out = None
    for a, b in ((0, 0), (1, 0), (0, 1)):
        part = lax.dot_general(
            left[a], right[b], (dims, ((), ())), preferred_element_type=jnp.float32
        )
        out = part if out is None else out + part
    return out


def outgoing(basis_ref, lines):
    return dots((basis_ref[0], basis_ref[1]), split(lines), ((1,), (1,)))


def incoming(parts, far_ref):
    return dots(split(jnp.concatenate(parts, axis=0)), (far_ref[0], far_ref[1]), ((0,), (0,)))


def own_block(lines, own_ref):
    return dots(split(lines), (own_ref[0], own_ref[1]), ((1,), (0,)))


def tile_energy(density, velocity, pressure):
    return pressure * (1.0 / (GAMMA - 1.0)) + 0.5 * density * (
        velocity[0] * velocity[0] + velocity[1] * velocity[1] + velocity[2] * velocity[2]
    )


def tile_flux(density, velocity, pressure, energy, metric, volume):
    contra = metric[0] * velocity[0] + metric[1] * velocity[1] + metric[2] * velocity[2]
    volume_contra = volume * contra
    mass = density * volume_contra
    push = volume * pressure
    pieces = [mass]
    for comp in range(3):
        pieces.append(mass * velocity[comp] + metric[comp] * push)
    pieces.append((energy + pressure) * volume_contra)
    return pieces


def pack_rows(tiles, root, near, pack):
    rows = len(tiles)
    head = tail = tiles[0]
    for row in range(1, rows):
        head = tiles[row] + root * head
        tail = tail + (root**row) * tiles[row]
    pack[0] = head
    pack[1] = tail
    for n in range(near):
        pack[2 + n] = tiles[n]
        pack[2 + near + n] = tiles[rows - near + n]


def azim_flux_kernel(density, velocity, pressure, azim_metric, volume, pack, flux):
    planes, rows, _ = density.shape
    for plane in range(planes):
        rho = density[plane]
        vel = [velocity[c, plane] for c in range(3)]
        pres = pressure[plane]
        energy = tile_energy(rho, vel, pres)
        metric = [azim_metric[c, plane] for c in range(3)]
        for f, piece in enumerate(tile_flux(rho, vel, pres, energy, metric, volume[plane])):
            flux[f, plane] = piece
    for f in range(FIELDS):
        turned = jnp.swapaxes(flux[f], 0, 1)
        pack_rows([turned[row] for row in range(rows)], DERIV_ROOT, 1, pack.at[0, :, f])


def section_local_kernel(
    place,
    density,
    velocity,
    pressure,
    axial_metric,
    azim_metric,
    volume,
    radial,
    own,
    basis,
    base_out,
    scale_out,
    edge_out,
    axial_flux,
    azim_flux,
    start,
):
    planes, rows, lanes = density.shape
    for plane in range(planes):
        rho = density[plane]
        vel = [velocity[c, plane] for c in range(3)]
        pres = pressure[plane]
        vol = volume[plane]
        energy = tile_energy(rho, vel, pres)
        axial = tile_flux(rho, vel, pres, energy, [axial_metric[c, plane] for c in range(3)], vol)
        azim = tile_flux(rho, vel, pres, energy, [azim_metric[c, plane] for c in range(3)], vol)
        state = [rho, rho * vel[0], rho * vel[1], rho * vel[2], energy]
        for f in range(FIELDS):
            axial_flux[f, plane] = axial[f]
            azim_flux[f, plane] = azim[f]
            start[f, plane] = state[f] + SECTION * radial[f, plane]
    scale = SECTION / volume[...]
    turned_scale = jnp.swapaxes(scale, 0, 1)
    scale_out[0] = turned_scale
    for f in range(FIELDS):
        flux = jnp.swapaxes(axial_flux[f], 0, 1).reshape(rows * planes, lanes)
        edge_out[:, f * rows * planes : (f + 1) * rows * planes] = outgoing(basis, flux)
        deriv = own_block(flux, own).reshape(rows, planes, lanes)
        azim = jnp.swapaxes(azim_flux[f], 0, 1)
        first = jnp.swapaxes(start[f], 0, 1)
        down = [None] * rows
        down[rows - 1] = azim[rows - 1]
        for row in range(rows - 2, -1, -1):
            down[row] = azim[row] + DERIV_ROOT * down[row + 1]
        up = None
        for row in range(rows):
            up = azim[row] if row == 0 else azim[row] + DERIV_ROOT * up
            total = deriv[row] + DERIV_FAR * (up - down[row])
            if row > 0:
                total = total - DERIV_NEAR * azim[row - 1]
            if row < rows - 1:
                total = total + DERIV_NEAR * azim[row + 1]
            base_out[0, f, row] = first[row] - turned_scale[row] * total


def chip_kernel(near, rows, root, place, mine, other, ahead, back, far):
    core = place[0]
    decay = root**rows

    def low(n):
        return jnp.where(core == 0, mine[0, n], other[0, n])

    def high(n):
        return jnp.where(core == 0, other[0, n], mine[0, n])

    head = high(0) + decay * low(0)
    tail = low(1) + decay * high(1)
    for out in (ahead, back, far):
        out[0, 0] = head
        out[0, 1] = tail
    for n in range(near):
        ahead[0, 2 + n] = high(2 + near + n)
        back[0, 2 + n] = low(2 + n)


def ring_kernel(chips, near, rows, root, place, own, left_in, right_in, *rest):
    far, (mine, theirs) = rest[: chips - 3], rest[chips - 3 :]
    core = place[0]
    wide = root ** (2 * rows)
    close = 1.0 / (1.0 - root ** (2 * rows * chips))
    left = wide ** (chips - 1) * own[0, 0]
    right = wide ** (chips - 1) * own[0, 1]
    for shift, there in enumerate([left_in, *far, right_in], start=1):
        left = left + wide ** (shift - 1) * there[0, 0]
        right = right + wide ** (chips - shift - 1) * there[0, 1]
    for out in (mine, theirs):
        out[0, 0] = close * left
        out[0, 1] = close * right
    for n in range(near):
        before, after = left_in[0, 2 + n], right_in[0, 2 + n]
        mine[0, 2 + n] = jnp.where(core == 0, before, after)
        theirs[0, 2 + n] = jnp.where(core == 0, after, before)


def surroundings(place, half, own, sib, sib_pack, near, root, rows):
    core = place[0]
    mine = (pl.program_id(0) // half) == core
    ring = [jnp.where(mine, own[0, n], sib[0, n]) for n in range(2 + near)]
    decay = root**rows
    zero, one = jnp.float32(0.0), jnp.float32(1.0)
    first = core == 0
    left = jnp.where(first, one, decay) * ring[0] + jnp.where(first, zero, one) * sib_pack[0, 0]
    right = jnp.where(first, decay, one) * ring[1] + jnp.where(first, one, zero) * sib_pack[0, 1]
    before = [jnp.where(first, ring[2 + n], sib_pack[0, 2 + near + n]) for n in range(near)]
    after = [jnp.where(first, sib_pack[0, 2 + n], ring[2 + n]) for n in range(near)]
    return left, right, before, after


def section_join_kernel(half, place, base, scale, own, sib, sib_pack, far, basis, *rest):
    edges, (out, edge_out, front) = rest[:-3], rest[-3:]
    rows, planes, lanes = scale.shape[1:]
    left, right, (before,), (after,) = surroundings(
        place, half, own, sib, sib_pack, 1, DERIV_ROOT, rows
    )
    for f in range(FIELDS):
        spot = slice(f * rows * planes, (f + 1) * rows * planes)
        axial = incoming([ref[:, spot] for ref in edges], far).reshape(rows, planes, lanes)
        for row in range(rows):
            azim = (DERIV_FAR * DERIV_ROOT ** (row + 1)) * left[f] - (
                DERIV_FAR * DERIV_ROOT ** (rows - row)
            ) * right[f]
            if row == 0:
                azim = azim - DERIV_NEAR * before[f]
            if row == rows - 1:
                azim = azim + DERIV_NEAR * after[f]
            out[0, f, row] = base[0, f, row] - scale[0, row] * (axial[row] + azim)
        edge_out[:, spot] = outgoing(basis, out[0, f].reshape(rows * planes, lanes))

    @pl.when(pl.program_id(0) == 0)
    def _():
        for row in range(rows):
            front[row : row + 1, :] = out[0, 2, row, 0:1, :] + out[0, 0, row, 0:1, :]


def axial_local_kernel(place, values, own, out):
    lines = values[0].reshape(-1, values.shape[-1])
    out[0] = (lines + own_block(lines, own)).reshape(out.shape[1:])


def axial_join_kernel(local, far, *rest):
    edges, (out, pack) = rest[:-2], rest[-2:]
    rows, planes, lanes = local.shape[2:]
    for f in range(FIELDS):
        spot = slice(f * rows * planes, (f + 1) * rows * planes)
        axial = incoming([ref[:, spot] for ref in edges], far).reshape(rows, planes, lanes)
        tiles = [local[0, f, row] + axial[row] for row in range(rows)]
        for row in range(rows):
            out[0, f, row] = tiles[row]
        pack_rows(tiles, FILTER_ROOT, 2, pack.at[0, :, f])


def azim_local_kernel(values, out):
    rows = values.shape[2]
    for f in range(FIELDS):
        down = [None] * rows
        down[rows - 1] = values[0, f, rows - 1]
        for row in range(rows - 2, -1, -1):
            down[row] = values[0, f, row] + FILTER_ROOT * down[row + 1]
        up = None
        for row in range(rows):
            here = values[0, f, row]
            up = here if row == 0 else here + FILTER_ROOT * up
            total = (1.0 + FILTER_MID - FILTER_FAR) * here + FILTER_FAR * (up + down[row])
            for step, weight in ((1, FILTER_ONE), (2, FILTER_TWO)):
                if row >= step:
                    total = total + weight * values[0, f, row - step]
                if row + step < rows:
                    total = total + weight * values[0, f, row + step]
            out[0, f, row] = total


def azim_join_kernel(half, place, local, own, sib, sib_pack, out):
    rows = local.shape[2]
    left, right, before, after = surroundings(
        place, half, own, sib, sib_pack, 2, FILTER_ROOT, rows
    )
    for f in range(FIELDS):
        tiles = []
        for row in range(rows):
            total = (
                local[0, f, row]
                + (FILTER_FAR * FILTER_ROOT ** (row + 1)) * left[f]
                + (FILTER_FAR * FILTER_ROOT ** (rows - row)) * right[f]
            )
            if row < 2:
                total = total + FILTER_TWO * before[row][f]
            if row == 0:
                total = total + FILTER_ONE * before[1][f]
            if row >= rows - 2:
                total = total + FILTER_TWO * after[row - (rows - 2)][f]
            if row == rows - 1:
                total = total + FILTER_ONE * after[0][f]
            tiles.append(total)
        out[f] = jnp.swapaxes(jnp.stack(tiles), 0, 1)


def weights_kernel(table, ids, area, out):
    entries = ids.shape[0]
    for entry in range(entries):
        chosen = ids[entry]
        found = jnp.zeros(chosen.shape, jnp.float32)
        for t in range(table.shape[0]):
            found = jnp.where(chosen == t, table[t], found)
        out[entry] = found * area[...]


def signals_kernel(place, fronts, around, along, weights, observers, bins, out):
    entries, rows, lanes = weights.shape
    columns = around.shape[2] // rows
    surface = jnp.full((rows, lanes), -1.0, jnp.float32)
    for a in range(fronts.shape[0] // columns):
        ring = fronts[a * columns : (a + 1) * columns].reshape(columns * rows, lanes)
        smooth = jnp.dot(
            around[0], ring, precision=lax.Precision.HIGHEST, preferred_element_type=jnp.float32
        )
        surface = surface + jnp.dot(
            smooth,
            along[0, a * lanes : (a + 1) * lanes],
            precision=lax.Precision.HIGHEST,
            preferred_element_type=jnp.float32,
        )
    observer_rows = lax.broadcasted_iota(jnp.int32, (out.shape[0], lanes), 0)
    bin_rows = lax.broadcasted_iota(jnp.int32, (out.shape[1], lanes), 0)
    out[...] = jnp.zeros_like(out)
    for row in range(rows):
        left, right = [], []
        for entry in range(entries):
            value = weights[entry, row : row + 1, :] * surface[row : row + 1, :]
            hit = observer_rows == observers[entry, row : row + 1, :]
            left.append(jnp.where(hit, 1.0, 0.0).astype(jnp.bfloat16))
            right.append(jnp.where(bin_rows == bins[entry, row : row + 1, :], value, 0.0))
        one_hot = jnp.concatenate(left, axis=1)
        high, low = split(jnp.concatenate(right, axis=1))
        for part in (high, low):
            out[...] += lax.dot_general(
                one_hot, part, (((1,), (1,)), ((), ())), preferred_element_type=jnp.float32
            )


def params(limit=VMEM_LIMIT):
    return pltpu.CompilerParams(vmem_limit_bytes=limit)


def cost(flops, moved):
    return pl.CostEstimate(flops=int(flops), bytes_accessed=int(moved), transcendentals=0)


def rotate(values, axis, count, shift):
    return lax.ppermute(values, axis, [(i, (i + shift) % count) for i in range(count)])


def sibling(values, count):
    return lax.ppermute(values, "azim", [(i, i ^ 1) for i in range(count)])


def azim_exchange(place, pack, count, near, root, rows):
    steps, values, fields, planes, lanes = pack.shape
    chips = count // 2
    half = steps // 2
    f32 = jnp.float32

    def block(size, start):
        if start:
            return pl.BlockSpec(
                (1, size, fields, planes, lanes), lambda k, at: (k + at[0] * half, 0, 0, 0, 0)
            )
        return pl.BlockSpec((1, size, fields, planes, lanes), lambda k, at: (k, 0, 0, 0, 0))

    def shape(size):
        return jax.ShapeDtypeStruct((half, size, fields, planes, lanes), f32)

    sib = sibling(pack, count)
    wide = 2 + near
    ahead, back, far = pl.pallas_call(
        functools.partial(chip_kernel, near, rows, root),
        grid_spec=pltpu.PrefetchScalarGridSpec(
            num_scalar_prefetch=1,
            grid=(half,),
            in_specs=[block(values, True)] * 2,
            out_specs=[block(wide, False)] * 2 + [block(2, False)],
        ),
        out_shape=[shape(wide)] * 2 + [shape(2)],
        compiler_params=params(),
        name="chip_moments",
    )(place, pack, sib)
    left_in = rotate(ahead, "azim", count, 2)
    right_in = rotate(back, "azim", count, -2)
    between = [rotate(far, "azim", count, 2 * shift) for shift in range(2, chips - 1)]
    return sib, far, left_in, right_in, between


def ring_join(place, far, left_in, right_in, between, count, near, root, rows):
    half, _, fields, planes, lanes = far.shape
    chips = count // 2
    wide = 2 + near

    def block(size):
        return pl.BlockSpec((1, size, fields, planes, lanes), lambda k, at: (k, 0, 0, 0, 0))

    out = jax.ShapeDtypeStruct((half, wide, fields, planes, lanes), jnp.float32)
    mine, theirs = pl.pallas_call(
        functools.partial(ring_kernel, chips, near, rows, root),
        grid_spec=pltpu.PrefetchScalarGridSpec(
            num_scalar_prefetch=1,
            grid=(half,),
            in_specs=[block(2), block(wide), block(wide)] + [block(2)] * (chips - 3),
            out_specs=[block(wide)] * 2,
        ),
        out_shape=[out, out],
        compiler_params=params(),
        name="ring_sums",
    )(place, far, left_in, right_in, *between)
    return mine, sibling(theirs, count)


def per_device(
    density,
    velocity,
    pressure,
    axial_metric,
    azim_metric,
    volume,
    radial_term,
    panel_area,
    observer_ids,
    bin_ids,
    weight_ids,
    bin_weights,
):
    planes, rows, lanes = density.shape
    along = lax.axis_size("axial")
    around = lax.axis_size("azim")
    devices = along * around
    steps = planes // CHUNK
    half = steps // 2
    lines = FIELDS * rows * CHUNK
    f32 = jnp.float32
    azim_at = lax.axis_index("azim")
    place = jnp.stack([azim_at % 2, lax.axis_index("axial"), azim_at]).astype(jnp.int32)

    own_d, basis_d, far_d = map(halves, axial_tables(along, lanes, DERIV_ALPHA, "deriv"))
    own_f, basis_f, far_f = map(halves, axial_tables(along, lanes, FILTER_ALPHA, "filter"))
    filter_along, filter_around = surface_tables(along, lanes, around, rows)

    def spec(shape, index):
        return pl.BlockSpec(shape, index)

    smem = pl.BlockSpec(memory_space=pltpu.SMEM)
    field = spec((CHUNK, rows, lanes), lambda k, at: (k, 0, 0))
    vector = spec((3, CHUNK, rows, lanes), lambda k, at: (0, k, 0, 0))
    wide = spec((FIELDS, CHUNK, rows, lanes), lambda k, at: (0, k, 0, 0))
    inner = spec((1, FIELDS, rows, CHUNK, lanes), lambda k, at: (k, 0, 0, 0, 0))
    inner_one = spec((1, rows, CHUNK, lanes), lambda k, at: (k, 0, 0, 0))
    edge = spec((BASIS, lines), lambda k, at: (0, k))

    def table(array):
        return spec((None,) + array.shape[1:], lambda k, at: (at[1],) + (0,) * (array.ndim - 1))

    def fixed(shape):
        return spec(shape, lambda k, at: (0,) * len(shape))

    def packed(size):
        return spec((1, size, FIELDS, CHUNK, lanes), lambda k, at: (k, 0, 0, 0, 0))

    def ring(size):
        return spec((1, size, FIELDS, CHUNK, lanes), lambda k, at: (k % half, 0, 0, 0, 0))

    def packed_shape(size):
        return jax.ShapeDtypeStruct((steps, size, FIELDS, CHUNK, lanes), f32)

    def call(kernel, name, ins, outs, shapes, args, flops, moved, scratch=(), limit=VMEM_LIMIT):
        return pl.pallas_call(
            kernel,
            grid_spec=pltpu.PrefetchScalarGridSpec(
                num_scalar_prefetch=1,
                grid=(steps,),
                in_specs=ins,
                out_specs=outs,
                scratch_shapes=scratch,
            ),
            out_shape=shapes,
            compiler_params=params(limit),
            cost_estimate=cost(flops, moved),
            name=name,
        )(place, *args)

    def unplaced(kernel):
        return lambda at, *refs: kernel(*refs)

    inner_shape = jax.ShapeDtypeStruct((steps, FIELDS, rows, CHUNK, lanes), f32)
    one_shape = jax.ShapeDtypeStruct((steps, rows, CHUNK, lanes), f32)
    edge_shape = jax.ShapeDtypeStruct((BASIS, steps * lines), f32)
    flux_scratch = pltpu.VMEM((FIELDS, CHUNK, rows, lanes), f32)
    block = planes * rows * lanes

    pack_d = call(
        unplaced(azim_flux_kernel),
        "azim_flux",
        [field, vector, field, vector, field],
        packed(4),
        packed_shape(4),
        (density, velocity, pressure, azim_metric, volume),
        100 * block,
        40 * block,
        scratch=[flux_scratch],
        limit=INPUT_LIMIT,
    )
    sib_d, far_m, left_in, right_in, between = azim_exchange(
        place, pack_d, around, 1, DERIV_ROOT, rows
    )

    weights = pl.pallas_call(
        weights_kernel,
        in_specs=[smem] + [pl.BlockSpec(memory_space=pltpu.VMEM)] * 2,
        out_specs=pl.BlockSpec(memory_space=pltpu.VMEM),
        out_shape=jax.ShapeDtypeStruct(weight_ids.shape, f32),
        compiler_params=params(),
        name="entry_weights",
    )(bin_weights, weight_ids, panel_area)

    base, scale, edge_d = call(
        section_local_kernel,
        "section_local",
        [field, vector, field, vector, vector, field, wide, table(own_d), fixed(basis_d.shape)],
        [inner, inner_one, edge],
        [inner_shape, one_shape, edge_shape],
        (
            density,
            velocity,
            pressure,
            axial_metric,
            azim_metric,
            volume,
            radial_term,
            own_d,
            basis_d,
        ),
        4000 * block,
        100 * block,
        scratch=[flux_scratch] * 3,
    )
    edges_d = [rotate(edge_d, "axial", along, s) for s in range(1, along)]
    mine, sib = ring_join(place, far_m, left_in, right_in, between, around, 1, DERIV_ROOT, rows)

    sectioned, edge_f, front = call(
        functools.partial(section_join_kernel, half),
        "section_join",
        [inner, inner_one, ring(3), ring(3), packed(4), table(far_d), fixed(basis_f.shape)]
        + [edge] * (along - 1),
        [inner, edge, fixed((rows, lanes))],
        [inner_shape, edge_shape, jax.ShapeDtypeStruct((rows, lanes), f32)],
        (base, scale, mine, sib, sib_d, far_d, basis_f, *edges_d),
        500 * block,
        48 * block,
    )
    edges_f = [rotate(edge_f, "axial", along, s) for s in range(1, along)]
    fronts = lax.all_to_all(
        jnp.broadcast_to(front[None], (devices, rows, lanes)), ("axial", "azim"), 0, 0, tiled=True
    )

    axial_local = call(
        axial_local_kernel,
        "axial_local",
        [inner, table(own_f)],
        inner,
        inner_shape,
        (sectioned, own_f),
        4000 * block,
        40 * block,
    )
    smoothed, pack_f = call(
        unplaced(axial_join_kernel),
        "axial_join",
        [inner, table(far_f)] + [edge] * (along - 1),
        [inner, packed(6)],
        [inner_shape, packed_shape(6)],
        (axial_local, far_f, *edges_f),
        500 * block,
        48 * block,
    )
    sib_f, far_m, left_in, right_in, between = azim_exchange(
        place, pack_f, around, 2, FILTER_ROOT, rows
    )

    azim_local = call(
        unplaced(azim_local_kernel),
        "azim_local",
        [inner],
        inner,
        inner_shape,
        (smoothed,),
        100 * block,
        40 * block,
    )

    whole = pl.BlockSpec(memory_space=pltpu.VMEM)
    partial = pl.pallas_call(
        signals_kernel,
        grid_spec=pltpu.PrefetchScalarGridSpec(
            num_scalar_prefetch=1,
            grid=(1,),
            in_specs=[
                fixed(fronts.shape),
                spec((1,) + filter_around.shape[1:], lambda k, at: (at[2], 0, 0)),
                spec((1,) + filter_along.shape[1:], lambda k, at: (at[1], 0, 0)),
                fixed(weights.shape),
                fixed(observer_ids.shape),
                fixed(bin_ids.shape),
            ],
            out_specs=fixed((OBSERVERS, TIME_BINS)),
        ),
        out_shape=jax.ShapeDtypeStruct((OBSERVERS, TIME_BINS), f32),
        compiler_params=params(),
        name="signals",
    )(place, fronts, filter_around, filter_along, weights, observer_ids, bin_ids)
    shares = lax.all_to_all(
        partial.reshape(devices, OBSERVERS // devices, TIME_BINS),
        ("axial", "azim"),
        0,
        0,
        tiled=True,
    )
    signals = jnp.sum(shares, axis=0)

    mine, sib = ring_join(place, far_m, left_in, right_in, between, around, 2, FILTER_ROOT, rows)
    new_state = call(
        functools.partial(azim_join_kernel, half),
        "azim_join",
        [inner, ring(4), ring(4), packed(6)],
        wide,
        jax.ShapeDtypeStruct((FIELDS, planes, rows, lanes), f32),
        (azim_local, mine, sib, sib_f),
        100 * block,
        48 * block,
    )
    return (new_state, signals)


def solution(mesh):
    placed = (
        P(None, "azim", "axial"),
        P(None, None, "azim", "axial"),
        P(None, "azim", "axial"),
        P(None, None, "azim", "axial"),
        P(None, None, "azim", "axial"),
        P(None, "azim", "axial"),
        P(None, None, "azim", "axial"),
        P("azim", "axial"),
        P(None, "azim", "axial"),
        P(None, "azim", "axial"),
        P(None, "azim", "axial"),
        P(),
    )
    return jax.shard_map(
        per_device,
        mesh=mesh,
        in_specs=placed,
        out_specs=(P(None, None, "azim", "axial"), P(("axial", "azim"), None)),
        check_vma=False,
    )
```

```python
import functools
import math

import jax
import jax.numpy as jnp
import numpy as np
from jax import lax
from jax.experimental import pallas as pl
from jax.experimental.pallas import tpu as pltpu
from jax.sharding import PartitionSpec as P

OBSERVERS = 512
TIME_BINS = 128

GAMMA = 1.4
SECTION = 0.25
DERIV_ALPHA = 1.0 / 3.0
FILTER_ALPHA = 0.499
FIELDS = 5
BASIS = 8
VMEM_LIMIT = 16 * 1024 * 1024
INPUT_LIMIT = 60 * 1024 * 1024


def decay_root(alpha):
    return (-1.0 + math.sqrt(1.0 - 4.0 * alpha * alpha)) / (2.0 * alpha)


DERIV_ROOT = decay_root(DERIV_ALPHA)
FILTER_ROOT = decay_root(FILTER_ALPHA)

DERIV_NEAR = 1.0 / 12.0
DERIV_FAR = (
    (25.0 / 36.0) * (DERIV_ROOT - 1.0 / DERIV_ROOT) / (1.0 + 2.0 * DERIV_ALPHA * DERIV_ROOT)
)

_B = FILTER_ALPHA
_EDGE = (1.0 - 2.0 * _B) / 64.0
_Q2 = 1.0 / _B
_Q1 = (-6.0 - _Q2) / _B
_Q0 = (12.0 - _Q1) / _B
_RHO = -8.0 - _Q0
FILTER_MID = _EDGE * (_Q0 + 2.0 * _Q2)
FILTER_ONE = _EDGE * _Q1
FILTER_TWO = _EDGE * _Q2
FILTER_FAR = _EDGE * _RHO / (1.0 + 2.0 * _B * FILTER_ROOT)


def open_operator(length, alpha, side):
    base = decay_root(alpha)
    tri = np.eye(length) + alpha * (np.eye(length, k=1) + np.eye(length, k=-1))
    tri[0, 0] = -alpha / base
    return np.linalg.solve(tri, side)


def deriv_matrix(length):
    return (7.0 / 9.0) * (np.eye(length, k=1) - np.eye(length, k=-1)) + (1.0 / 36.0) * (
        np.eye(length, k=2) - np.eye(length, k=-2)
    )


def filter_matrix(length):
    beta = FILTER_ALPHA
    coeffs = [
        (11.0 + 10.0 * beta) / 16.0,
        (15.0 + 34.0 * beta) / 32.0,
        (-3.0 + 6.0 * beta) / 16.0,
        (1.0 - 2.0 * beta) / 32.0,
    ]
    total = coeffs[0] * np.eye(length)
    for shift in range(1, 4):
        total = total + 0.5 * coeffs[shift] * (np.eye(length, k=shift) + np.eye(length, k=-shift))
    return total


def axial_tables(count, width, alpha, kind):
    length = count * width
    side = deriv_matrix(length) if kind == "deriv" else filter_matrix(length)
    whole = open_operator(length, alpha, side)
    base = decay_root(alpha)
    basis = np.zeros((BASIS, width))
    for edge in range(3):
        basis[edge, edge] = 1.0
        basis[3 + edge, width - 3 + edge] = 1.0
    basis[6] = base ** np.arange(width - 1, -1, -1, dtype=np.float64)
    basis[7] = base ** np.arange(width, dtype=np.float64)
    inverse = np.linalg.pinv(basis)
    own = np.zeros((count, width, width))
    far = np.zeros((count, max(count - 1, 1) * BASIS, width))
    for here in range(count):
        rows = whole[here * width : (here + 1) * width]
        own[here] = rows[:, here * width : (here + 1) * width].T
        if kind == "filter":
            own[here] -= np.eye(width)
        for shift in range(1, count):
            there = (here - shift) % count
            block = rows[:, there * width : (there + 1) * width]
            far[here, (shift - 1) * BASIS : shift * BASIS] = (block @ inverse).T
    return own, basis, far


def cycle_operator(length, alpha, coeffs, sign):
    turn = np.roll(np.eye(length), 1, axis=1)
    side = coeffs[0] * np.eye(length)
    for shift in range(1, len(coeffs)):
        step = np.linalg.matrix_power(turn, shift)
        side = side + coeffs[shift] * (step + sign * step.T)
    return np.linalg.solve(np.eye(length) + alpha * (turn + turn.T), side)


def surface_tables(along, width, around, rows):
    length, ring = along * width, around * rows
    deriv_along = open_operator(length, DERIV_ALPHA, deriv_matrix(length)).T
    deriv_around = cycle_operator(ring, DERIV_ALPHA, [0.0, 7.0 / 9.0, 1.0 / 36.0], -1.0)
    filter_along = open_operator(length, FILTER_ALPHA, filter_matrix(length))
    filter_along = filter_along.reshape(along, width, length).transpose(0, 2, 1)
    beta = FILTER_ALPHA
    coeffs = [
        (11.0 + 10.0 * beta) / 16.0,
        (15.0 + 34.0 * beta) / 64.0,
        (-3.0 + 6.0 * beta) / 32.0,
        (1.0 - 2.0 * beta) / 64.0,
    ]
    filter_around = cycle_operator(ring, beta, coeffs, 1.0).reshape(around, rows, ring)
    return (
        halves(deriv_along),
        halves(deriv_around),
        filter_along.astype(np.float32),
        filter_around.astype(np.float32),
    )


def halves(table):
    high = np.asarray(table, np.float32).astype(jnp.bfloat16)
    low = (np.asarray(table, np.float64) - high.astype(np.float64)).astype(jnp.bfloat16)
    return np.stack([high, low], axis=-3)


def split(values):
    high = values.astype(jnp.bfloat16)
    return high, (values - high.astype(jnp.float32)).astype(jnp.bfloat16)


def dots(left, right, dims):
    out = None
    for a, b in ((0, 0), (1, 0), (0, 1)):
        part = lax.dot_general(
            left[a], right[b], (dims, ((), ())), preferred_element_type=jnp.float32
        )
        out = part if out is None else out + part
    return out


def outgoing(basis_ref, lines):
    return dots((basis_ref[0], basis_ref[1]), split(lines), ((1,), (1,)))


def incoming(parts, far_ref):
    return dots(split(jnp.concatenate(parts, axis=0)), (far_ref[0], far_ref[1]), ((0,), (0,)))


def own_block(lines, own_ref):
    return dots(split(lines), (own_ref[0], own_ref[1]), ((1,), (0,)))


def tile_energy(density, velocity, pressure):
    return pressure * (1.0 / (GAMMA - 1.0)) + 0.5 * density * (
        velocity[0] * velocity[0] + velocity[1] * velocity[1] + velocity[2] * velocity[2]
    )


def tile_flux(density, velocity, pressure, energy, metric, volume):
    contra = metric[0] * velocity[0] + metric[1] * velocity[1] + metric[2] * velocity[2]
    volume_contra = volume * contra
    mass = density * volume_contra
    push = volume * pressure
    pieces = [mass]
    for comp in range(3):
        pieces.append(mass * velocity[comp] + metric[comp] * push)
    pieces.append((energy + pressure) * volume_contra)
    return pieces


def core_index():
    return lax.rem(lax.axis_index("azim"), 2)


def chip_index():
    return lax.div(lax.axis_index("azim"), 2)


def ring_weights(chips, turn, wide):
    levels = chips.bit_length() - 1
    size = 2 * (levels + 1)
    sends = np.zeros((levels, 2, chips, size))
    sums = np.zeros((2, chips, size))
    unit = np.eye(size)
    for chip in range(chips):
        spot = (chip + turn) % chips
        head, tail = unit[0], unit[1]
        left = right = np.zeros(size)
        for level in range(levels):
            group = 1 << level
            inside = spot % group
            sends[level, :, chip] = head, tail
            head_in, tail_in = unit[2 * level + 2], unit[2 * level + 3]
            if (spot >> level) & 1:
                left = left + wide**inside * head_in
                head, tail = head + wide**group * head_in, tail_in + wide**group * tail
            else:
                right = right + wide ** (group - 1 - inside) * tail_in
                head, tail = head_in + wide**group * head, tail + wide**group * tail_in
        close = 1.0 / (1.0 - wide**chips)
        sums[0, chip] = left + close * wide**spot * head
        sums[1, chip] = right + close * wide ** (chips - 1 - spot) * tail
    return sends, sums


def chosen(index, values):
    if not np.any(values):
        return None
    out = jnp.float32(values[0])
    for at in range(1, len(values)):
        if values[at] != values[at - 1] or np.any(values != values[0]):
            out = jnp.where(index == at, jnp.float32(values[at]), out)
    return out


def slot(value, field, height):
    start = (value * FIELDS + field) * height
    return slice(start, start + height)


def mixed(chip, table, sources, field, height):
    total = None
    for at, source in enumerate(sources):
        for part in range(2):
            weight = chosen(chip, table[:, 2 * at + part])
            if weight is not None:
                term = weight * source[slot(part, field, height)]
                total = term if total is None else total + term
    return total


def moments(tiles, root):
    head = tail = tiles[0]
    for row in range(1, len(tiles)):
        head = tiles[row] + root * head
        tail = tail + (root**row) * tiles[row]
    return head, tail


def fetched(sources, buffers, sem, pieces):
    copies = [
        [
            pltpu.make_async_copy(source.at[where], buffer.at[there], sem.at[at, n])
            for n, (source, buffer, (where, there)) in enumerate(zip(sources, buffers, piece))
        ]
        for at, piece in enumerate(pieces)
    ]
    for group in copies:
        for copy in group:
            copy.start()
    return copies


def azim_flux_kernel(mine, density, velocity, pressure, azim_metric, volume, out, pack, *scratch):
    *buffers, flux, sem = scratch
    chunks, _, rows, planes, _ = out.shape
    core = core_index()
    start = (core if mine else 1 - core) * chunks * planes
    pieces = []
    for chunk in range(chunks):
        here, there = pl.ds(start + chunk * planes, planes), pl.ds(chunk * planes, planes)
        whole = slice(None)
        pieces.append(
            [(here, there), ((whole, here), (whole, there)), (here, there)]
            + [((whole, here), (whole, there)), (here, there)]
        )
    groups = fetched((density, velocity, pressure, azim_metric, volume), buffers, sem, pieces)
    first = core == 0
    for chunk in range(chunks):
        for copy in groups[chunk]:
            copy.wait()
        rho_in, vel_in, pres_in, metric_in, vol_in = buffers
        for plane in range(planes):
            at = chunk * planes + plane
            rho, pres = rho_in[at], pres_in[at]
            vel = [vel_in[c, at] for c in range(3)]
            energy = tile_energy(rho, vel, pres)
            metric = [metric_in[c, at] for c in range(3)]
            for f, piece in enumerate(tile_flux(rho, vel, pres, energy, metric, vol_in[at])):
                flux[f, plane] = piece
        for f in range(FIELDS):
            turned = jnp.swapaxes(flux[f], 0, 1)
            out[chunk, f] = turned
            tiles = [turned[row] for row in range(rows)]
            pack[chunk, 0, f], pack[chunk, 1, f] = moments(tiles, DERIV_ROOT)
            pack[chunk, 2, f] = jnp.where(first, tiles[0], tiles[rows - 1])


def put_moments(field, head, tail, low, high, held):
    on_left = lax.rem(chip_index() + pl.program_id(0), 2) == 0
    near, height = len(low), head.shape[0]
    held[slot(0, field, height)] = head
    held[slot(1, field, height)] = tail
    for n in range(near):
        held[slot(2 + n, field, height)] = jnp.where(on_left, high[n], low[n])
        held[slot(2 + near + n, field, height)] = jnp.where(on_left, low[n], high[n])


def hand_out(held, pack_a, pack_b, edge_a, edge_b):
    size = held.shape[0] - edge_a.shape[0]
    for turn, (pack, edge) in enumerate(((pack_a, edge_a), (pack_b, edge_b))):

        @pl.when(pl.program_id(0) == turn)
        def _(pack=pack, edge=edge):
            pack[:size] = held[:size]
            edge[...] = held[size:]


def chip_moments_kernel(rows, keep, other, pack_a, pack_b, edge_a, edge_b):
    first = core_index() == 0
    decay, one = jnp.float32(DERIV_ROOT**rows), jnp.float32(1.0)
    near, away = jnp.where(first, decay, one), jnp.where(first, one, decay)
    height = keep.shape[3]
    for turn, (pack, edge) in enumerate(((pack_a, edge_a), (pack_b, edge_b))):
        on_left = lax.rem(chip_index() + turn, 2) == 0
        mine = first != on_left
        for f in range(FIELDS):
            head, tail, row = (keep[turn, n, f] for n in range(3))
            head_in, tail_in, row_in = (other[turn, n, f] for n in range(3))
            pack[slot(0, f, height)] = near * head + away * head_in
            pack[slot(1, f, height)] = away * tail + near * tail_in
            pack[slot(2, f, height)] = jnp.where(mine, row, row_in)
            edge[slot(0, f, height)] = jnp.where(mine, row_in, row)


def totals_kernel(table, joined, near, height, shares, *refs):
    chip = chip_index()
    if shares:
        *refs, held, send_a, send_b, kept = refs
    else:
        *refs, send_a, send_b = refs
    count = len(refs) // 2
    for turn, send in enumerate((send_a, send_b)):
        mine = refs[turn * count : (turn + 1) * count]
        sources = mine[:-1] if joined else mine
        for f in range(FIELDS):
            send[slot(0, f, height)] = mixed(chip, table[turn][0], sources, f, height)
            send[slot(1, f, height)] = mixed(chip, table[turn][1], sources, f, height)
        if joined:
            size = 2 * FIELDS * height
            send[size : size + mine[-1].shape[0]] = mine[-1][...]
        if shares and turn == 0:
            source = sources[-1]
            into = send.shape[0] - kept.shape[0]
            arrived = source.shape[0] - held.shape[0]
            for at in range(held.shape[0] // shares):
                spot = at * shares
                total = held[spot : spot + shares] + source[arrived + spot : arrived + spot + shares]
                there = (at // 2) * shares
                if at % 2:
                    send[into + there : into + there + shares] = total
                else:
                    kept[there : there + shares] = total


def ring_kernel(table, near, height, shares, *refs):
    chip = chip_index()
    if shares:
        *refs, held, out, signals_kept, signals_sent = refs
    else:
        *refs, out = refs
    count = len(refs) // 2
    for turn in range(2):
        *sources, edge = refs[turn * count : (turn + 1) * count]
        on_left = lax.rem(chip + turn, 2) == 0
        start = 0 if edge.shape[0] == near * FIELDS * height else 2
        for f in range(FIELDS):
            out[turn, 0, f] = mixed(chip, table[turn][0], sources, f, height)
            out[turn, 1, f] = mixed(chip, table[turn][1], sources, f, height)
            for n in range(near):
                paired = sources[1][slot(2 + n, f, height)]
                other = edge[slot(start + n, f, height)]
                out[turn, 2 + n, f] = jnp.where(on_left, other, paired)
                out[turn, 2 + near + n, f] = jnp.where(on_left, paired, other)
        if shares and turn == 0:
            source = sources[-1]
            total = held[...] + source[source.shape[0] - shares :]
            half = shares // 2
            first = core_index() == 0
            signals_kept[...] = jnp.where(first, total[:half], total[half:])
            signals_sent[...] = jnp.where(first, total[half:], total[:half])


def section_local_kernel(
    density,
    velocity,
    pressure,
    axial_metric,
    volume,
    radial,
    own,
    basis,
    base_out,
    scale_out,
    edge_out,
    axial_flux,
    start,
):
    planes, rows, lanes = density.shape
    for plane in range(planes):
        rho = density[plane]
        vel = [velocity[c, plane] for c in range(3)]
        pres = pressure[plane]
        vol = volume[plane]
        energy = tile_energy(rho, vel, pres)
        axial = tile_flux(rho, vel, pres, energy, [axial_metric[c, plane] for c in range(3)], vol)
        state = [rho, rho * vel[0], rho * vel[1], rho * vel[2], energy]
        for f in range(FIELDS):
            axial_flux[f, plane] = axial[f]
            start[f, plane] = state[f] + SECTION * radial[f, plane]
    scale = jnp.swapaxes(SECTION / volume[...], 0, 1)
    scale_out[0] = scale
    for f in range(FIELDS):
        flux = jnp.swapaxes(axial_flux[f], 0, 1).reshape(rows * planes, lanes)
        edge_out[:, f * rows * planes : (f + 1) * rows * planes] = outgoing(basis, flux)
        deriv = own_block(flux, own).reshape(rows, planes, lanes)
        base_out[0, f] = jnp.swapaxes(start[f], 0, 1) - scale * deriv


def section_axial_kernel(base, scale, far, *rest):
    edges, out = rest[:-1], rest[-1]
    rows, planes, lanes = scale.shape[1:]
    for f in range(FIELDS):
        spot = slice(f * rows * planes, (f + 1) * rows * planes)
        axial = incoming([ref[:, spot] for ref in edges], far).reshape(rows, planes, lanes)
        out[0, f] = base[0, f] - scale[0] * axial
    out[0, FIELDS] = scale[0]


def section_azim_kernel(flux_keep, flux_in, base_keep, base_in, out, scale_out):
    rows = flux_keep.shape[2]
    first = core_index() == 0

    def both(mine, theirs, f):
        low = [jnp.where(first, mine[0, f, row], theirs[0, f, row]) for row in range(rows)]
        high = [jnp.where(first, theirs[0, f, row], mine[0, f, row]) for row in range(rows)]
        return low + high

    scale = both(base_keep, base_in, FIELDS)
    for row in range(2 * rows):
        scale_out[0, row] = scale[row]
    for f in range(FIELDS):
        azim = both(flux_keep, flux_in, f)
        base = both(base_keep, base_in, f)
        last = 2 * rows - 1
        down = [None] * (last + 1)
        down[last] = azim[last]
        for row in range(last - 1, -1, -1):
            down[row] = azim[row] + DERIV_ROOT * down[row + 1]
        up = None
        for row in range(last + 1):
            up = azim[row] if row == 0 else azim[row] + DERIV_ROOT * up
            total = DERIV_FAR * (up - down[row])
            if row > 0:
                total = total - DERIV_NEAR * azim[row - 1]
            if row < last:
                total = total + DERIV_NEAR * azim[row + 1]
            out[0, f, row] = base[row] - scale_out[0, row] * total


def section_join_kernel(base, scale, ring, basis, partial, out, *edges):
    rows, planes, lanes = scale.shape[1:]
    step = pl.program_id(0)
    width = rows * planes
    for f in range(FIELDS):
        left, right, before, after = (ring[0, n, f] for n in range(4))
        for row in range(rows):
            azim = (DERIV_FAR * DERIV_ROOT ** (row + 1)) * left - (
                DERIV_FAR * DERIV_ROOT ** (rows - row)
            ) * right
            if row == 0:
                azim = azim - DERIV_NEAR * before
            if row == rows - 1:
                azim = azim + DERIV_NEAR * after
            out[0, f, row] = base[0, f, row] - scale[0, row] * azim
        sent = outgoing(basis, out[0, f].reshape(width, lanes))
        spot = pl.multiple_of((step * FIELDS + f) * width, 128)
        for edge in edges:
            edge[:, pl.ds(spot, width)] = sent

    @pl.when(step == 0)
    def _():
        count = len(edges) + 1
        share = partial.shape[0] // count
        for shift, edge in enumerate(edges, start=1):
            owner = lax.rem(lax.axis_index("axial") + shift, count)
            start = edge.shape[1] - share // 8 * lanes
            for at in range(share // 8):
                piece = pl.multiple_of(owner * share + 8 * at, 8)
                edge[:, start + at * lanes : start + (at + 1) * lanes] = partial[pl.ds(piece, 8), :]


def axial_local_kernel(values, own, out):
    lines = values[0].reshape(-1, values.shape[-1])
    out[0] = (lines + own_block(lines, own)).reshape(out.shape[1:])


def mirror_masks(chips):
    return [(2 << level) - 1 for level in range(chips.bit_length() - 1)]


def axial_join_kernel(chips, local, far, partial, *rest):
    edges, (out, *outs, kept, held, summed) = rest[:-8], rest[-8:]
    rows, planes, lanes = local.shape[2:]
    step = pl.program_id(0)
    width = rows * planes
    for f in range(FIELDS):
        spot = pl.multiple_of((step * FIELDS + f) * width, 128)
        axial = incoming([ref[:, pl.ds(spot, width)] for ref in edges], far)
        axial = axial.reshape(rows, planes, lanes)
        tiles = [local[0, f, row] + axial[row] for row in range(rows)]
        for row in range(rows):
            out[0, f, row] = tiles[row]
        head, tail = moments(tiles, FILTER_ROOT)
        put_moments(f, head, tail, tiles[:2], tiles[rows - 2 :], held)
    hand_out(held, *outs)

    @pl.when(step == 0)
    def _():
        share = summed.shape[0]
        start = edges[0].shape[1] - share // 8 * lanes
        mine = lax.axis_index("axial") * share
        for at in range(share // 8):
            total = partial[pl.ds(pl.multiple_of(mine + 8 * at, 8), 8), :]
            for edge in edges:
                total = total + edge[:, start + at * lanes : start + (at + 1) * lanes]
            summed[8 * at : 8 * at + 8] = total
        size = share // chips
        send = outs[0]
        into = send.shape[0] - kept.shape[0]
        masks = mirror_masks(chips)
        for at in range(chips):
            there = chip_index()
            for level, mask in enumerate(masks):
                if (at >> level) & 1:
                    there = jnp.bitwise_xor(there, mask)
            rows_there = summed[pl.ds(pl.multiple_of(there * size, 8), size), :]
            place = (at // 2) * size
            if at % 2:
                send[into + place : into + place + size] = rows_there
            else:
                kept[place : place + size] = rows_there


def azim_local_kernel(values, out):
    rows = values.shape[2]
    for f in range(FIELDS):
        down = [None] * rows
        down[rows - 1] = values[0, f, rows - 1]
        for row in range(rows - 2, -1, -1):
            down[row] = values[0, f, row] + FILTER_ROOT * down[row + 1]
        up = None
        for row in range(rows):
            here = values[0, f, row]
            up = here if row == 0 else here + FILTER_ROOT * up
            total = (1.0 + FILTER_MID - FILTER_FAR) * here + FILTER_FAR * (up + down[row])
            for step, weight in ((1, FILTER_ONE), (2, FILTER_TWO)):
                if row >= step:
                    total = total + weight * values[0, f, row - step]
                if row + step < rows:
                    total = total + weight * values[0, f, row + step]
            out[0, f, row] = total


def joined_rows(upper, local, ring, field):
    rows = local.shape[2]
    one, zero = jnp.float32(1.0), jnp.float32(0.0)
    decay = jnp.float32(FILTER_ROOT**rows)
    left = jnp.where(upper, decay, one) * ring[0, 0, field]
    right = jnp.where(upper, one, decay) * ring[0, 1, field]
    low, high = jnp.where(upper, zero, one), jnp.where(upper, one, zero)
    before = [low * ring[0, 2 + n, field] for n in range(2)]
    after = [high * ring[0, 4 + n, field] for n in range(2)]
    tiles = []
    for row in range(rows):
        total = (
            local[0, field, row]
            + (FILTER_FAR * FILTER_ROOT ** (row + 1)) * left
            + (FILTER_FAR * FILTER_ROOT ** (rows - row)) * right
        )
        if row < 2:
            total = total + FILTER_TWO * before[row]
        if row == 0:
            total = total + FILTER_ONE * before[1]
        if row >= rows - 2:
            total = total + FILTER_TWO * after[row - (rows - 2)]
        if row == rows - 1:
            total = total + FILTER_ONE * after[0]
        tiles.append(total)
    return tiles


def azim_send_kernel(local, ring, signals, out):
    height = local.shape[3]
    for f in range(FIELDS):
        for row, tile in enumerate(joined_rows(core_index() == 0, local, ring, f)):
            start = (f * local.shape[2] + row) * height
            out[0, start : start + height] = tile
    end = FIELDS * local.shape[2] * height
    out[0, end : end + signals.shape[0]] = signals[...]


def azim_keep_kernel(local, ring, out):
    for f in range(FIELDS):
        tiles = joined_rows(core_index() == 1, local, ring, f)
        out[f] = jnp.swapaxes(jnp.stack(tiles), 0, 1)


def place_rows_kernel(values, kept, partial, out, signals):
    planes, rows, lanes = out.shape[1:]
    size = rows * planes
    for f in range(FIELDS):
        turned = values[0, f * size : (f + 1) * size].reshape(rows, planes, lanes)
        out[f] = jnp.swapaxes(turned, 0, 1)
    signals[...] = kept[...] + values[0, FIELDS * size : FIELDS * size + kept.shape[0]]


def front_kernel(
    density, velocity, pressure, axial_metric, azim_metric, volume, radial, out, *scratch
):
    *buffers, sem = scratch
    sources = (density, velocity, pressure, axial_metric, azim_metric, volume, radial)
    whole = slice(None)
    one, many = (pl.ds(0, 1), whole), ((whole, pl.ds(0, 1)), whole)
    (group,) = fetched(sources, buffers, sem, [[one, many, one, many, many, one, many]])
    for copy in group:
        copy.wait()
    rho_in, vel_in, pres_in, axial_in, azim_in, vol_in, radial_in = buffers
    rho, pres, vol = rho_in[0], pres_in[0], vol_in[0]
    vel = [vel_in[c, 0] for c in range(3)]
    energy = tile_energy(rho, vel, pres)
    axial = tile_flux(rho, vel, pres, energy, [axial_in[c, 0] for c in range(3)], vol)
    azim = tile_flux(rho, vel, pres, energy, [azim_in[c, 0] for c in range(3)], vol)
    base = rho + rho * vel[1] + SECTION * (radial_in[0, 0] + radial_in[2, 0])
    for at, piece in enumerate((base, SECTION / vol, axial[0] + axial[2], azim[0] + azim[2])):
        for device in range(out.shape[0]):
            out[device, at] = piece


def signals_kernel(
    fronts,
    deriv_along,
    deriv_around,
    filter_along,
    filter_around,
    weight_table,
    weights,
    area,
    observers,
    bins,
    out,
    *scratch,
):
    *buffers, chosen_rows, chosen_bins, sem = scratch
    sources = (fronts, deriv_along, deriv_around, filter_along, filter_around)
    sources = sources + (weight_table, weights, area, observers, bins)
    whole = slice(None)
    pieces = [(whole, whole)] * len(sources)
    pieces[3] = (lax.axis_index("axial"), whole)
    pieces[4] = (lax.axis_index("azim"), whole)
    (group,) = fetched(sources, buffers, sem, [pieces])
    for copy in group:
        copy.wait()
    fronts, deriv_along, deriv_around, filter_along, filter_around = buffers[:5]
    weight_table, weights, area, observers, bins = buffers[5:]
    entries, rows, lanes = weights.shape
    columns = filter_around.shape[1] // rows
    count = fronts.shape[0] // columns

    def plane(at):
        blocks = [
            jnp.concatenate([fronts[a * columns + c, at] for c in range(columns)], axis=0)
            for a in range(count)
        ]
        return jnp.concatenate(blocks, axis=1)

    base, scale, axial, azim = (plane(at) for at in range(4))
    deriv = dots(split(axial), (deriv_along[0], deriv_along[1]), ((1,), (0,)))
    deriv = deriv + dots((deriv_around[0], deriv_around[1]), split(azim), ((1,), (0,)))
    section = base - scale * deriv
    smooth = jnp.dot(
        filter_around[...],
        section,
        precision=lax.Precision.HIGHEST,
        preferred_element_type=jnp.float32,
    )
    surface = -1.0 + jnp.dot(
        smooth,
        filter_along[...],
        precision=lax.Precision.HIGHEST,
        preferred_element_type=jnp.float32,
    )
    surface = area[...] * surface
    observer_rows = lax.broadcasted_iota(jnp.int32, (out.shape[0], lanes), 0)
    bin_rows = lax.broadcasted_iota(jnp.int32, (out.shape[1], lanes), 0)
    height = out.shape[1]
    for entry in range(entries):
        picked = weights[entry]
        found = jnp.zeros(picked.shape, jnp.float32)
        for t in range(weight_table.shape[0]):
            found = jnp.where(picked == t, weight_table[t], found)
        values = found * surface
        for row in range(rows):
            at = (row * entries + entry) * lanes
            hit = observer_rows == observers[entry, row : row + 1, :]
            chosen_rows[:, at : at + lanes] = jnp.where(hit, 1.0, 0.0).astype(jnp.bfloat16)
            hit = bin_rows == bins[entry, row : row + 1, :]
            high, low = split(jnp.where(hit, values[row : row + 1, :], 0.0))
            chosen_bins[:height, at : at + lanes] = high
            chosen_bins[height:, at : at + lanes] = low
    total = lax.dot_general(
        chosen_rows[...],
        chosen_bins[...],
        (((1,), (1,)), ((), ())),
        preferred_element_type=jnp.float32,
    )
    out[...] = total[:, :height] + total[:, height:]


def params(limit=VMEM_LIMIT):
    return pltpu.CompilerParams(vmem_limit_bytes=limit)


def cost(flops, moved):
    return pl.CostEstimate(flops=1, bytes_accessed=1, transcendentals=0)


def rotate(values, axis, count, shift):
    return lax.ppermute(values, axis, [(i, (i + shift) % count) for i in range(count)])


def sibling(values, count):
    return lax.ppermute(values, "azim", [(i, i ^ 1) for i in range(count)])


def partner(values, count, turn, level):
    chips = count // 2
    pairs = []
    for i in range(count):
        chip, core = divmod(i, 2)
        there = ((((chip + turn) % chips) ^ ((2 << level) - 1)) - turn) % chips
        pairs.append((i, 2 * there + core))
    return lax.ppermute(values, "azim", pairs)


def waiting(kernel, count, wait):
    if not wait:
        return kernel
    return lambda *refs: kernel(*refs[:count], *refs[count + len(wait) :])


def whole_call(kernel, name, shapes, args, wait=()):
    whole = pl.BlockSpec(memory_space=pltpu.VMEM)
    return pl.pallas_call(
        waiting(kernel, len(args), wait),
        in_specs=[whole] * len(args) + [pl.BlockSpec(memory_space=pl.ANY)] * len(wait),
        out_specs=[whole] * len(shapes),
        out_shape=shapes,
        compiler_params=params(),
        cost_estimate=cost(1, 1),
        name=name,
    )(*args, *wait)


def ring_exchange(packs, edges, count, near, height, wide, wait=(), held=None, shares=0):
    chips = count // 2
    levels = chips.bit_length() - 1
    tables = [ring_weights(chips, turn, wide) for turn in range(2)]
    lanes = packs[0].shape[1]
    rows = FIELDS * height
    joined = levels == 2

    def flat(size):
        return jax.ShapeDtypeStruct((size, lanes), jnp.float32)

    sources = [[packs[turn], partner(packs[turn], count, turn, 0)] for turn in range(2)]
    if not joined:
        edges = [partner(edges[turn], count, 1 - turn, 0) for turn in range(2)]
    for level in range(1, levels):
        size = (2 + near if joined else 2) * rows
        args = [a for turn in range(2) for a in sources[turn] + ([edges[turn]] if joined else [])]
        shapes = [flat(size), flat(size)]
        if shares:
            args.append(held)
            left = held.shape[0] // 2
            shapes = [flat(size + left), flat(size), flat(left)]
        sends = whole_call(
            functools.partial(
                totals_kernel, [t[0][level] for t in tables], joined, near, height, shares
            ),
            "group_totals",
            shapes,
            args,
            wait,
        )
        if shares:
            held = sends[2]
        for turn in range(2):
            sources[turn].append(partner(sends[turn], count, turn, level))
    args = [
        a for turn in range(2) for a in sources[turn] + [sources[turn][-1] if joined else edges[turn]]
    ]
    shapes = [jax.ShapeDtypeStruct((2, 2 + 2 * near, FIELDS, height, lanes), jnp.float32)]
    if shares:
        args.append(held)
        shapes = shapes + [flat(shares // 2)] * 2

    def sums(wait=()):
        return whole_call(
            functools.partial(ring_kernel, [t[1] for t in tables], near, height, shares),
            "ring_sums",
            shapes,
            args,
            wait,
        )

    return sums, sends[0]


def per_device(
    density,
    velocity,
    pressure,
    axial_metric,
    azim_metric,
    volume,
    radial_term,
    panel_area,
    observer_ids,
    bin_ids,
    weight_ids,
    bin_weights,
):
    planes, rows, lanes = density.shape
    along = lax.axis_size("axial")
    around = lax.axis_size("azim")
    devices = along * around
    part = planes // 4
    lines = FIELDS * rows * part
    f32 = jnp.float32

    own_d, basis_d, far_d = map(halves, axial_tables(along, lanes, DERIV_ALPHA, "deriv"))
    own_f, basis_f, far_f = map(halves, axial_tables(along, lanes, FILTER_ALPHA, "filter"))
    deriv_along, deriv_around, filter_along, filter_around = surface_tables(
        along, lanes, around, rows
    )

    spec = pl.BlockSpec

    def every(k):
        return k

    def kept(k):
        return core_index() * 2 + k

    def sent(k):
        return (1 - core_index()) * 2 + k

    def field(where):
        return spec((part, rows, lanes), lambda k: (where(k), 0, 0))

    def vector(where, size=3):
        return spec((size, part, rows, lanes), lambda k: (0, where(k), 0, 0))

    def inner(where, size=FIELDS, tall=rows):
        return spec((1, size, tall, part, lanes), lambda k: (where(k), 0, 0, 0, 0))

    def inner_one(where, tall=rows):
        return spec((1, tall, part, lanes), lambda k: (where(k), 0, 0, 0))

    def edge(where, width=lines):
        return spec((BASIS, width), lambda k: (0, where(k)))

    def row_half(upper):
        return spec((1, FIELDS, rows, part, lanes), lambda k: (k, 0, upper(), 0, 0))

    def table(array):
        return spec((None,) + array.shape[1:], lambda k: (lax.axis_index("axial"),) + (0,) * (array.ndim - 1))

    def fixed(shape):
        return spec(shape, lambda k: (0,) * len(shape))

    def ring_spec(near):
        return spec((1, 2 + 2 * near, FIELDS, part, lanes), lambda k: (k, 0, 0, 0, 0))

    def shaped(*shape):
        return jax.ShapeDtypeStruct(shape, f32)

    def call(
        kernel, name, steps, ins, outs, shapes, args, wait=(), limit=VMEM_LIMIT, scratch=(), **more
    ):
        return pl.pallas_call(
            waiting(kernel, len(args), wait),
            grid=(steps,),
            in_specs=ins + [spec(memory_space=pl.ANY)] * len(wait),
            out_specs=outs,
            scratch_shapes=scratch,
            out_shape=shapes,
            compiler_params=params(limit),
            cost_estimate=cost(1, 1),
            name=name,
            **more,
        )(*args, *wait)

    tall = 2 * rows
    flux_scratch = pltpu.VMEM((FIELDS, part, rows, lanes), f32)
    half_shape = shaped(2, FIELDS, rows, part, lanes)
    chip_shape = shaped(2, FIELDS, tall, part, lanes)

    def apart(kernel, name, shapes, args, scratch, wait=(), limit=INPUT_LIMIT):
        several = isinstance(shapes, list)
        vmem = spec(memory_space=pltpu.VMEM)
        return pl.pallas_call(
            waiting(kernel, len(args), wait),
            in_specs=[spec(memory_space=pltpu.HBM)] * len(args)
            + [spec(memory_space=pl.ANY)] * len(wait),
            out_specs=[vmem] * len(shapes) if several else vmem,
            out_shape=shapes,
            scratch_shapes=scratch,
            compiler_params=params(limit),
            cost_estimate=cost(1, 1),
            name=name,
        )(*args, *wait)

    one, three, five = [(1, rows, lanes)], [(3, 1, rows, lanes)], [(FIELDS, 1, rows, lanes)]
    front = apart(
        front_kernel,
        "surface_front",
        shaped(devices, 4, rows, lanes),
        (density, velocity, pressure, axial_metric, azim_metric, volume, radial_term),
        [pltpu.VMEM(shape, f32) for shape in one + three + one + three + three + one + five]
        + [pltpu.SemaphoreType.DMA((1, 7))],
    )
    fronts = lax.all_to_all(front, ("axial", "azim"), 0, 0, tiled=True)

    def azim_flux(mine, name, wait=()):
        one, three = (2 * part, rows, lanes), (3, 2 * part, rows, lanes)
        return apart(
            functools.partial(azim_flux_kernel, mine),
            name,
            [half_shape, shaped(2, 3, FIELDS, part, lanes)],
            (density, velocity, pressure, azim_metric, volume),
            [pltpu.VMEM(shape, f32) for shape in (one, three, one, three, one)]
            + [flux_scratch, pltpu.SemaphoreType.DMA((2, 5))],
            wait,
        )

    flux_sent, pack_sent = azim_flux(False, "azim_flux_sent", (front,))
    pack_in = sibling(pack_sent, around)
    flux_in = sibling(flux_sent, around)
    flux_kept, pack_kept = azim_flux(True, "azim_flux_kept")
    *packs, edge_a, edge_b = whole_call(
        functools.partial(chip_moments_kernel, rows),
        "chip_moments",
        [shaped(3 * FIELDS * part, lanes)] * 2 + [shaped(FIELDS * part, lanes)] * 2,
        (pack_kept, pack_in),
    )

    base, scale, edge_d = call(
        section_local_kernel,
        "section_local",
        4,
        [
            field(every),
            vector(every),
            field(every),
            vector(every),
            field(every),
            vector(every, FIELDS),
            table(own_d),
            fixed(basis_d.shape),
        ],
        [inner(every), inner_one(every), edge(every)],
        [
            shaped(4, FIELDS, rows, part, lanes),
            shaped(4, rows, part, lanes),
            shaped(BASIS, 4 * lines),
        ],
        (density, velocity, pressure, axial_metric, volume, radial_term, own_d, basis_d),
        wait=(packs[0], flux_in),
        scratch=[flux_scratch] * 2,
    )
    sums_d, sends_d = ring_exchange(
        packs, [edge_a, edge_b], around, 1, part, DERIV_ROOT ** (2 * rows), wait=(edge_d,)
    )
    edges_d = [rotate(edge_d, "axial", along, s) for s in range(1, along)]

    def section_axial(where, name, wait):
        return call(
            section_axial_kernel,
            name,
            2,
            [inner(where), inner_one(where), table(far_d)] + [edge(where)] * (along - 1),
            inner(every, FIELDS + 1),
            shaped(2, FIELDS + 1, rows, part, lanes),
            (base, scale, far_d, *edges_d),
            wait=wait,
        )

    base_kept = section_axial(kept, "section_axial_kept", (sends_d,))
    base_in = sibling(section_axial(sent, "section_axial_sent", (base_kept,)), around)

    operands = (
        fronts,
        jnp.asarray(deriv_along),
        jnp.asarray(deriv_around),
        jnp.asarray(filter_along),
        jnp.asarray(filter_around),
        bin_weights,
        weight_ids,
        panel_area,
        observer_ids,
        bin_ids,
    )
    scratch = [pltpu.VMEM(x.shape, x.dtype) for x in operands]
    scratch[3] = pltpu.VMEM(filter_along.shape[1:], f32)
    scratch[4] = pltpu.VMEM(filter_around.shape[1:], f32)
    scratch[5] = pltpu.SMEM(bin_weights.shape, f32)
    partial = apart(
        signals_kernel,
        "signals",
        shaped(OBSERVERS, TIME_BINS),
        operands,
        scratch
        + [
            pltpu.VMEM((OBSERVERS, weight_ids.size), jnp.bfloat16),
            pltpu.VMEM((2 * TIME_BINS, weight_ids.size), jnp.bfloat16),
            pltpu.SemaphoreType.DMA((1, len(operands))),
        ],
        wait=(sends_d,),
        limit=VMEM_LIMIT,
    )

    base_chip, scale_chip = call(
        section_azim_kernel,
        "section_azim",
        2,
        [inner(every), inner(every), inner(every, FIELDS + 1), inner(every, FIELDS + 1)],
        [inner(every, tall=tall), inner_one(every, tall)],
        [chip_shape, shaped(2, tall, part, lanes)],
        (flux_kept, flux_in, base_kept, base_in),
    )

    (ring_d,) = sums_d((partial, base_chip))

    share = OBSERVERS // along
    edge_shape = (BASIS, 4 * lines + share // 8 * lanes)
    sectioned, *edges_f = call(
        section_join_kernel,
        "section_join",
        2,
        [
            inner(every, tall=tall),
            inner_one(every, tall),
            ring_spec(1),
            fixed(basis_f.shape),
            fixed(partial.shape),
        ],
        [inner(every, tall=tall)] + [fixed(edge_shape)] * (along - 1),
        [chip_shape] + [shaped(*edge_shape)] * (along - 1),
        (base_chip, scale_chip, ring_d, basis_f, partial),
    )
    edges_f = [rotate(edges_f[s - 1], "axial", along, s) for s in range(1, along)]
    axial_local = call(
        axial_local_kernel,
        "axial_local",
        2,
        [inner(every, tall=tall), table(own_f)],
        inner(every, tall=tall),
        chip_shape,
        (sectioned, own_f),
    )
    chips = around // 2
    height = FIELDS * part
    shapes = [4 * height + share // 2, 4 * height, 2 * height, 2 * height, share // 2]
    shapes = [(size, lanes) for size in shapes]
    smoothed, *packs, edge_a, edge_b, held = call(
        functools.partial(axial_join_kernel, chips),
        "axial_join",
        2,
        [inner(every, tall=tall), table(far_f), fixed(partial.shape)]
        + [fixed(edge_shape)] * (along - 1),
        [inner(every, tall=tall)] + [fixed(shape) for shape in shapes],
        [chip_shape] + [shaped(*shape) for shape in shapes],
        (axial_local, far_f, partial, *edges_f),
        scratch=[pltpu.VMEM((6 * height, lanes), f32), pltpu.VMEM((share, lanes), f32)],
    )
    sums_f, sends_f = ring_exchange(
        packs,
        [edge_a, edge_b],
        around,
        2,
        part,
        FILTER_ROOT ** (2 * rows),
        held=held,
        shares=share // chips,
    )
    azim_local = call(
        azim_local_kernel,
        "azim_local",
        2,
        [inner(every, tall=tall)],
        inner(every, tall=tall),
        chip_shape,
        (smoothed,),
        wait=(sends_f,),
    )
    ring_f, signals_kept, signals_sent = sums_f()
    state_shape = shaped(FIELDS, planes, rows, lanes)
    own_signals = signals_kept.shape
    flat = rows * height + -(-own_signals[0] // 8) * 8
    flat_spec = spec((1, flat, lanes), lambda k: (k, 0, 0))
    rows_sent = call(
        azim_send_kernel,
        "azim_join_sent",
        2,
        [row_half(lambda: 1 - core_index()), ring_spec(2), fixed(own_signals)],
        flat_spec,
        shaped(2, flat, lanes),
        (azim_local, ring_f, signals_sent),
    )
    rows_in = sibling(rows_sent, around)
    mine = call(
        azim_keep_kernel,
        "azim_join_kept",
        2,
        [row_half(core_index), ring_spec(2)],
        vector(kept, FIELDS),
        state_shape,
        (azim_local, ring_f),
    )
    return call(
        place_rows_kernel,
        "place_rows",
        2,
        [flat_spec, fixed(own_signals), spec(memory_space=pl.ANY)],
        [vector(sent, FIELDS), fixed(own_signals)],
        [state_shape, shaped(*own_signals)],
        (rows_in, signals_kept, mine),
        input_output_aliases={2: 0},
    )


def solution(mesh):
    placed = (
        P(None, "azim", "axial"),
        P(None, None, "azim", "axial"),
        P(None, "azim", "axial"),
        P(None, None, "azim", "axial"),
        P(None, None, "azim", "axial"),
        P(None, "azim", "axial"),
        P(None, None, "azim", "axial"),
        P("azim", "axial"),
        P(None, "azim", "axial"),
        P(None, "azim", "axial"),
        P(None, "azim", "axial"),
        P(),
    )
    return jax.shard_map(
        per_device,
        mesh=mesh,
        in_specs=placed,
        out_specs=(P(None, None, "azim", "axial"), P(("axial", "azim"), None)),
        check_vma=False,
    )
```

```python
import functools
import math

import jax
import jax.numpy as jnp
import numpy as np
from jax import lax
from jax.experimental import pallas as pl
from jax.experimental.pallas import tpu as pltpu
from jax.sharding import PartitionSpec as P

OBSERVERS = 512
TIME_BINS = 128

GAMMA = 1.4
SECTION = 0.25
DERIV_ALPHA = 1.0 / 3.0
FILTER_ALPHA = 0.499
FIELDS = 5
BASIS = 8
VMEM_LIMIT = 16 * 1024 * 1024
INPUT_LIMIT = 60 * 1024 * 1024


def decay_root(alpha):
    return (-1.0 + math.sqrt(1.0 - 4.0 * alpha * alpha)) / (2.0 * alpha)


DERIV_ROOT = decay_root(DERIV_ALPHA)
FILTER_ROOT = decay_root(FILTER_ALPHA)

DERIV_NEAR = 1.0 / 12.0
DERIV_FAR = (
    (25.0 / 36.0) * (DERIV_ROOT - 1.0 / DERIV_ROOT) / (1.0 + 2.0 * DERIV_ALPHA * DERIV_ROOT)
)

_B = FILTER_ALPHA
_EDGE = (1.0 - 2.0 * _B) / 64.0
_Q2 = 1.0 / _B
_Q1 = (-6.0 - _Q2) / _B
_Q0 = (12.0 - _Q1) / _B
_RHO = -8.0 - _Q0
FILTER_MID = _EDGE * (_Q0 + 2.0 * _Q2)
FILTER_ONE = _EDGE * _Q1
FILTER_TWO = _EDGE * _Q2
FILTER_FAR = _EDGE * _RHO / (1.0 + 2.0 * _B * FILTER_ROOT)


def open_operator(length, alpha, side):
    base = decay_root(alpha)
    tri = np.eye(length) + alpha * (np.eye(length, k=1) + np.eye(length, k=-1))
    tri[0, 0] = -alpha / base
    return np.linalg.solve(tri, side)


def deriv_matrix(length):
    return (7.0 / 9.0) * (np.eye(length, k=1) - np.eye(length, k=-1)) + (1.0 / 36.0) * (
        np.eye(length, k=2) - np.eye(length, k=-2)
    )


def filter_matrix(length):
    beta = FILTER_ALPHA
    coeffs = [
        (11.0 + 10.0 * beta) / 16.0,
        (15.0 + 34.0 * beta) / 32.0,
        (-3.0 + 6.0 * beta) / 16.0,
        (1.0 - 2.0 * beta) / 32.0,
    ]
    total = coeffs[0] * np.eye(length)
    for shift in range(1, 4):
        total = total + 0.5 * coeffs[shift] * (np.eye(length, k=shift) + np.eye(length, k=-shift))
    return total


def axial_tables(count, width, alpha, kind):
    length = count * width
    side = deriv_matrix(length) if kind == "deriv" else filter_matrix(length)
    whole = open_operator(length, alpha, side)
    base = decay_root(alpha)
    basis = np.zeros((BASIS, width))
    for edge in range(3):
        basis[edge, edge] = 1.0
        basis[3 + edge, width - 3 + edge] = 1.0
    basis[6] = base ** np.arange(width - 1, -1, -1, dtype=np.float64)
    basis[7] = base ** np.arange(width, dtype=np.float64)
    inverse = np.linalg.pinv(basis)
    own = np.zeros((count, width, width))
    far = np.zeros((count, max(count - 1, 1) * BASIS, width))
    for here in range(count):
        rows = whole[here * width : (here + 1) * width]
        own[here] = rows[:, here * width : (here + 1) * width].T
        if kind == "filter":
            own[here] -= np.eye(width)
        for shift in range(1, count):
            there = here ^ shift
            block = rows[:, there * width : (there + 1) * width]
            far[here, (shift - 1) * BASIS : shift * BASIS] = (block @ inverse).T
    return own, basis, far


def surface_table(around, rows):
    length = around * rows
    turn = np.roll(np.eye(length), 1, axis=1)
    beta = FILTER_ALPHA
    side = (11.0 + 10.0 * beta) / 16.0 * np.eye(length)
    coeffs = [(15.0 + 34.0 * beta) / 64.0, (-3.0 + 6.0 * beta) / 32.0, (1.0 - 2.0 * beta) / 64.0]
    for shift, weight in enumerate(coeffs, start=1):
        step = np.linalg.matrix_power(turn, shift)
        side = side + weight * (step + step.T)
    cycle = np.linalg.solve(np.eye(length) + beta * (turn + turn.T), side)
    return cycle.reshape(around // 2, 2 * rows, length).astype(np.float32)


def halves(table):
    high = np.asarray(table, np.float32).astype(jnp.bfloat16)
    low = (np.asarray(table, np.float64) - high.astype(np.float64)).astype(jnp.bfloat16)
    return np.stack([high, low], axis=-3)


def split(values):
    high = values.astype(jnp.bfloat16)
    return high, (values - high.astype(jnp.float32)).astype(jnp.bfloat16)


def dots(left, right, dims):
    out = None
    for a, b in ((0, 0), (1, 0), (0, 1)):
        part = lax.dot_general(
            left[a], right[b], (dims, ((), ())), preferred_element_type=jnp.float32
        )
        out = part if out is None else out + part
    return out


def outgoing(basis_ref, lines):
    return dots((basis_ref[0], basis_ref[1]), split(lines), ((1,), (1,)))


def incoming(parts, far_ref):
    return dots(split(jnp.concatenate(parts, axis=0)), (far_ref[0], far_ref[1]), ((0,), (0,)))


def own_block(lines, own_ref):
    return dots(split(lines), (own_ref[0], own_ref[1]), ((1,), (0,)))


def tile_energy(density, velocity, pressure):
    return pressure * (1.0 / (GAMMA - 1.0)) + 0.5 * density * (
        velocity[0] * velocity[0] + velocity[1] * velocity[1] + velocity[2] * velocity[2]
    )


def tile_flux(density, velocity, pressure, energy, metric, volume):
    contra = metric[0] * velocity[0] + metric[1] * velocity[1] + metric[2] * velocity[2]
    volume_contra = volume * contra
    mass = density * volume_contra
    push = volume * pressure
    pieces = [mass]
    for comp in range(3):
        pieces.append(mass * velocity[comp] + metric[comp] * push)
    pieces.append((energy + pressure) * volume_contra)
    return pieces


def core_index():
    return lax.rem(lax.axis_index("azim"), 2)


def chip_index():
    return lax.div(lax.axis_index("azim"), 2)


def ring_weights(chips, turn, wide):
    levels = chips.bit_length() - 1
    size = 2 * (levels + 1)
    sends = np.zeros((levels, 2, chips, size))
    sums = np.zeros((2, chips, size))
    unit = np.eye(size)
    for chip in range(chips):
        spot = (chip + turn) % chips
        head, tail = unit[0], unit[1]
        left = right = np.zeros(size)
        for level in range(levels):
            group = 1 << level
            inside = spot % group
            sends[level, :, chip] = head, tail
            head_in, tail_in = unit[2 * level + 2], unit[2 * level + 3]
            if (spot >> level) & 1:
                left = left + wide**inside * head_in
                head, tail = head + wide**group * head_in, tail_in + wide**group * tail
            else:
                right = right + wide ** (group - 1 - inside) * tail_in
                head, tail = head_in + wide**group * head, tail + wide**group * tail_in
        close = 1.0 / (1.0 - wide**chips)
        sums[0, chip] = left + close * wide**spot * head
        sums[1, chip] = right + close * wide ** (chips - 1 - spot) * tail
    return sends, sums


def chosen(index, values):
    if not np.any(values):
        return None
    out = jnp.float32(values[0])
    for at in range(1, len(values)):
        if values[at] != values[at - 1] or np.any(values != values[0]):
            out = jnp.where(index == at, jnp.float32(values[at]), out)
    return out


def slot(value, field, height):
    start = (value * FIELDS + field) * height
    return slice(start, start + height)


def mixed(chip, table, sources, field, height):
    total = None
    for at, source in enumerate(sources):
        for part in range(2):
            weight = chosen(chip, table[:, 2 * at + part])
            if weight is not None:
                term = weight * source[slot(part, field, height)]
                total = term if total is None else total + term
    return total


def moments(tiles, root):
    head = tail = tiles[0]
    for row in range(1, len(tiles)):
        head = tiles[row] + root * head
        tail = tail + (root**row) * tiles[row]
    return head, tail


def fetched(sources, buffers, sem, pieces):
    copies = [
        [
            pltpu.make_async_copy(source.at[where], buffer.at[there], sem.at[at, n])
            for n, (source, buffer, (where, there)) in enumerate(zip(sources, buffers, piece))
        ]
        for at, piece in enumerate(pieces)
    ]
    for group in copies:
        for copy in group:
            copy.start()
    return copies


def azim_flux_kernel(mine, density, velocity, pressure, azim_metric, volume, out, pack, *scratch):
    *buffers, flux, sem = scratch
    chunks, _, rows, planes, _ = out.shape
    core = core_index()
    start = (core if mine else 1 - core) * chunks * planes
    pieces = []
    for chunk in range(chunks):
        here, there = pl.ds(start + chunk * planes, planes), pl.ds(chunk * planes, planes)
        whole = slice(None)
        pieces.append(
            [(here, there), ((whole, here), (whole, there)), (here, there)]
            + [((whole, here), (whole, there)), (here, there)]
        )
    groups = fetched((density, velocity, pressure, azim_metric, volume), buffers, sem, pieces)
    first = core == 0
    for chunk in range(chunks):
        for copy in groups[chunk]:
            copy.wait()
        rho_in, vel_in, pres_in, metric_in, vol_in = buffers
        for plane in range(planes):
            at = chunk * planes + plane
            rho, pres = rho_in[at], pres_in[at]
            vel = [vel_in[c, at] for c in range(3)]
            energy = tile_energy(rho, vel, pres)
            metric = [metric_in[c, at] for c in range(3)]
            for f, piece in enumerate(tile_flux(rho, vel, pres, energy, metric, vol_in[at])):
                flux[f, plane] = piece
        for f in range(FIELDS):
            turned = jnp.swapaxes(flux[f], 0, 1)
            out[chunk, f] = turned
            tiles = [turned[row] for row in range(rows)]
            pack[chunk, 0, f], pack[chunk, 1, f] = moments(tiles, DERIV_ROOT)
            pack[chunk, 2, f] = jnp.where(first, tiles[0], tiles[rows - 1])


def put_moments(step, field, head, tail, low, high, pack, edge):
    on_left = lax.rem(chip_index() + step, 2) == 0
    height = head.shape[0]
    pack[slot(0, field, height)] = head
    pack[slot(1, field, height)] = tail
    for n in range(len(low)):
        pack[slot(2 + n, field, height)] = jnp.where(on_left, high[n], low[n])
        edge[slot(n, field, height)] = jnp.where(on_left, low[n], high[n])


def chip_moments_kernel(rows, keep, other, pack_a, pack_b, edge_a, edge_b):
    first = core_index() == 0
    decay, one = jnp.float32(DERIV_ROOT**rows), jnp.float32(1.0)
    near, away = jnp.where(first, decay, one), jnp.where(first, one, decay)
    height = keep.shape[3]
    for turn, (pack, edge) in enumerate(((pack_a, edge_a), (pack_b, edge_b))):
        on_left = lax.rem(chip_index() + turn, 2) == 0
        mine = first != on_left
        for f in range(FIELDS):
            head, tail, row = (keep[turn, n, f] for n in range(3))
            head_in, tail_in, row_in = (other[turn, n, f] for n in range(3))
            pack[slot(0, f, height)] = near * head + away * head_in
            pack[slot(1, f, height)] = away * tail + near * tail_in
            pack[slot(2, f, height)] = jnp.where(mine, row, row_in)
            edge[slot(0, f, height)] = jnp.where(mine, row_in, row)


def totals_kernel(table, joined, near, height, *refs):
    chip = chip_index()
    *refs, send_a, send_b = refs
    count = len(refs) // 2
    for turn, send in enumerate((send_a, send_b)):
        mine = refs[turn * count : (turn + 1) * count]
        sources = mine[:-1] if joined else mine
        for f in range(FIELDS):
            send[slot(0, f, height)] = mixed(chip, table[turn][0], sources, f, height)
            send[slot(1, f, height)] = mixed(chip, table[turn][1], sources, f, height)
        if joined:
            send[2 * FIELDS * height :] = mine[-1][...]


def ring_kernel(table, near, height, *refs):
    chip = chip_index()
    *refs, out = refs
    count = len(refs) // 2
    for turn in range(2):
        *sources, edge = refs[turn * count : (turn + 1) * count]
        on_left = lax.rem(chip + turn, 2) == 0
        start = 0 if edge.shape[0] == near * FIELDS * height else 2
        for f in range(FIELDS):
            out[turn, 0, f] = mixed(chip, table[turn][0], sources, f, height)
            out[turn, 1, f] = mixed(chip, table[turn][1], sources, f, height)
            for n in range(near):
                paired = sources[1][slot(2 + n, f, height)]
                other = edge[slot(start + n, f, height)]
                out[turn, 2 + n, f] = jnp.where(on_left, other, paired)
                out[turn, 2 + near + n, f] = jnp.where(on_left, paired, other)


def section_local_kernel(
    density,
    velocity,
    pressure,
    axial_metric,
    volume,
    radial,
    own,
    basis,
    base_out,
    scale_out,
    edge_out,
    axial_flux,
    start,
):
    planes, rows, lanes = density.shape
    for plane in range(planes):
        rho = density[plane]
        vel = [velocity[c, plane] for c in range(3)]
        pres = pressure[plane]
        vol = volume[plane]
        energy = tile_energy(rho, vel, pres)
        axial = tile_flux(rho, vel, pres, energy, [axial_metric[c, plane] for c in range(3)], vol)
        state = [rho, rho * vel[0], rho * vel[1], rho * vel[2], energy]
        for f in range(FIELDS):
            axial_flux[f, plane] = axial[f]
            start[f, plane] = state[f] + SECTION * radial[f, plane]
    scale = jnp.swapaxes(SECTION / volume[...], 0, 1)
    scale_out[0] = scale
    for f in range(FIELDS):
        flux = jnp.swapaxes(axial_flux[f], 0, 1).reshape(rows * planes, lanes)
        edge_out[:, f * rows * planes : (f + 1) * rows * planes] = outgoing(basis, flux)
        deriv = own_block(flux, own).reshape(rows, planes, lanes)
        base_out[0, f] = jnp.swapaxes(start[f], 0, 1) - scale * deriv


def section_axial_kernel(base, scale, far, *rest):
    *edges, out_kept, out_sent = rest
    fields, rows, planes, lanes = base.shape[1:]
    core = core_index()
    weights = far.at[lax.axis_index("axial")]
    for mine, out in ((core, out_kept), (1 - core, out_sent)):
        for chunk in range(2):
            at = 2 * mine + chunk
            for f in range(fields):
                spot = pl.multiple_of((at * fields + f) * rows * planes, 128)
                parts = [ref[:, pl.ds(spot, rows * planes)] for ref in edges]
                axial = incoming(parts, weights).reshape(rows, planes, lanes)
                out[chunk, f] = base[at, f] - scale[at] * axial
            out[chunk, fields] = scale[at]


def section_join_kernel(step, flux_keep, flux_in, base_keep, base_in, ring, basis, out, edge):
    rows, planes, lanes = flux_keep.shape[2:]
    first = core_index() == 0
    last = 2 * rows - 1
    width = 2 * rows * planes

    for f in range(FIELDS):
        azim = [both_row(first, flux_keep, flux_in, f, row) for row in range(last + 1)]
        left, right, before, after = (ring[0, n, f] for n in range(4))
        down = [None] * (last + 1)
        down[last] = azim[last] + DERIV_ROOT * right
        for row in range(last - 1, -1, -1):
            down[row] = azim[row] + DERIV_ROOT * down[row + 1]
        up = left
        for row in range(last + 1):
            up = azim[row] + DERIV_ROOT * up
            total = DERIV_FAR * (up - down[row])
            total = total - DERIV_NEAR * (azim[row - 1] if row > 0 else before)
            total = total + DERIV_NEAR * (azim[row + 1] if row < last else after)
            base = both_row(first, base_keep, base_in, f, row)
            scale = both_row(first, base_keep, base_in, FIELDS, row)
            out[0, f, row] = base - scale * total
        spot = (step * FIELDS + f) * width
        edge[:, spot : spot + width] = outgoing(basis, out[0, f].reshape(width, lanes))


def both_row(first, mine, theirs, field, row):
    rows = mine.shape[2]
    if row < rows:
        return jnp.where(first, mine[0, field, row], theirs[0, field, row])
    return jnp.where(first, theirs[0, field, row - rows], mine[0, field, row - rows])


def axial_local_kernel(step, values, own, out):
    weights = own.at[lax.axis_index("axial")]
    for f in range(FIELDS):
        lines = values[0, f].reshape(-1, values.shape[-1])
        out[0, f] = (lines + own_block(lines, weights)).reshape(out.shape[2:])


def axial_join_kernel(step, local, far, *rest):
    edges, (out, pack_a, pack_b, edge_a, edge_b, front) = rest[:-6], rest[-6:]
    pack, away = ((pack_a, edge_a), (pack_b, edge_b))[step]
    weights = far.at[lax.axis_index("axial")]
    rows, planes, lanes = local.shape[2:]
    width = rows * planes
    for f in range(FIELDS):
        spot = (step * FIELDS + f) * width
        axial = incoming([ref[:, spot : spot + width] for ref in edges], weights)
        axial = axial.reshape(rows, planes, lanes)
        tiles = [local[0, f, row] + axial[row] for row in range(rows)]
        for row in range(rows):
            out[0, f, row] = tiles[row]
        head, tail = moments(tiles, FILTER_ROOT)
        put_moments(step, f, head, tail, tiles[:2], tiles[rows - 2 :], pack, away)
    if step == 0:
        for row in range(rows):
            front[row : row + 1, :] = out[0, 2, row, 0:1, :] + out[0, 0, row, 0:1, :]
        for other in (pack_a, pack_b):
            other[other.shape[0] - rows :] = front[...]


def azim_local_kernel(step, values, out):
    rows = values.shape[2]
    for f in range(FIELDS):
        down = [None] * rows
        down[rows - 1] = values[0, f, rows - 1]
        for row in range(rows - 2, -1, -1):
            down[row] = values[0, f, row] + FILTER_ROOT * down[row + 1]
        up = None
        for row in range(rows):
            here = values[0, f, row]
            up = here if row == 0 else here + FILTER_ROOT * up
            total = (1.0 + FILTER_MID - FILTER_FAR) * here + FILTER_FAR * (up + down[row])
            for step, weight in ((1, FILTER_ONE), (2, FILTER_TWO)):
                if row >= step:
                    total = total + weight * values[0, f, row - step]
                if row + step < rows:
                    total = total + weight * values[0, f, row + step]
            out[0, f, row] = total


def joined_rows(upper, local, ring, field):
    rows = local.shape[2]
    one, zero = jnp.float32(1.0), jnp.float32(0.0)
    decay = jnp.float32(FILTER_ROOT**rows)
    left = jnp.where(upper, decay, one) * ring[0, 0, field]
    right = jnp.where(upper, one, decay) * ring[0, 1, field]
    low, high = jnp.where(upper, zero, one), jnp.where(upper, one, zero)
    before = [low * ring[0, 2 + n, field] for n in range(2)]
    after = [high * ring[0, 4 + n, field] for n in range(2)]
    tiles = []
    for row in range(rows):
        total = (
            local[0, field, row]
            + (FILTER_FAR * FILTER_ROOT ** (row + 1)) * left
            + (FILTER_FAR * FILTER_ROOT ** (rows - row)) * right
        )
        if row < 2:
            total = total + FILTER_TWO * before[row]
        if row == 0:
            total = total + FILTER_ONE * before[1]
        if row >= rows - 2:
            total = total + FILTER_TWO * after[row - (rows - 2)]
        if row == rows - 1:
            total = total + FILTER_ONE * after[0]
        tiles.append(total)
    return tiles


def azim_send_kernel(step, local, ring, out):
    rows = local.shape[2] // 2
    upper = 1 - core_index()
    there = local.at[:, :, pl.ds(upper * rows, rows)]
    for f in range(FIELDS):
        for row, tile in enumerate(joined_rows(upper == 1, there, ring, f)):
            out[0, f, row] = tile


def azim_keep_kernel(local, ring, out):
    for f in range(FIELDS):
        tiles = joined_rows(core_index() == 1, local, ring, f)
        out[f] = jnp.swapaxes(jnp.stack(tiles), 0, 1)


def place_rows_kernel(values, partial, out):
    for f in range(FIELDS):
        out[f] = jnp.swapaxes(values[0, f], 0, 1)


def entries_kernel(weight_table, weights, area, observers, bins, value, chosen_rows, chosen_bins):
    entries, rows, lanes = weights.shape
    observer_rows = lax.broadcasted_iota(jnp.int32, (chosen_rows.shape[0], lanes), 0)
    bin_rows = lax.broadcasted_iota(jnp.int32, (chosen_bins.shape[0], lanes), 0)
    for entry in range(entries):
        picked = weights[entry]
        found = jnp.zeros(picked.shape, jnp.float32)
        for part in range(weight_table.shape[0]):
            there = picked - part * lanes
            inside = (there >= 0) & (there < lanes)
            columns = jnp.broadcast_to(weight_table[part : part + 1, :], picked.shape)
            part_found = jnp.take_along_axis(columns, jnp.where(inside, there, 0), axis=1)
            found = jnp.where(inside, part_found, found)
        value[entry] = found * area[...]
        for row in range(rows):
            at = (row * entries + entry) * lanes
            hit = observer_rows == observers[entry, row : row + 1, :]
            chosen_rows[:, at : at + lanes] = jnp.where(hit, 1.0, 0.0).astype(jnp.bfloat16)
            hit = bin_rows == bins[entry, row : row + 1, :]
            chosen_bins[:, at : at + lanes] = jnp.where(hit, 1.0, 0.0).astype(jnp.bfloat16)


def surface_kernel(masks, around, front, *rest):
    *arrived, kept, sent, ring = rest
    rows = front.shape[0]
    chip = chip_index()
    for mask, ref in zip((0, *masks), (front, *arrived)):
        spot = pl.multiple_of(jnp.bitwise_xor(chip, mask) * rows, 8)
        ring[pl.ds(spot, rows), :] = ref[ref.shape[0] - rows :]
    surface = -1.0 + jnp.dot(
        around[chip],
        ring[...],
        precision=lax.Precision.HIGHEST,
        preferred_element_type=jnp.float32,
    )
    kept[...] = surface[: rows // 2]
    sent[...] = surface[rows // 2 :]


def signals_kernel(surface, surface_in, value, chosen_rows, chosen_bins, out, placed):
    entries, rows, lanes = value.shape
    height = out.shape[1]
    cells = jnp.where(core_index() == 0, surface[...], surface_in[...])
    for entry in range(entries):
        high, low = split(value[entry] * cells)
        for row in range(rows):
            at = (row * entries + entry) * lanes
            hit = chosen_bins[:, at : at + lanes]
            placed[:height, at : at + lanes] = hit * high[row : row + 1, :]
            placed[height:, at : at + lanes] = hit * low[row : row + 1, :]
    total = lax.dot_general(
        chosen_rows[...],
        placed[...],
        (((1,), (1,)), ((), ())),
        preferred_element_type=jnp.float32,
    )
    out[...] = total[:, :height] + total[:, height:]


def params(limit=VMEM_LIMIT):
    return pltpu.CompilerParams(vmem_limit_bytes=limit)


def cost(flops, moved):
    return pl.CostEstimate(flops=1, bytes_accessed=1, transcendentals=0)


def swap(values, axis, count, mask):
    return lax.ppermute(values, axis, [(i, i ^ mask) for i in range(count)])


def sibling(values, count):
    return lax.ppermute(values, "azim", [(i, i ^ 1) for i in range(count)])


def partner(values, count, turn, level):
    chips = count // 2
    pairs = []
    for i in range(count):
        chip, core = divmod(i, 2)
        there = ((((chip + turn) % chips) ^ ((2 << level) - 1)) - turn) % chips
        pairs.append((i, 2 * there + core))
    return lax.ppermute(values, "azim", pairs)


def waiting(kernel, count, wait):
    if not wait:
        return kernel
    return lambda *refs: kernel(*refs[:count], *refs[count + len(wait) :])


def by_chunk(kernel, blocked):
    def run(*refs):
        for step in range(2):
            pieces = [
                ref.at[step : step + 1] if cut else ref for ref, cut in zip(refs, blocked, strict=True)
            ]
            kernel(step, *pieces)

    return run


def whole_call(kernel, name, shapes, args, wait=(), scratch=()):
    whole = pl.BlockSpec(memory_space=pltpu.VMEM)
    return pl.pallas_call(
        waiting(kernel, len(args), wait),
        in_specs=[whole] * len(args) + [pl.BlockSpec(memory_space=pl.ANY)] * len(wait),
        out_specs=[whole] * len(shapes),
        out_shape=shapes,
        scratch_shapes=scratch,
        compiler_params=params(),
        cost_estimate=cost(1, 1),
        name=name,
    )(*args, *wait)


def ring_exchange(packs, arrived, edges, count, near, height, wide, wait=()):
    chips = count // 2
    levels = chips.bit_length() - 1
    tables = [ring_weights(chips, turn, wide) for turn in range(2)]
    lanes = packs[0].shape[1]
    rows = FIELDS * height
    joined = levels == 2
    sources = [[packs[turn], arrived[turn]] for turn in range(2)]
    if not joined:
        edges = [partner(edges[turn], count, 1 - turn, 0) for turn in range(2)]
    for level in range(1, levels):
        size = (2 + near if joined else 2) * rows
        args = [a for turn in range(2) for a in sources[turn] + ([edges[turn]] if joined else [])]
        sends = whole_call(
            functools.partial(totals_kernel, [t[0][level] for t in tables], joined, near, height),
            "group_totals",
            [jax.ShapeDtypeStruct((size, lanes), jnp.float32)] * 2,
            args,
            wait,
        )
        for turn in range(2):
            sources[turn].append(partner(sends[turn], count, turn, level))
    args = [
        a for turn in range(2) for a in sources[turn] + [sources[turn][-1] if joined else edges[turn]]
    ]

    def sums(wait=()):
        return whole_call(
            functools.partial(ring_kernel, [t[1] for t in tables], near, height),
            "ring_sums",
            [jax.ShapeDtypeStruct((2, 2 + 2 * near, FIELDS, height, lanes), jnp.float32)],
            args,
            wait,
        )[0]

    return sums, sends[0], [source[-1] for source in sources]


def per_device(
    density,
    velocity,
    pressure,
    axial_metric,
    azim_metric,
    volume,
    radial_term,
    panel_area,
    observer_ids,
    bin_ids,
    weight_ids,
    bin_weights,
):
    planes, rows, lanes = density.shape
    along = lax.axis_size("axial")
    around = lax.axis_size("azim")
    devices = along * around
    part = planes // 4
    lines = FIELDS * rows * part
    f32 = jnp.float32

    own_d, basis_d, far_d = map(halves, axial_tables(along, lanes, DERIV_ALPHA, "deriv"))
    own_f, basis_f, far_f = map(halves, axial_tables(along, lanes, FILTER_ALPHA, "filter"))
    filter_around = surface_table(around, rows)

    spec = pl.BlockSpec

    def every(k):
        return k

    def kept(k):
        return core_index() * 2 + k

    def sent(k):
        return (1 - core_index()) * 2 + k

    def field(where):
        return spec((part, rows, lanes), lambda k: (where(k), 0, 0))

    def vector(where, size=3):
        return spec((size, part, rows, lanes), lambda k: (0, where(k), 0, 0))

    def inner(where, size=FIELDS, tall=rows):
        return spec((1, size, tall, part, lanes), lambda k: (where(k), 0, 0, 0, 0))

    def inner_one(where, tall=rows):
        return spec((1, tall, part, lanes), lambda k: (where(k), 0, 0, 0))

    def edge(where, width=lines):
        return spec((BASIS, width), lambda k: (0, where(k)))

    def row_half(upper):
        return spec((1, FIELDS, rows, part, lanes), lambda k: (k, 0, upper(), 0, 0))

    def table(array):
        return spec((None,) + array.shape[1:], lambda k: (lax.axis_index("axial"),) + (0,) * (array.ndim - 1))

    def fixed(shape):
        return spec(shape, lambda k: (0,) * len(shape))

    def ring_spec(near):
        return spec((1, 2 + 2 * near, FIELDS, part, lanes), lambda k: (k, 0, 0, 0, 0))

    def shaped(*shape):
        return jax.ShapeDtypeStruct(shape, f32)

    def call(
        kernel, name, steps, ins, outs, shapes, args, wait=(), limit=VMEM_LIMIT, scratch=(), **more
    ):
        return pl.pallas_call(
            waiting(kernel, len(args), wait),
            grid=(steps,),
            in_specs=ins + [spec(memory_space=pl.ANY)] * len(wait),
            out_specs=outs,
            scratch_shapes=scratch,
            out_shape=shapes,
            compiler_params=params(limit),
            cost_estimate=cost(1, 1),
            name=name,
            **more,
        )(*args, *wait)

    tall = 2 * rows
    flux_scratch = pltpu.VMEM((FIELDS, part, rows, lanes), f32)
    half_shape = shaped(2, FIELDS, rows, part, lanes)
    chip_shape = shaped(2, FIELDS, tall, part, lanes)

    def apart(kernel, name, shapes, args, scratch, wait=(), limit=INPUT_LIMIT):
        several = isinstance(shapes, list)
        vmem = spec(memory_space=pltpu.VMEM)
        return pl.pallas_call(
            waiting(kernel, len(args), wait),
            in_specs=[spec(memory_space=pltpu.HBM)] * len(args)
            + [spec(memory_space=pl.ANY)] * len(wait),
            out_specs=[vmem] * len(shapes) if several else vmem,
            out_shape=shapes,
            scratch_shapes=scratch,
            compiler_params=params(limit),
            cost_estimate=cost(1, 1),
            name=name,
        )(*args, *wait)

    def azim_flux(mine, name, limit):
        one, three = (2 * part, rows, lanes), (3, 2 * part, rows, lanes)
        return apart(
            functools.partial(azim_flux_kernel, mine),
            name,
            [half_shape, shaped(2, 3, FIELDS, part, lanes)],
            (density, velocity, pressure, azim_metric, volume),
            [pltpu.VMEM(shape, f32) for shape in (one, three, one, three, one)]
            + [flux_scratch, pltpu.SemaphoreType.DMA((2, 5))],
            limit=limit,
        )

    flux_sent, pack_sent = azim_flux(False, "azim_flux_sent", INPUT_LIMIT)
    pack_in = sibling(pack_sent, around)
    flux_in = sibling(flux_sent, around)
    flux_kept, pack_kept = azim_flux(True, "azim_flux_kept", VMEM_LIMIT)
    *packs, edge_a, edge_b = whole_call(
        functools.partial(chip_moments_kernel, rows),
        "chip_moments",
        [shaped(3 * FIELDS * part, lanes)] * 2 + [shaped(FIELDS * part, lanes)] * 2,
        (pack_kept, pack_in),
    )

    arrived = [partner(packs[turn], around, turn, 0) for turn in range(2)]
    base, scale, edge_d = call(
        section_local_kernel,
        "section_local",
        4,
        [
            field(every),
            vector(every),
            field(every),
            vector(every),
            field(every),
            vector(every, FIELDS),
            table(own_d),
            fixed(basis_d.shape),
        ],
        [inner(every), inner_one(every), edge(every)],
        [
            shaped(4, FIELDS, rows, part, lanes),
            shaped(4, rows, part, lanes),
            shaped(BASIS, 4 * lines),
        ],
        (density, velocity, pressure, axial_metric, volume, radial_term, own_d, basis_d),
        wait=(packs[0], flux_in),
        scratch=[flux_scratch] * 2,
    )
    edges_d = [swap(edge_d, "axial", along, mask) for mask in range(1, along)]
    sums_d, sends_d, last_d = ring_exchange(
        packs, arrived, [edge_a, edge_b], around, 1, part, DERIV_ROOT ** (2 * rows), wait=(edge_d,)
    )

    base_kept, base_sent = whole_call(
        section_axial_kernel,
        "section_axial",
        [shaped(2, FIELDS + 1, rows, part, lanes)] * 2,
        (base, scale, jnp.asarray(far_d), *edges_d),
        wait=last_d,
    )
    base_in = sibling(base_sent, around)

    ring_d = sums_d()
    sectioned, edge_f = whole_call(
        by_chunk(section_join_kernel, [True] * 5 + [False, True, False]),
        "section_join",
        [chip_shape, shaped(BASIS, 4 * lines)],
        (flux_kept, flux_in, base_kept, base_in, ring_d, jnp.asarray(basis_f)),
    )
    edges_f = [swap(edge_f, "axial", along, mask) for mask in range(1, along)]
    (axial_local,) = whole_call(
        by_chunk(axial_local_kernel, [True, False, True]),
        "axial_local",
        [chip_shape],
        (sectioned, jnp.asarray(own_f)),
    )
    value, chosen_rows, chosen_bins = whole_call(
        entries_kernel,
        "entries",
        [
            shaped(*weight_ids.shape),
            jax.ShapeDtypeStruct((OBSERVERS, weight_ids.size), jnp.bfloat16),
            jax.ShapeDtypeStruct((TIME_BINS, weight_ids.size), jnp.bfloat16),
        ],
        (bin_weights.reshape(-1, lanes), weight_ids, panel_area, observer_ids, bin_ids),
        wait=(edge_f,),
    )
    chips = around // 2
    height = FIELDS * part
    shapes = [4 * height + tall] * 2 + [2 * height] * 2 + [tall]
    smoothed, *packs, edge_a, edge_b, front = whole_call(
        by_chunk(axial_join_kernel, [True] + [False] * along + [True] + [False] * 5),
        "axial_join",
        [chip_shape] + [shaped(size, lanes) for size in shapes],
        (axial_local, jnp.asarray(far_f), *edges_f),
        wait=(value,),
    )
    arrived = [partner(packs[turn], around, turn, 0) for turn in range(2)]

    masks = list(range(1, chips))
    fronts = [arrived[0], None, arrived[1]] if chips == 4 else [None] * (chips - 1)
    for at, mask in enumerate(masks):
        if fronts[at] is None:
            pairs = [(i, 2 * ((i // 2) ^ mask) + i % 2) for i in range(around)]
            fronts[at] = lax.ppermute(front, "azim", pairs)
    surface, surface_sent = whole_call(
        functools.partial(surface_kernel, masks),
        "surface",
        [shaped(rows, lanes)] * 2,
        (jnp.asarray(filter_around), front, *fronts),
        scratch=[pltpu.VMEM((around * rows, lanes), f32)],
    )
    surface_in = lax.ppermute(surface_sent, "azim", [(i, i + 1) for i in range(0, around, 2)])
    sums_f, sends_f, _ = ring_exchange(
        packs,
        arrived,
        [edge_a, edge_b],
        around,
        2,
        part,
        FILTER_ROOT ** (2 * rows),
        wait=(fronts[1],),
    )
    (partial,) = whole_call(
        signals_kernel,
        "signals",
        [shaped(OBSERVERS, TIME_BINS)],
        (surface, surface_in, value, chosen_rows, chosen_bins),
        wait=(sends_f,),
        scratch=[pltpu.VMEM((2 * TIME_BINS, weight_ids.size), jnp.bfloat16)],
    )
    shares = lax.all_to_all(
        partial.reshape(devices, OBSERVERS // devices, TIME_BINS),
        ("axial", "azim"),
        0,
        0,
        tiled=True,
    )
    (azim_local,) = whole_call(
        by_chunk(azim_local_kernel, [True, True]),
        "azim_local",
        [chip_shape],
        (smoothed,),
        wait=(sends_f,),
    )
    ring_f = sums_f((partial,))
    state_shape = shaped(FIELDS, planes, rows, lanes)
    (rows_sent,) = whole_call(
        by_chunk(azim_send_kernel, [True] * 3),
        "azim_join_sent",
        [half_shape],
        (azim_local, ring_f),
    )
    rows_in = sibling(rows_sent, around)
    mine = call(
        azim_keep_kernel,
        "azim_join_kept",
        2,
        [row_half(core_index), ring_spec(2)],
        vector(kept, FIELDS),
        state_shape,
        (azim_local, ring_f),
    )
    new_state = call(
        place_rows_kernel,
        "place_rows",
        2,
        [inner(every), spec(memory_space=pl.ANY)],
        vector(sent, FIELDS),
        state_shape,
        (rows_in, mine),
        input_output_aliases={1: 0},
    )
    shares, new_state = lax.optimization_barrier((shares, new_state))
    return new_state, jnp.sum(shares, axis=0)


def solution(mesh):
    placed = (
        P(None, "azim", "axial"),
        P(None, None, "azim", "axial"),
        P(None, "azim", "axial"),
        P(None, None, "azim", "axial"),
        P(None, None, "azim", "axial"),
        P(None, "azim", "axial"),
        P(None, None, "azim", "axial"),
        P("azim", "axial"),
        P(None, "azim", "axial"),
        P(None, "azim", "axial"),
        P(None, "azim", "axial"),
        P(),
    )
    return jax.shard_map(
        per_device,
        mesh=mesh,
        in_specs=placed,
        out_specs=(P(None, None, "azim", "axial"), P(("axial", "azim"), None)),
        check_vma=False,
    )
```

```python
import functools
import math

import jax
import jax.numpy as jnp
import numpy as np
from jax import lax
from jax.experimental import pallas as pl
from jax.experimental.pallas import tpu as pltpu
from jax.sharding import PartitionSpec as P

OBSERVERS = 512
TIME_BINS = 128

GAMMA = 1.4
SECTION = 0.25
DERIV_ALPHA = 1.0 / 3.0
FILTER_ALPHA = 0.499
FIELDS = 5
BASIS = 8
VMEM_LIMIT = 16 * 1024 * 1024
INPUT_LIMIT = 60 * 1024 * 1024


def decay_root(alpha):
    return (-1.0 + math.sqrt(1.0 - 4.0 * alpha * alpha)) / (2.0 * alpha)


DERIV_ROOT = decay_root(DERIV_ALPHA)
FILTER_ROOT = decay_root(FILTER_ALPHA)

DERIV_NEAR = 1.0 / 12.0
DERIV_FAR = (
    (25.0 / 36.0) * (DERIV_ROOT - 1.0 / DERIV_ROOT) / (1.0 + 2.0 * DERIV_ALPHA * DERIV_ROOT)
)

_B = FILTER_ALPHA
_EDGE = (1.0 - 2.0 * _B) / 64.0
_Q2 = 1.0 / _B
_Q1 = (-6.0 - _Q2) / _B
_Q0 = (12.0 - _Q1) / _B
_RHO = -8.0 - _Q0
FILTER_MID = _EDGE * (_Q0 + 2.0 * _Q2)
FILTER_ONE = _EDGE * _Q1
FILTER_TWO = _EDGE * _Q2
FILTER_FAR = _EDGE * _RHO / (1.0 + 2.0 * _B * FILTER_ROOT)


def open_operator(length, alpha, side):
    base = decay_root(alpha)
    tri = np.eye(length) + alpha * (np.eye(length, k=1) + np.eye(length, k=-1))
    tri[0, 0] = -alpha / base
    return np.linalg.solve(tri, side)


def deriv_matrix(length):
    return (7.0 / 9.0) * (np.eye(length, k=1) - np.eye(length, k=-1)) + (1.0 / 36.0) * (
        np.eye(length, k=2) - np.eye(length, k=-2)
    )


def filter_matrix(length):
    beta = FILTER_ALPHA
    coeffs = [
        (11.0 + 10.0 * beta) / 16.0,
        (15.0 + 34.0 * beta) / 32.0,
        (-3.0 + 6.0 * beta) / 16.0,
        (1.0 - 2.0 * beta) / 32.0,
    ]
    total = coeffs[0] * np.eye(length)
    for shift in range(1, 4):
        total = total + 0.5 * coeffs[shift] * (np.eye(length, k=shift) + np.eye(length, k=-shift))
    return total


def axial_tables(count, width, alpha, kind):
    length = count * width
    side = deriv_matrix(length) if kind == "deriv" else filter_matrix(length)
    whole = open_operator(length, alpha, side)
    base = decay_root(alpha)
    basis = np.zeros((BASIS, width))
    for edge in range(3):
        basis[edge, edge] = 1.0
        basis[3 + edge, width - 3 + edge] = 1.0
    basis[6] = base ** np.arange(width - 1, -1, -1, dtype=np.float64)
    basis[7] = base ** np.arange(width, dtype=np.float64)
    inverse = np.linalg.pinv(basis)
    own = np.zeros((count, width, width))
    far = np.zeros((count, max(count - 1, 1) * BASIS, width))
    for here in range(count):
        rows = whole[here * width : (here + 1) * width]
        own[here] = rows[:, here * width : (here + 1) * width].T
        if kind == "filter":
            own[here] -= np.eye(width)
        for shift in range(1, count):
            there = here ^ shift
            block = rows[:, there * width : (there + 1) * width]
            far[here, (shift - 1) * BASIS : shift * BASIS] = (block @ inverse).T
    return own, basis, far


def surface_table(around, rows):
    length = around * rows
    turn = np.roll(np.eye(length), 1, axis=1)
    beta = FILTER_ALPHA
    side = (11.0 + 10.0 * beta) / 16.0 * np.eye(length)
    coeffs = [(15.0 + 34.0 * beta) / 64.0, (-3.0 + 6.0 * beta) / 32.0, (1.0 - 2.0 * beta) / 64.0]
    for shift, weight in enumerate(coeffs, start=1):
        step = np.linalg.matrix_power(turn, shift)
        side = side + weight * (step + step.T)
    cycle = np.linalg.solve(np.eye(length) + beta * (turn + turn.T), side)
    return cycle.reshape(around // 2, 2 * rows, length).astype(np.float32)


def halves(table):
    high = np.asarray(table, np.float32).astype(jnp.bfloat16)
    low = (np.asarray(table, np.float64) - high.astype(np.float64)).astype(jnp.bfloat16)
    return np.stack([high, low], axis=-3)


def split(values):
    high = values.astype(jnp.bfloat16)
    return high, (values - high.astype(jnp.float32)).astype(jnp.bfloat16)


def dots(left, right, dims):
    out = None
    for a, b in ((0, 0), (1, 0), (0, 1)):
        part = lax.dot_general(
            left[a], right[b], (dims, ((), ())), preferred_element_type=jnp.float32
        )
        out = part if out is None else out + part
    return out


def outgoing(basis_ref, lines):
    return dots((basis_ref[0], basis_ref[1]), split(lines), ((1,), (1,)))


def incoming(parts, far_ref):
    return dots(split(jnp.concatenate(parts, axis=0)), (far_ref[0], far_ref[1]), ((0,), (0,)))


def own_block(lines, own_ref):
    return dots(split(lines), (own_ref[0], own_ref[1]), ((1,), (0,)))


def tile_energy(density, velocity, pressure):
    return pressure * (1.0 / (GAMMA - 1.0)) + 0.5 * density * (
        velocity[0] * velocity[0] + velocity[1] * velocity[1] + velocity[2] * velocity[2]
    )


def tile_flux(density, velocity, pressure, energy, metric, volume):
    contra = metric[0] * velocity[0] + metric[1] * velocity[1] + metric[2] * velocity[2]
    volume_contra = volume * contra
    mass = density * volume_contra
    push = volume * pressure
    pieces = [mass]
    for comp in range(3):
        pieces.append(mass * velocity[comp] + metric[comp] * push)
    pieces.append((energy + pressure) * volume_contra)
    return pieces


def core_index():
    return lax.rem(lax.axis_index("azim"), 2)


def chip_index():
    return lax.div(lax.axis_index("azim"), 2)


def ring_weights(chips, turn, wide):
    levels = chips.bit_length() - 1
    size = 2 * (levels + 1)
    sends = np.zeros((levels, 2, chips, size))
    sums = np.zeros((2, chips, size))
    unit = np.eye(size)
    for chip in range(chips):
        spot = (chip + turn) % chips
        head, tail = unit[0], unit[1]
        left = right = np.zeros(size)
        for level in range(levels):
            group = 1 << level
            inside = spot % group
            sends[level, :, chip] = head, tail
            head_in, tail_in = unit[2 * level + 2], unit[2 * level + 3]
            if (spot >> level) & 1:
                left = left + wide**inside * head_in
                head, tail = head + wide**group * head_in, tail_in + wide**group * tail
            else:
                right = right + wide ** (group - 1 - inside) * tail_in
                head, tail = head_in + wide**group * head, tail + wide**group * tail_in
        close = 1.0 / (1.0 - wide**chips)
        sums[0, chip] = left + close * wide**spot * head
        sums[1, chip] = right + close * wide ** (chips - 1 - spot) * tail
    return sends, sums


def chosen(index, values):
    if not np.any(values):
        return None
    out = jnp.float32(values[0])
    for at in range(1, len(values)):
        if values[at] != values[at - 1] or np.any(values != values[0]):
            out = jnp.where(index == at, jnp.float32(values[at]), out)
    return out


def slot(value, field, height):
    start = (value * FIELDS + field) * height
    return slice(start, start + height)


def mixed(chip, table, sources, field, height):
    total = None
    for at, source in enumerate(sources):
        for part in range(2):
            weight = chosen(chip, table[:, 2 * at + part])
            if weight is not None:
                term = weight * source[slot(part, field, height)]
                total = term if total is None else total + term
    return total


def moments(tiles, root):
    head = tail = tiles[0]
    for row in range(1, len(tiles)):
        head = tiles[row] + root * head
        tail = tail + (root**row) * tiles[row]
    return head, tail


def fetched(sources, buffers, sem, pieces):
    copies = [
        [
            pltpu.make_async_copy(source.at[where], buffer.at[there], sem.at[at, n])
            for n, (source, buffer, (where, there)) in enumerate(zip(sources, buffers, piece))
        ]
        for at, piece in enumerate(pieces)
    ]
    for group in copies:
        for copy in group:
            copy.start()
    return copies


def azim_flux_kernel(mine, density, velocity, pressure, azim_metric, volume, out, pack, *scratch):
    *buffers, flux, sem = scratch
    chunks, _, rows, planes, _ = out.shape
    core = core_index()
    start = (core if mine else 1 - core) * chunks * planes
    pieces = []
    for chunk in range(chunks):
        here, there = pl.ds(start + chunk * planes, planes), pl.ds(chunk * planes, planes)
        whole = slice(None)
        pieces.append(
            [(here, there), ((whole, here), (whole, there)), (here, there)]
            + [((whole, here), (whole, there)), (here, there)]
        )
    groups = fetched((density, velocity, pressure, azim_metric, volume), buffers, sem, pieces)
    first = core == 0
    for chunk in range(chunks):
        for copy in groups[chunk]:
            copy.wait()
        rho_in, vel_in, pres_in, metric_in, vol_in = buffers
        for plane in range(planes):
            at = chunk * planes + plane
            rho, pres = rho_in[at], pres_in[at]
            vel = [vel_in[c, at] for c in range(3)]
            energy = tile_energy(rho, vel, pres)
            metric = [metric_in[c, at] for c in range(3)]
            for f, piece in enumerate(tile_flux(rho, vel, pres, energy, metric, vol_in[at])):
                flux[f, plane] = piece
        for f in range(FIELDS):
            turned = jnp.swapaxes(flux[f], 0, 1)
            out[chunk, f] = turned
            tiles = [turned[row] for row in range(rows)]
            pack[chunk, 0, f], pack[chunk, 1, f] = moments(tiles, DERIV_ROOT)
            pack[chunk, 2, f] = jnp.where(first, tiles[0], tiles[rows - 1])


def put_moments(step, field, head, tail, low, high, pack, edge):
    on_left = lax.rem(chip_index() + step, 2) == 0
    height = head.shape[0]
    pack[slot(0, field, height)] = head
    pack[slot(1, field, height)] = tail
    for n in range(len(low)):
        pack[slot(2 + n, field, height)] = jnp.where(on_left, high[n], low[n])
        edge[slot(n, field, height)] = jnp.where(on_left, low[n], high[n])


def chip_moments_kernel(rows, keep, other, pack_a, pack_b, edge_a, edge_b):
    first = core_index() == 0
    decay, one = jnp.float32(DERIV_ROOT**rows), jnp.float32(1.0)
    near, away = jnp.where(first, decay, one), jnp.where(first, one, decay)
    height = keep.shape[3]
    for turn, (pack, edge) in enumerate(((pack_a, edge_a), (pack_b, edge_b))):
        on_left = lax.rem(chip_index() + turn, 2) == 0
        mine = first != on_left
        for f in range(FIELDS):
            head, tail, row = (keep[turn, n, f] for n in range(3))
            head_in, tail_in, row_in = (other[turn, n, f] for n in range(3))
            pack[slot(0, f, height)] = near * head + away * head_in
            pack[slot(1, f, height)] = away * tail + near * tail_in
            pack[slot(2, f, height)] = jnp.where(mine, row, row_in)
            edge[slot(0, f, height)] = jnp.where(mine, row_in, row)


def totals_kernel(table, joined, near, height, *refs):
    chip = chip_index()
    *refs, send_a, send_b = refs
    count = len(refs) // 2
    for turn, send in enumerate((send_a, send_b)):
        mine = refs[turn * count : (turn + 1) * count]
        sources = mine[:-1] if joined else mine
        for f in range(FIELDS):
            send[slot(0, f, height)] = mixed(chip, table[turn][0], sources, f, height)
            send[slot(1, f, height)] = mixed(chip, table[turn][1], sources, f, height)
        if joined:
            send[2 * FIELDS * height :] = mine[-1][...]


def ring_kernel(table, near, height, *refs):
    chip = chip_index()
    *refs, out = refs
    count = len(refs) // 2
    for turn in range(2):
        *sources, edge = refs[turn * count : (turn + 1) * count]
        on_left = lax.rem(chip + turn, 2) == 0
        start = 0 if edge.shape[0] == near * FIELDS * height else 2
        for f in range(FIELDS):
            out[turn, 0, f] = mixed(chip, table[turn][0], sources, f, height)
            out[turn, 1, f] = mixed(chip, table[turn][1], sources, f, height)
            for n in range(near):
                paired = sources[1][slot(2 + n, f, height)]
                other = edge[slot(start + n, f, height)]
                out[turn, 2 + n, f] = jnp.where(on_left, other, paired)
                out[turn, 2 + near + n, f] = jnp.where(on_left, paired, other)


def section_local_kernel(
    density,
    velocity,
    pressure,
    axial_metric,
    volume,
    radial,
    own,
    basis,
    base_out,
    scale_out,
    edge_out,
    axial_flux,
    start,
):
    planes, rows, lanes = density.shape
    for plane in range(planes):
        rho = density[plane]
        vel = [velocity[c, plane] for c in range(3)]
        pres = pressure[plane]
        vol = volume[plane]
        energy = tile_energy(rho, vel, pres)
        axial = tile_flux(rho, vel, pres, energy, [axial_metric[c, plane] for c in range(3)], vol)
        state = [rho, rho * vel[0], rho * vel[1], rho * vel[2], energy]
        for f in range(FIELDS):
            axial_flux[f, plane] = axial[f]
            start[f, plane] = state[f] + SECTION * radial[f, plane]
    scale = jnp.swapaxes(SECTION / volume[...], 0, 1)
    scale_out[0] = scale
    for f in range(FIELDS):
        flux = jnp.swapaxes(axial_flux[f], 0, 1).reshape(rows * planes, lanes)
        edge_out[:, f * rows * planes : (f + 1) * rows * planes] = outgoing(basis, flux)
        deriv = own_block(flux, own).reshape(rows, planes, lanes)
        base_out[0, f] = jnp.swapaxes(start[f], 0, 1) - scale * deriv


def section_split_kernel(base, scale, edge, kept, sent):
    fields, rows, planes, lanes = base.shape[1:]
    size = rows * planes
    core = core_index()
    for mine, out in ((core, kept), (1 - core, sent)):
        for chunk in range(2):
            at = 2 * mine + chunk
            for f in range(fields + 1):
                spot = (chunk * (fields + 1) + f) * size
                piece = base[at, f] if f < fields else scale[at]
                out[spot : spot + size] = piece.reshape(size, lanes)
            for f in range(fields):
                from_spot = pl.multiple_of((at * fields + f) * size, 128)
                spot = 2 * (fields + 1) * size + (chunk * fields + f) * BASIS
                out[spot : spot + BASIS] = edge[:, pl.ds(from_spot, size)]


def edge_both_kernel(kept, arrived, edge):
    lanes = kept.shape[1]
    start = kept.shape[0] - 2 * FIELDS * BASIS
    first = core_index() == 0
    for at in range(2 * FIELDS):
        piece = slice(start + at * BASIS, start + (at + 1) * BASIS)
        mine, theirs = kept[piece], arrived[piece]
        spot = 2 * at * lanes
        edge[:, spot : spot + lanes] = jnp.where(first, mine, theirs)
        edge[:, spot + lanes : spot + 2 * lanes] = jnp.where(first, theirs, mine)


def both_row(first, mine, theirs, row):
    rows = mine.shape[0]
    if row < rows:
        return jnp.where(first, mine[row], theirs[row])
    return jnp.where(first, theirs[row - rows], mine[row - rows])


def section_join_kernel(
    step, flux_keep, flux_in, base_keep, base_in, ring, basis, far, *rest
):
    *edges, out, edge = rest
    rows, planes, lanes = flux_keep.shape[2:]
    first = core_index() == 0
    last = 2 * rows - 1
    width = 2 * rows * planes
    size = rows * planes
    weights = far.at[lax.axis_index("axial")]

    def base_rows(f):
        spot = (step * (FIELDS + 1) + f) * size
        halves = [ref[spot : spot + size].reshape(rows, planes, lanes) for ref in (base_keep, base_in)]
        return [both_row(first, *halves, row) for row in range(last + 1)]

    scale = base_rows(FIELDS)
    for f in range(FIELDS):
        spot = (step * FIELDS + f) * width
        axial = incoming([ref[:, spot : spot + width] for ref in edges], weights)
        axial = axial.reshape(2 * rows, planes, lanes)
        base = base_rows(f)
        azim = [both_row(first, flux_keep[0, f], flux_in[0, f], row) for row in range(last + 1)]
        left, right, before, after = (ring[0, n, f] for n in range(4))
        down = [None] * (last + 1)
        down[last] = azim[last] + DERIV_ROOT * right
        for row in range(last - 1, -1, -1):
            down[row] = azim[row] + DERIV_ROOT * down[row + 1]
        up = left
        for row in range(last + 1):
            up = azim[row] + DERIV_ROOT * up
            total = axial[row] + DERIV_FAR * (up - down[row])
            total = total - DERIV_NEAR * (azim[row - 1] if row > 0 else before)
            total = total + DERIV_NEAR * (azim[row + 1] if row < last else after)
            out[0, f, row] = base[row] - scale[row] * total
        edge[:, spot : spot + width] = outgoing(basis, out[0, f].reshape(width, lanes))


def axial_local_kernel(step, values, own, out):
    weights = own.at[lax.axis_index("axial")]
    for f in range(FIELDS):
        lines = values[0, f].reshape(-1, values.shape[-1])
        out[0, f] = (lines + own_block(lines, weights)).reshape(out.shape[2:])


def axial_join_kernel(step, local, far, *rest):
    edges, (out, pack_a, pack_b, edge_a, edge_b, front) = rest[:-6], rest[-6:]
    pack, away = ((pack_a, edge_a), (pack_b, edge_b))[step]
    weights = far.at[lax.axis_index("axial")]
    rows, planes, lanes = local.shape[2:]
    width = rows * planes
    for f in range(FIELDS):
        spot = (step * FIELDS + f) * width
        axial = incoming([ref[:, spot : spot + width] for ref in edges], weights)
        axial = axial.reshape(rows, planes, lanes)
        tiles = [local[0, f, row] + axial[row] for row in range(rows)]
        for row in range(rows):
            out[0, f, row] = tiles[row]
        head, tail = moments(tiles, FILTER_ROOT)
        put_moments(step, f, head, tail, tiles[:2], tiles[rows - 2 :], pack, away)
    if step == 0:
        for row in range(rows):
            front[row : row + 1, :] = out[0, 2, row, 0:1, :] + out[0, 0, row, 0:1, :]
        for other in (pack_a, pack_b):
            other[other.shape[0] - rows :] = front[...]


def azim_local_kernel(step, values, out):
    rows = values.shape[2]
    for f in range(FIELDS):
        down = [None] * rows
        down[rows - 1] = values[0, f, rows - 1]
        for row in range(rows - 2, -1, -1):
            down[row] = values[0, f, row] + FILTER_ROOT * down[row + 1]
        up = None
        for row in range(rows):
            here = values[0, f, row]
            up = here if row == 0 else here + FILTER_ROOT * up
            total = (1.0 + FILTER_MID - FILTER_FAR) * here + FILTER_FAR * (up + down[row])
            for step, weight in ((1, FILTER_ONE), (2, FILTER_TWO)):
                if row >= step:
                    total = total + weight * values[0, f, row - step]
                if row + step < rows:
                    total = total + weight * values[0, f, row + step]
            out[0, f, row] = total


def joined_rows(upper, local, ring, field):
    rows = local.shape[2]
    one, zero = jnp.float32(1.0), jnp.float32(0.0)
    decay = jnp.float32(FILTER_ROOT**rows)
    left = jnp.where(upper, decay, one) * ring[0, 0, field]
    right = jnp.where(upper, one, decay) * ring[0, 1, field]
    low, high = jnp.where(upper, zero, one), jnp.where(upper, one, zero)
    before = [low * ring[0, 2 + n, field] for n in range(2)]
    after = [high * ring[0, 4 + n, field] for n in range(2)]
    tiles = []
    for row in range(rows):
        total = (
            local[0, field, row]
            + (FILTER_FAR * FILTER_ROOT ** (row + 1)) * left
            + (FILTER_FAR * FILTER_ROOT ** (rows - row)) * right
        )
        if row < 2:
            total = total + FILTER_TWO * before[row]
        if row == 0:
            total = total + FILTER_ONE * before[1]
        if row >= rows - 2:
            total = total + FILTER_TWO * after[row - (rows - 2)]
        if row == rows - 1:
            total = total + FILTER_ONE * after[0]
        tiles.append(total)
    return tiles


def azim_send_kernel(step, local, ring, out):
    rows = local.shape[2] // 2
    upper = 1 - core_index()
    there = local.at[:, :, pl.ds(upper * rows, rows)]
    for f in range(FIELDS):
        for row, tile in enumerate(joined_rows(upper == 1, there, ring, f)):
            out[0, f, row] = tile


def azim_keep_kernel(local, ring, out):
    for f in range(FIELDS):
        tiles = joined_rows(core_index() == 1, local, ring, f)
        out[f] = jnp.swapaxes(jnp.stack(tiles), 0, 1)


def place_rows_kernel(values, partial, out):
    for f in range(FIELDS):
        out[f] = jnp.swapaxes(values[0, f], 0, 1)


def entries_kernel(weight_table, weights, area, observers, bins, value, chosen_rows, chosen_bins):
    entries, rows, lanes = weights.shape
    observer_rows = lax.broadcasted_iota(jnp.int32, (chosen_rows.shape[0], lanes), 0)
    bin_rows = lax.broadcasted_iota(jnp.int32, (chosen_bins.shape[0], lanes), 0)
    for entry in range(entries):
        picked = weights[entry]
        found = jnp.zeros(picked.shape, jnp.float32)
        for part in range(weight_table.shape[0]):
            there = picked - part * lanes
            inside = (there >= 0) & (there < lanes)
            columns = jnp.broadcast_to(weight_table[part : part + 1, :], picked.shape)
            part_found = jnp.take_along_axis(columns, jnp.where(inside, there, 0), axis=1)
            found = jnp.where(inside, part_found, found)
        value[entry] = found * area[...]
        for row in range(rows):
            at = (row * entries + entry) * lanes
            hit = observer_rows == observers[entry, row : row + 1, :]
            chosen_rows[:, at : at + lanes] = jnp.where(hit, 1.0, 0.0).astype(jnp.bfloat16)
            hit = bin_rows == bins[entry, row : row + 1, :]
            chosen_bins[:, at : at + lanes] = jnp.where(hit, 1.0, 0.0).astype(jnp.bfloat16)


def surface_kernel(masks, around, front, *rest):
    *arrived, kept, sent, ring = rest
    rows = front.shape[0]
    chip = chip_index()
    for mask, ref in zip((0, *masks), (front, *arrived)):
        spot = pl.multiple_of(jnp.bitwise_xor(chip, mask) * rows, 8)
        ring[pl.ds(spot, rows), :] = ref[ref.shape[0] - rows :]
    surface = -1.0 + jnp.dot(
        around[chip],
        ring[...],
        precision=lax.Precision.HIGHEST,
        preferred_element_type=jnp.float32,
    )
    kept[...] = surface[: rows // 2]
    sent[...] = surface[rows // 2 :]


def signals_kernel(surface, surface_in, value, chosen_rows, chosen_bins, out, placed):
    entries, rows, lanes = value.shape
    height = out.shape[1]
    cells = jnp.where(core_index() == 0, surface[...], surface_in[...])
    for entry in range(entries):
        high, low = split(value[entry] * cells)
        for row in range(rows):
            at = (row * entries + entry) * lanes
            hit = chosen_bins[:, at : at + lanes]
            placed[:height, at : at + lanes] = hit * high[row : row + 1, :]
            placed[height:, at : at + lanes] = hit * low[row : row + 1, :]
    total = lax.dot_general(
        chosen_rows[...],
        placed[...],
        (((1,), (1,)), ((), ())),
        preferred_element_type=jnp.float32,
    )
    out[...] = total[:, :height] + total[:, height:]


def params(limit=VMEM_LIMIT):
    return pltpu.CompilerParams(vmem_limit_bytes=limit)


def cost(flops, moved):
    return pl.CostEstimate(flops=1, bytes_accessed=1, transcendentals=0)


def swap(values, axis, count, mask):
    return lax.ppermute(values, axis, [(i, i ^ mask) for i in range(count)])


def sibling(values, count):
    return lax.ppermute(values, "azim", [(i, i ^ 1) for i in range(count)])


def partner(values, count, turn, level):
    chips = count // 2
    pairs = []
    for i in range(count):
        chip, core = divmod(i, 2)
        there = ((((chip + turn) % chips) ^ ((2 << level) - 1)) - turn) % chips
        pairs.append((i, 2 * there + core))
    return lax.ppermute(values, "azim", pairs)


def waiting(kernel, count, wait):
    if not wait:
        return kernel
    return lambda *refs: kernel(*refs[:count], *refs[count + len(wait) :])


def by_chunk(kernel, blocked):
    def run(*refs):
        for step in range(2):
            pieces = [
                ref.at[step : step + 1] if cut else ref for ref, cut in zip(refs, blocked, strict=True)
            ]
            kernel(step, *pieces)

    return run


def whole_call(kernel, name, shapes, args, wait=(), scratch=()):
    whole = pl.BlockSpec(memory_space=pltpu.VMEM)
    return pl.pallas_call(
        waiting(kernel, len(args), wait),
        in_specs=[whole] * len(args) + [pl.BlockSpec(memory_space=pl.ANY)] * len(wait),
        out_specs=[whole] * len(shapes),
        out_shape=shapes,
        scratch_shapes=scratch,
        compiler_params=params(),
        cost_estimate=cost(1, 1),
        name=name,
    )(*args, *wait)


def ring_exchange(packs, arrived, edges, count, near, height, wide, wait=()):
    chips = count // 2
    levels = chips.bit_length() - 1
    tables = [ring_weights(chips, turn, wide) for turn in range(2)]
    lanes = packs[0].shape[1]
    rows = FIELDS * height
    joined = levels == 2
    sources = [[packs[turn], arrived[turn]] for turn in range(2)]
    if not joined:
        edges = [partner(edges[turn], count, 1 - turn, 0) for turn in range(2)]
    for level in range(1, levels):
        size = (2 + near if joined else 2) * rows
        args = [a for turn in range(2) for a in sources[turn] + ([edges[turn]] if joined else [])]
        sends = whole_call(
            functools.partial(totals_kernel, [t[0][level] for t in tables], joined, near, height),
            "group_totals",
            [jax.ShapeDtypeStruct((size, lanes), jnp.float32)] * 2,
            args,
            wait,
        )
        for turn in range(2):
            sources[turn].append(partner(sends[turn], count, turn, level))
    args = [
        a for turn in range(2) for a in sources[turn] + [sources[turn][-1] if joined else edges[turn]]
    ]

    def sums(wait=()):
        return whole_call(
            functools.partial(ring_kernel, [t[1] for t in tables], near, height),
            "ring_sums",
            [jax.ShapeDtypeStruct((2, 2 + 2 * near, FIELDS, height, lanes), jnp.float32)],
            args,
            wait,
        )[0]

    return sums, sends[0]


def per_device(
    density,
    velocity,
    pressure,
    axial_metric,
    azim_metric,
    volume,
    radial_term,
    panel_area,
    observer_ids,
    bin_ids,
    weight_ids,
    bin_weights,
):
    planes, rows, lanes = density.shape
    along = lax.axis_size("axial")
    around = lax.axis_size("azim")
    devices = along * around
    part = planes // 4
    lines = FIELDS * rows * part
    f32 = jnp.float32

    own_d, basis_d, far_d = map(halves, axial_tables(along, lanes, DERIV_ALPHA, "deriv"))
    own_f, basis_f, far_f = map(halves, axial_tables(along, lanes, FILTER_ALPHA, "filter"))
    filter_around = surface_table(around, rows)

    spec = pl.BlockSpec

    def every(k):
        return k

    def kept(k):
        return core_index() * 2 + k

    def sent(k):
        return (1 - core_index()) * 2 + k

    def field(where):
        return spec((part, rows, lanes), lambda k: (where(k), 0, 0))

    def vector(where, size=3):
        return spec((size, part, rows, lanes), lambda k: (0, where(k), 0, 0))

    def inner(where, size=FIELDS, tall=rows):
        return spec((1, size, tall, part, lanes), lambda k: (where(k), 0, 0, 0, 0))

    def inner_one(where, tall=rows):
        return spec((1, tall, part, lanes), lambda k: (where(k), 0, 0, 0))

    def edge(where, width=lines):
        return spec((BASIS, width), lambda k: (0, where(k)))

    def row_half(upper):
        return spec((1, FIELDS, rows, part, lanes), lambda k: (k, 0, upper(), 0, 0))

    def table(array):
        return spec((None,) + array.shape[1:], lambda k: (lax.axis_index("axial"),) + (0,) * (array.ndim - 1))

    def fixed(shape):
        return spec(shape, lambda k: (0,) * len(shape))

    def ring_spec(near):
        return spec((1, 2 + 2 * near, FIELDS, part, lanes), lambda k: (k, 0, 0, 0, 0))

    def shaped(*shape):
        return jax.ShapeDtypeStruct(shape, f32)

    def call(
        kernel, name, steps, ins, outs, shapes, args, wait=(), limit=VMEM_LIMIT, scratch=(), **more
    ):
        return pl.pallas_call(
            waiting(kernel, len(args), wait),
            grid=(steps,),
            in_specs=ins + [spec(memory_space=pl.ANY)] * len(wait),
            out_specs=outs,
            scratch_shapes=scratch,
            out_shape=shapes,
            compiler_params=params(limit),
            cost_estimate=cost(1, 1),
            name=name,
            **more,
        )(*args, *wait)

    tall = 2 * rows
    flux_scratch = pltpu.VMEM((FIELDS, part, rows, lanes), f32)
    half_shape = shaped(2, FIELDS, rows, part, lanes)
    chip_shape = shaped(2, FIELDS, tall, part, lanes)

    def apart(kernel, name, shapes, args, scratch, wait=(), limit=INPUT_LIMIT):
        several = isinstance(shapes, list)
        vmem = spec(memory_space=pltpu.VMEM)
        return pl.pallas_call(
            waiting(kernel, len(args), wait),
            in_specs=[spec(memory_space=pltpu.HBM)] * len(args)
            + [spec(memory_space=pl.ANY)] * len(wait),
            out_specs=[vmem] * len(shapes) if several else vmem,
            out_shape=shapes,
            scratch_shapes=scratch,
            compiler_params=params(limit),
            cost_estimate=cost(1, 1),
            name=name,
        )(*args, *wait)

    def azim_flux(mine, name, limit):
        one, three = (2 * part, rows, lanes), (3, 2 * part, rows, lanes)
        return apart(
            functools.partial(azim_flux_kernel, mine),
            name,
            [half_shape, shaped(2, 3, FIELDS, part, lanes)],
            (density, velocity, pressure, azim_metric, volume),
            [pltpu.VMEM(shape, f32) for shape in (one, three, one, three, one)]
            + [flux_scratch, pltpu.SemaphoreType.DMA((2, 5))],
            limit=limit,
        )

    flux_sent, pack_sent = azim_flux(False, "azim_flux_sent", INPUT_LIMIT)
    pack_in = sibling(pack_sent, around)
    flux_in = sibling(flux_sent, around)
    flux_kept, pack_kept = azim_flux(True, "azim_flux_kept", VMEM_LIMIT)
    *packs, edge_a, edge_b = whole_call(
        functools.partial(chip_moments_kernel, rows),
        "chip_moments",
        [shaped(3 * FIELDS * part, lanes)] * 2 + [shaped(FIELDS * part, lanes)] * 2,
        (pack_kept, pack_in),
    )

    arrived = [partner(packs[turn], around, turn, 0) for turn in range(2)]
    base, scale, edge_d = call(
        section_local_kernel,
        "section_local",
        4,
        [
            field(every),
            vector(every),
            field(every),
            vector(every),
            field(every),
            vector(every, FIELDS),
            table(own_d),
            fixed(basis_d.shape),
        ],
        [inner(every), inner_one(every), edge(every)],
        [
            shaped(4, FIELDS, rows, part, lanes),
            shaped(4, rows, part, lanes),
            shaped(BASIS, 4 * lines),
        ],
        (density, velocity, pressure, axial_metric, volume, radial_term, own_d, basis_d),
        wait=(packs[0], flux_in),
        scratch=[flux_scratch] * 2,
    )
    flat = shaped(2 * (FIELDS + 1) * rows * part + 2 * FIELDS * BASIS, lanes)
    base_kept, base_sent = whole_call(
        section_split_kernel, "section_split", [flat, flat], (base, scale, edge_d)
    )
    base_in = sibling(base_sent, around)
    (edge_d,) = whole_call(
        edge_both_kernel, "edge_both", [shaped(BASIS, 4 * lines)], (base_kept, base_in)
    )
    edges_d = [swap(edge_d, "axial", along, mask) for mask in range(1, along)]
    sums_d, sends_d = ring_exchange(
        packs, arrived, [edge_a, edge_b], around, 1, part, DERIV_ROOT ** (2 * rows)
    )

    ring_d = sums_d()
    sectioned, edge_f = whole_call(
        by_chunk(
            section_join_kernel,
            [True] * 2 + [False] * 2 + [True] + [False] * (along + 1) + [True, False],
        ),
        "section_join",
        [chip_shape, shaped(BASIS, 4 * lines)],
        (
            flux_kept,
            flux_in,
            base_kept,
            base_in,
            ring_d,
            jnp.asarray(basis_f),
            jnp.asarray(far_d),
            *edges_d,
        ),
    )
    edges_f = [swap(edge_f, "axial", along, mask) for mask in range(1, along)]
    (axial_local,) = whole_call(
        by_chunk(axial_local_kernel, [True, False, True]),
        "axial_local",
        [chip_shape],
        (sectioned, jnp.asarray(own_f)),
    )
    value, chosen_rows, chosen_bins = whole_call(
        entries_kernel,
        "entries",
        [
            shaped(*weight_ids.shape),
            jax.ShapeDtypeStruct((OBSERVERS, weight_ids.size), jnp.bfloat16),
            jax.ShapeDtypeStruct((TIME_BINS, weight_ids.size), jnp.bfloat16),
        ],
        (bin_weights.reshape(-1, lanes), weight_ids, panel_area, observer_ids, bin_ids),
        wait=(edge_f,),
    )
    chips = around // 2
    height = FIELDS * part
    shapes = [4 * height + tall] * 2 + [2 * height] * 2 + [tall]
    smoothed, *packs, edge_a, edge_b, front = whole_call(
        by_chunk(axial_join_kernel, [True] + [False] * along + [True] + [False] * 5),
        "axial_join",
        [chip_shape] + [shaped(size, lanes) for size in shapes],
        (axial_local, jnp.asarray(far_f), *edges_f),
        wait=(value,),
    )
    arrived = [partner(packs[turn], around, turn, 0) for turn in range(2)]

    masks = list(range(1, chips))
    fronts = [arrived[0], None, arrived[1]] if chips == 4 else [None] * (chips - 1)
    for at, mask in enumerate(masks):
        if fronts[at] is None:
            pairs = [(i, 2 * ((i // 2) ^ mask) + i % 2) for i in range(around)]
            fronts[at] = lax.ppermute(front, "azim", pairs)
    surface, surface_sent = whole_call(
        functools.partial(surface_kernel, masks),
        "surface",
        [shaped(rows, lanes)] * 2,
        (jnp.asarray(filter_around), front, *fronts),
        scratch=[pltpu.VMEM((around * rows, lanes), f32)],
    )
    surface_in = lax.ppermute(surface_sent, "azim", [(i, i + 1) for i in range(0, around, 2)])
    sums_f, sends_f = ring_exchange(
        packs,
        arrived,
        [edge_a, edge_b],
        around,
        2,
        part,
        FILTER_ROOT ** (2 * rows),
        wait=(fronts[1],),
    )
    (partial,) = whole_call(
        signals_kernel,
        "signals",
        [shaped(OBSERVERS, TIME_BINS)],
        (surface, surface_in, value, chosen_rows, chosen_bins),
        wait=(sends_f,),
        scratch=[pltpu.VMEM((2 * TIME_BINS, weight_ids.size), jnp.bfloat16)],
    )
    shares = lax.all_to_all(
        partial.reshape(devices, OBSERVERS // devices, TIME_BINS),
        ("axial", "azim"),
        0,
        0,
        tiled=True,
    )
    (azim_local,) = whole_call(
        by_chunk(azim_local_kernel, [True, True]),
        "azim_local",
        [chip_shape],
        (smoothed,),
        wait=(sends_f,),
    )
    ring_f = sums_f((partial,))
    state_shape = shaped(FIELDS, planes, rows, lanes)
    (rows_sent,) = whole_call(
        by_chunk(azim_send_kernel, [True] * 3),
        "azim_join_sent",
        [half_shape],
        (azim_local, ring_f),
    )
    rows_in = sibling(rows_sent, around)
    mine = call(
        azim_keep_kernel,
        "azim_join_kept",
        2,
        [row_half(core_index), ring_spec(2)],
        vector(kept, FIELDS),
        state_shape,
        (azim_local, ring_f),
    )
    new_state = call(
        place_rows_kernel,
        "place_rows",
        2,
        [inner(every), spec(memory_space=pl.ANY)],
        vector(sent, FIELDS),
        state_shape,
        (rows_in, mine),
        input_output_aliases={1: 0},
    )
    shares, new_state = lax.optimization_barrier((shares, new_state))
    return new_state, jnp.sum(shares, axis=0)


def solution(mesh):
    placed = (
        P(None, "azim", "axial"),
        P(None, None, "azim", "axial"),
        P(None, "azim", "axial"),
        P(None, None, "azim", "axial"),
        P(None, None, "azim", "axial"),
        P(None, "azim", "axial"),
        P(None, None, "azim", "axial"),
        P("azim", "axial"),
        P(None, "azim", "axial"),
        P(None, "azim", "axial"),
        P(None, "azim", "axial"),
        P(),
    )
    return jax.shard_map(
        per_device,
        mesh=mesh,
        in_specs=placed,
        out_specs=(P(None, None, "azim", "axial"), P(("axial", "azim"), None)),
        check_vma=False,
    )
```

```python
import functools
import math

import jax
import jax.numpy as jnp
import numpy as np
from jax import lax
from jax.experimental import pallas as pl
from jax.experimental.pallas import tpu as pltpu
from jax.sharding import PartitionSpec as P

OBSERVERS = 512
TIME_BINS = 128

GAMMA = 1.4
SECTION = 0.25
DERIV_ALPHA = 1.0 / 3.0
FILTER_ALPHA = 0.499
FIELDS = 5
BASIS = 8
VMEM_LIMIT = 16 * 1024 * 1024
INPUT_LIMIT = 60 * 1024 * 1024


def decay_root(alpha):
    return (-1.0 + math.sqrt(1.0 - 4.0 * alpha * alpha)) / (2.0 * alpha)


DERIV_ROOT = decay_root(DERIV_ALPHA)
FILTER_ROOT = decay_root(FILTER_ALPHA)

DERIV_NEAR = 1.0 / 12.0
DERIV_FAR = (
    (25.0 / 36.0) * (DERIV_ROOT - 1.0 / DERIV_ROOT) / (1.0 + 2.0 * DERIV_ALPHA * DERIV_ROOT)
)

_B = FILTER_ALPHA
_EDGE = (1.0 - 2.0 * _B) / 64.0
_Q2 = 1.0 / _B
_Q1 = (-6.0 - _Q2) / _B
_Q0 = (12.0 - _Q1) / _B
_RHO = -8.0 - _Q0
FILTER_MID = _EDGE * (_Q0 + 2.0 * _Q2)
FILTER_ONE = _EDGE * _Q1
FILTER_TWO = _EDGE * _Q2
FILTER_FAR = _EDGE * _RHO / (1.0 + 2.0 * _B * FILTER_ROOT)


def open_operator(length, alpha, side):
    base = decay_root(alpha)
    tri = np.eye(length) + alpha * (np.eye(length, k=1) + np.eye(length, k=-1))
    tri[0, 0] = -alpha / base
    return np.linalg.solve(tri, side)


def deriv_matrix(length):
    return (7.0 / 9.0) * (np.eye(length, k=1) - np.eye(length, k=-1)) + (1.0 / 36.0) * (
        np.eye(length, k=2) - np.eye(length, k=-2)
    )


def filter_matrix(length):
    beta = FILTER_ALPHA
    coeffs = [
        (11.0 + 10.0 * beta) / 16.0,
        (15.0 + 34.0 * beta) / 32.0,
        (-3.0 + 6.0 * beta) / 16.0,
        (1.0 - 2.0 * beta) / 32.0,
    ]
    total = coeffs[0] * np.eye(length)
    for shift in range(1, 4):
        total = total + 0.5 * coeffs[shift] * (np.eye(length, k=shift) + np.eye(length, k=-shift))
    return total


def axial_tables(count, width, alpha, kind):
    length = count * width
    side = deriv_matrix(length) if kind == "deriv" else filter_matrix(length)
    whole = open_operator(length, alpha, side)
    base = decay_root(alpha)
    basis = np.zeros((BASIS, width))
    for edge in range(3):
        basis[edge, edge] = 1.0
        basis[3 + edge, width - 3 + edge] = 1.0
    basis[6] = base ** np.arange(width - 1, -1, -1, dtype=np.float64)
    basis[7] = base ** np.arange(width, dtype=np.float64)
    inverse = np.linalg.pinv(basis)
    own = np.zeros((count, width, width))
    far = np.zeros((count, max(count - 1, 1) * BASIS, width))
    for here in range(count):
        rows = whole[here * width : (here + 1) * width]
        own[here] = rows[:, here * width : (here + 1) * width].T
        if kind == "filter":
            own[here] -= np.eye(width)
        for shift in range(1, count):
            there = here ^ shift
            block = rows[:, there * width : (there + 1) * width]
            far[here, (shift - 1) * BASIS : shift * BASIS] = (block @ inverse).T
    return own, basis, far


def surface_table(around, rows):
    length = around * rows
    turn = np.roll(np.eye(length), 1, axis=1)
    beta = FILTER_ALPHA
    side = (11.0 + 10.0 * beta) / 16.0 * np.eye(length)
    coeffs = [(15.0 + 34.0 * beta) / 64.0, (-3.0 + 6.0 * beta) / 32.0, (1.0 - 2.0 * beta) / 64.0]
    for shift, weight in enumerate(coeffs, start=1):
        step = np.linalg.matrix_power(turn, shift)
        side = side + weight * (step + step.T)
    cycle = np.linalg.solve(np.eye(length) + beta * (turn + turn.T), side)
    return cycle.reshape(around // 2, 2 * rows, length).astype(np.float32)


def halves(table):
    high = np.asarray(table, np.float32).astype(jnp.bfloat16)
    low = (np.asarray(table, np.float64) - high.astype(np.float64)).astype(jnp.bfloat16)
    return np.stack([high, low], axis=-3)


def split(values):
    high = values.astype(jnp.bfloat16)
    return high, (values - high.astype(jnp.float32)).astype(jnp.bfloat16)


def dots(left, right, dims):
    out = None
    for a, b in ((0, 0), (1, 0), (0, 1)):
        part = lax.dot_general(
            left[a], right[b], (dims, ((), ())), preferred_element_type=jnp.float32
        )
        out = part if out is None else out + part
    return out


def outgoing(basis_ref, lines):
    return dots((basis_ref[0], basis_ref[1]), split(lines), ((1,), (1,)))


def incoming(parts, far_ref):
    return dots(split(jnp.concatenate(parts, axis=0)), (far_ref[0], far_ref[1]), ((0,), (0,)))


def own_block(lines, own_ref):
    return dots(split(lines), (own_ref[0], own_ref[1]), ((1,), (0,)))


def tile_energy(density, velocity, pressure):
    return pressure * (1.0 / (GAMMA - 1.0)) + 0.5 * density * (
        velocity[0] * velocity[0] + velocity[1] * velocity[1] + velocity[2] * velocity[2]
    )


def tile_flux(density, velocity, pressure, energy, metric, volume):
    contra = metric[0] * velocity[0] + metric[1] * velocity[1] + metric[2] * velocity[2]
    volume_contra = volume * contra
    mass = density * volume_contra
    push = volume * pressure
    pieces = [mass]
    for comp in range(3):
        pieces.append(mass * velocity[comp] + metric[comp] * push)
    pieces.append((energy + pressure) * volume_contra)
    return pieces


def core_index():
    return lax.rem(lax.axis_index("azim"), 2)


def chip_index():
    return lax.div(lax.axis_index("azim"), 2)


def ring_weights(chips, turn, wide):
    levels = chips.bit_length() - 1
    size = 2 * (levels + 1)
    sends = np.zeros((levels, 2, chips, size))
    sums = np.zeros((2, chips, size))
    unit = np.eye(size)
    for chip in range(chips):
        spot = (chip + turn) % chips
        head, tail = unit[0], unit[1]
        left = right = np.zeros(size)
        for level in range(levels):
            group = 1 << level
            inside = spot % group
            sends[level, :, chip] = head, tail
            head_in, tail_in = unit[2 * level + 2], unit[2 * level + 3]
            if (spot >> level) & 1:
                left = left + wide**inside * head_in
                head, tail = head + wide**group * head_in, tail_in + wide**group * tail
            else:
                right = right + wide ** (group - 1 - inside) * tail_in
                head, tail = head_in + wide**group * head, tail + wide**group * tail_in
        close = 1.0 / (1.0 - wide**chips)
        sums[0, chip] = left + close * wide**spot * head
        sums[1, chip] = right + close * wide ** (chips - 1 - spot) * tail
    return sends, sums


def chosen(index, values):
    if not np.any(values):
        return None
    out = jnp.float32(values[0])
    for at in range(1, len(values)):
        if values[at] != values[at - 1] or np.any(values != values[0]):
            out = jnp.where(index == at, jnp.float32(values[at]), out)
    return out


def slot(value, field, height):
    start = (value * FIELDS + field) * height
    return slice(start, start + height)


def mixed(chip, table, sources, field, height):
    total = None
    for at, source in enumerate(sources):
        for part in range(2):
            weight = chosen(chip, table[:, 2 * at + part])
            if weight is not None:
                term = weight * source[slot(part, field, height)]
                total = term if total is None else total + term
    return total


def moments(tiles, root):
    head = tail = tiles[0]
    for row in range(1, len(tiles)):
        head = tiles[row] + root * head
        tail = tail + (root**row) * tiles[row]
    return head, tail


def fetched(sources, buffers, sem, pieces):
    copies = [
        [
            pltpu.make_async_copy(source.at[where], buffer.at[there], sem.at[at, n])
            for n, (source, buffer, (where, there)) in enumerate(zip(sources, buffers, piece))
        ]
        for at, piece in enumerate(pieces)
    ]
    for group in copies:
        for copy in group:
            copy.start()
    return copies


def azim_flux_kernel(mine, density, velocity, pressure, azim_metric, volume, out, pack, *scratch):
    *buffers, flux, sem = scratch
    chunks, _, rows, planes, _ = out.shape
    core = core_index()
    start = (core if mine else 1 - core) * chunks * planes
    pieces = []
    for chunk in range(chunks):
        here, there = pl.ds(start + chunk * planes, planes), pl.ds(chunk * planes, planes)
        whole = slice(None)
        pieces.append(
            [(here, there), ((whole, here), (whole, there)), (here, there)]
            + [((whole, here), (whole, there)), (here, there)]
        )
    groups = fetched((density, velocity, pressure, azim_metric, volume), buffers, sem, pieces)
    first = core == 0
    for chunk in range(chunks):
        for copy in groups[chunk]:
            copy.wait()
        rho_in, vel_in, pres_in, metric_in, vol_in = buffers
        for plane in range(planes):
            at = chunk * planes + plane
            rho, pres = rho_in[at], pres_in[at]
            vel = [vel_in[c, at] for c in range(3)]
            energy = tile_energy(rho, vel, pres)
            metric = [metric_in[c, at] for c in range(3)]
            for f, piece in enumerate(tile_flux(rho, vel, pres, energy, metric, vol_in[at])):
                flux[f, plane] = piece
        for f in range(FIELDS):
            turned = jnp.swapaxes(flux[f], 0, 1)
            out[chunk, f] = turned
            tiles = [turned[row] for row in range(rows)]
            pack[chunk, 0, f], pack[chunk, 1, f] = moments(tiles, DERIV_ROOT)
            pack[chunk, 2, f] = jnp.where(first, tiles[0], tiles[rows - 1])


def put_moments(step, field, head, tail, low, high, pack, edge):
    on_left = lax.rem(chip_index() + step, 2) == 0
    height = head.shape[0]
    pack[slot(0, field, height)] = head
    pack[slot(1, field, height)] = tail
    for n in range(len(low)):
        pack[slot(2 + n, field, height)] = jnp.where(on_left, high[n], low[n])
        edge[slot(n, field, height)] = jnp.where(on_left, low[n], high[n])


def chip_moments_kernel(rows, keep, other, pack_a, pack_b, edge_a, edge_b):
    first = core_index() == 0
    decay, one = jnp.float32(DERIV_ROOT**rows), jnp.float32(1.0)
    near, away = jnp.where(first, decay, one), jnp.where(first, one, decay)
    height = keep.shape[3]
    for turn, (pack, edge) in enumerate(((pack_a, edge_a), (pack_b, edge_b))):
        on_left = lax.rem(chip_index() + turn, 2) == 0
        mine = first != on_left
        for f in range(FIELDS):
            head, tail, row = (keep[turn, n, f] for n in range(3))
            head_in, tail_in, row_in = (other[turn, n, f] for n in range(3))
            pack[slot(0, f, height)] = near * head + away * head_in
            pack[slot(1, f, height)] = away * tail + near * tail_in
            pack[slot(2, f, height)] = jnp.where(mine, row, row_in)
            edge[slot(0, f, height)] = jnp.where(mine, row_in, row)


def totals_kernel(table, joined, near, height, *refs):
    chip = chip_index()
    *refs, send_a, send_b = refs
    count = len(refs) // 2
    for turn, send in enumerate((send_a, send_b)):
        mine = refs[turn * count : (turn + 1) * count]
        sources = mine[:-1] if joined else mine
        for f in range(FIELDS):
            send[slot(0, f, height)] = mixed(chip, table[turn][0], sources, f, height)
            send[slot(1, f, height)] = mixed(chip, table[turn][1], sources, f, height)
        if joined:
            send[2 * FIELDS * height :] = mine[-1][...]


def ring_kernel(table, near, height, *refs):
    chip = chip_index()
    *refs, out = refs
    count = len(refs) // 2
    for turn in range(2):
        *sources, edge = refs[turn * count : (turn + 1) * count]
        on_left = lax.rem(chip + turn, 2) == 0
        start = 0 if edge.shape[0] == near * FIELDS * height else 2
        for f in range(FIELDS):
            out[turn, 0, f] = mixed(chip, table[turn][0], sources, f, height)
            out[turn, 1, f] = mixed(chip, table[turn][1], sources, f, height)
            for n in range(near):
                paired = sources[1][slot(2 + n, f, height)]
                other = edge[slot(start + n, f, height)]
                out[turn, 2 + n, f] = jnp.where(on_left, other, paired)
                out[turn, 2 + near + n, f] = jnp.where(on_left, paired, other)


def section_local_kernel(
    density,
    velocity,
    pressure,
    axial_metric,
    volume,
    radial,
    own,
    basis,
    base_out,
    scale_out,
    edge_out,
    axial_flux,
    start,
):
    planes, rows, lanes = density.shape
    for plane in range(planes):
        rho = density[plane]
        vel = [velocity[c, plane] for c in range(3)]
        pres = pressure[plane]
        vol = volume[plane]
        energy = tile_energy(rho, vel, pres)
        axial = tile_flux(rho, vel, pres, energy, [axial_metric[c, plane] for c in range(3)], vol)
        state = [rho, rho * vel[0], rho * vel[1], rho * vel[2], energy]
        for f in range(FIELDS):
            axial_flux[f, plane] = axial[f]
            start[f, plane] = state[f] + SECTION * radial[f, plane]
    scale = jnp.swapaxes(SECTION / volume[...], 0, 1)
    scale_out[0] = scale
    for f in range(FIELDS):
        flux = jnp.swapaxes(axial_flux[f], 0, 1).reshape(rows * planes, lanes)
        edge_out[:, f * rows * planes : (f + 1) * rows * planes] = outgoing(basis, flux)
        deriv = own_block(flux, own).reshape(rows, planes, lanes)
        base_out[0, f] = jnp.swapaxes(start[f], 0, 1) - scale * deriv


def section_split_kernel(base, scale, edge, kept, sent):
    fields, rows, planes, lanes = base.shape[1:]
    size = rows * planes
    core = core_index()
    for mine, out in ((core, kept), (1 - core, sent)):
        for chunk in range(2):
            at = 2 * mine + chunk
            for f in range(fields + 1):
                spot = (chunk * (fields + 1) + f) * size
                piece = base[at, f] if f < fields else scale[at]
                out[spot : spot + size] = piece.reshape(size, lanes)
            for f in range(fields):
                from_spot = pl.multiple_of((at * fields + f) * size, 128)
                spot = 2 * (fields + 1) * size + (chunk * fields + f) * BASIS
                out[spot : spot + BASIS] = edge[:, pl.ds(from_spot, size)]


def edge_both_kernel(kept, arrived, edge):
    lanes = kept.shape[1]
    start = kept.shape[0] - 2 * FIELDS * BASIS
    first = core_index() == 0
    for at in range(2 * FIELDS):
        piece = slice(start + at * BASIS, start + (at + 1) * BASIS)
        mine, theirs = kept[piece], arrived[piece]
        spot = 2 * at * lanes
        edge[:, spot : spot + lanes] = jnp.where(first, mine, theirs)
        edge[:, spot + lanes : spot + 2 * lanes] = jnp.where(first, theirs, mine)


def both_row(first, mine, theirs, row):
    rows = mine.shape[0]
    if row < rows:
        return jnp.where(first, mine[row], theirs[row])
    return jnp.where(first, theirs[row - rows], mine[row - rows])


def section_join_kernel(
    step, flux_keep, flux_in, base_keep, base_in, ring, basis, far, *rest
):
    *edges, out, edge = rest
    rows, planes, lanes = flux_keep.shape[2:]
    first = core_index() == 0
    last = 2 * rows - 1
    width = 2 * rows * planes
    size = rows * planes
    weights = far.at[lax.axis_index("axial")]

    def base_rows(f):
        spot = (step * (FIELDS + 1) + f) * size
        halves = [ref[spot : spot + size].reshape(rows, planes, lanes) for ref in (base_keep, base_in)]
        return [both_row(first, *halves, row) for row in range(last + 1)]

    scale = base_rows(FIELDS)
    for f in range(FIELDS):
        spot = (step * FIELDS + f) * width
        axial = incoming([ref[:, spot : spot + width] for ref in edges], weights)
        axial = axial.reshape(2 * rows, planes, lanes)
        base = base_rows(f)
        azim = [both_row(first, flux_keep[0, f], flux_in[0, f], row) for row in range(last + 1)]
        left, right, before, after = (ring[0, n, f] for n in range(4))
        down = [None] * (last + 1)
        down[last] = azim[last] + DERIV_ROOT * right
        for row in range(last - 1, -1, -1):
            down[row] = azim[row] + DERIV_ROOT * down[row + 1]
        up = left
        for row in range(last + 1):
            up = azim[row] + DERIV_ROOT * up
            total = axial[row] + DERIV_FAR * (up - down[row])
            total = total - DERIV_NEAR * (azim[row - 1] if row > 0 else before)
            total = total + DERIV_NEAR * (azim[row + 1] if row < last else after)
            out[0, f, row] = base[row] - scale[row] * total
        edge[:, spot : spot + width] = outgoing(basis, out[0, f].reshape(width, lanes))


def axial_local_kernel(step, values, own, out):
    weights = own.at[lax.axis_index("axial")]
    for f in range(FIELDS):
        lines = values[0, f].reshape(-1, values.shape[-1])
        out[0, f] = (lines + own_block(lines, weights)).reshape(out.shape[2:])


def axial_join_kernel(step, local, far, *rest):
    edges, (out, pack_a, pack_b, edge_a, edge_b, front) = rest[:-6], rest[-6:]
    pack, away = ((pack_a, edge_a), (pack_b, edge_b))[step]
    weights = far.at[lax.axis_index("axial")]
    rows, planes, lanes = local.shape[2:]
    width = rows * planes
    for f in range(FIELDS):
        spot = (step * FIELDS + f) * width
        axial = incoming([ref[:, spot : spot + width] for ref in edges], weights)
        axial = axial.reshape(rows, planes, lanes)
        tiles = [local[0, f, row] + axial[row] for row in range(rows)]
        for row in range(rows):
            out[0, f, row] = tiles[row]
        head, tail = moments(tiles, FILTER_ROOT)
        put_moments(step, f, head, tail, tiles[:2], tiles[rows - 2 :], pack, away)
    if step == 0:
        for row in range(rows):
            front[row : row + 1, :] = out[0, 2, row, 0:1, :] + out[0, 0, row, 0:1, :]
        for other in (pack_a, pack_b):
            other[other.shape[0] - rows :] = front[...]


def azim_local_kernel(step, values, out):
    rows = values.shape[2]
    for f in range(FIELDS):
        down = [None] * rows
        down[rows - 1] = values[0, f, rows - 1]
        for row in range(rows - 2, -1, -1):
            down[row] = values[0, f, row] + FILTER_ROOT * down[row + 1]
        up = None
        for row in range(rows):
            here = values[0, f, row]
            up = here if row == 0 else here + FILTER_ROOT * up
            total = (1.0 + FILTER_MID - FILTER_FAR) * here + FILTER_FAR * (up + down[row])
            for step, weight in ((1, FILTER_ONE), (2, FILTER_TWO)):
                if row >= step:
                    total = total + weight * values[0, f, row - step]
                if row + step < rows:
                    total = total + weight * values[0, f, row + step]
            out[0, f, row] = total


def joined_rows(upper, local, ring, field):
    rows = local.shape[2]
    one, zero = jnp.float32(1.0), jnp.float32(0.0)
    decay = jnp.float32(FILTER_ROOT**rows)
    left = jnp.where(upper, decay, one) * ring[0, 0, field]
    right = jnp.where(upper, one, decay) * ring[0, 1, field]
    low, high = jnp.where(upper, zero, one), jnp.where(upper, one, zero)
    before = [low * ring[0, 2 + n, field] for n in range(2)]
    after = [high * ring[0, 4 + n, field] for n in range(2)]
    tiles = []
    for row in range(rows):
        total = (
            local[0, field, row]
            + (FILTER_FAR * FILTER_ROOT ** (row + 1)) * left
            + (FILTER_FAR * FILTER_ROOT ** (rows - row)) * right
        )
        if row < 2:
            total = total + FILTER_TWO * before[row]
        if row == 0:
            total = total + FILTER_ONE * before[1]
        if row >= rows - 2:
            total = total + FILTER_TWO * after[row - (rows - 2)]
        if row == rows - 1:
            total = total + FILTER_ONE * after[0]
        tiles.append(total)
    return tiles


def azim_send_kernel(step, local, ring, out):
    rows = local.shape[2] // 2
    upper = 1 - core_index()
    there = local.at[:, :, pl.ds(upper * rows, rows)]
    for f in range(FIELDS):
        for row, tile in enumerate(joined_rows(upper == 1, there, ring, f)):
            out[0, f, row] = tile


def azim_keep_kernel(local, ring, out):
    for f in range(FIELDS):
        tiles = joined_rows(core_index() == 1, local, ring, f)
        out[f] = jnp.swapaxes(jnp.stack(tiles), 0, 1)


def place_rows_kernel(values, partial, out):
    for f in range(FIELDS):
        out[f] = jnp.swapaxes(values[0, f], 0, 1)


def entries_kernel(weight_table, weights, area, observers, bins, value, chosen_rows, chosen_bins):
    entries, rows, lanes = weights.shape
    observer_rows = lax.broadcasted_iota(jnp.int32, (chosen_rows.shape[0], lanes), 0)
    bin_rows = lax.broadcasted_iota(jnp.int32, (chosen_bins.shape[0], lanes), 0)
    for entry in range(entries):
        picked = weights[entry]
        found = jnp.zeros(picked.shape, jnp.float32)
        for part in range(weight_table.shape[0]):
            there = picked - part * lanes
            inside = (there >= 0) & (there < lanes)
            columns = jnp.broadcast_to(weight_table[part : part + 1, :], picked.shape)
            part_found = jnp.take_along_axis(columns, jnp.where(inside, there, 0), axis=1)
            found = jnp.where(inside, part_found, found)
        value[entry] = found * area[...]
        for row in range(rows):
            at = (row * entries + entry) * lanes
            hit = observer_rows == observers[entry, row : row + 1, :]
            chosen_rows[:, at : at + lanes] = jnp.where(hit, 1.0, 0.0).astype(jnp.bfloat16)
            hit = bin_rows == bins[entry, row : row + 1, :]
            chosen_bins[:, at : at + lanes] = jnp.where(hit, 1.0, 0.0).astype(jnp.bfloat16)


def surface_kernel(masks, around, front, *rest):
    *arrived, kept, sent, ring = rest
    rows = front.shape[0]
    chip = chip_index()
    for mask, ref in zip((0, *masks), (front, *arrived)):
        spot = pl.multiple_of(jnp.bitwise_xor(chip, mask) * rows, 8)
        ring[pl.ds(spot, rows), :] = ref[ref.shape[0] - rows :]
    surface = -1.0 + jnp.dot(
        around[chip],
        ring[...],
        precision=lax.Precision.HIGHEST,
        preferred_element_type=jnp.float32,
    )
    kept[...] = surface[: rows // 2]
    sent[...] = surface[rows // 2 :]


def signals_kernel(surface, surface_in, value, chosen_rows, chosen_bins, out, placed):
    entries, rows, lanes = value.shape
    height = out.shape[1]
    cells = jnp.where(core_index() == 0, surface[...], surface_in[...])
    for entry in range(entries):
        high, low = split(value[entry] * cells)
        for row in range(rows):
            at = (row * entries + entry) * lanes
            hit = chosen_bins[:, at : at + lanes]
            placed[:height, at : at + lanes] = hit * high[row : row + 1, :]
            placed[height:, at : at + lanes] = hit * low[row : row + 1, :]
    total = lax.dot_general(
        chosen_rows[...],
        placed[...],
        (((1,), (1,)), ((), ())),
        preferred_element_type=jnp.float32,
    )
    out[...] = total[:, :height] + total[:, height:]


def params(limit=VMEM_LIMIT):
    return pltpu.CompilerParams(vmem_limit_bytes=limit)


def cost(flops, moved):
    return pl.CostEstimate(flops=1, bytes_accessed=1, transcendentals=0)


def swap(values, axis, count, mask):
    return lax.ppermute(values, axis, [(i, i ^ mask) for i in range(count)])


def sibling(values, count):
    return lax.ppermute(values, "azim", [(i, i ^ 1) for i in range(count)])


def partner(values, count, turn, level):
    chips = count // 2
    pairs = []
    for i in range(count):
        chip, core = divmod(i, 2)
        there = ((((chip + turn) % chips) ^ ((2 << level) - 1)) - turn) % chips
        pairs.append((i, 2 * there + core))
    return lax.ppermute(values, "azim", pairs)


def waiting(kernel, count, wait):
    if not wait:
        return kernel
    return lambda *refs: kernel(*refs[:count], *refs[count + len(wait) :])


def by_chunk(kernel, blocked):
    def run(*refs):
        for step in range(2):
            pieces = [
                ref.at[step : step + 1] if cut else ref for ref, cut in zip(refs, blocked, strict=True)
            ]
            kernel(step, *pieces)

    return run


def whole_call(kernel, name, shapes, args, wait=(), scratch=()):
    whole = pl.BlockSpec(memory_space=pltpu.VMEM)
    return pl.pallas_call(
        waiting(kernel, len(args), wait),
        in_specs=[whole] * len(args) + [pl.BlockSpec(memory_space=pl.ANY)] * len(wait),
        out_specs=[whole] * len(shapes),
        out_shape=shapes,
        scratch_shapes=scratch,
        compiler_params=params(),
        cost_estimate=cost(1, 1),
        name=name,
    )(*args, *wait)


def ring_exchange(packs, arrived, edges, count, near, height, wide, wait=()):
    chips = count // 2
    levels = chips.bit_length() - 1
    tables = [ring_weights(chips, turn, wide) for turn in range(2)]
    lanes = packs[0].shape[1]
    rows = FIELDS * height
    joined = levels == 2
    sources = [[packs[turn], arrived[turn]] for turn in range(2)]
    if not joined:
        edges = [partner(edges[turn], count, 1 - turn, 0) for turn in range(2)]
    for level in range(1, levels):
        size = (2 + near if joined else 2) * rows
        args = [a for turn in range(2) for a in sources[turn] + ([edges[turn]] if joined else [])]
        sends = whole_call(
            functools.partial(totals_kernel, [t[0][level] for t in tables], joined, near, height),
            "group_totals",
            [jax.ShapeDtypeStruct((size, lanes), jnp.float32)] * 2,
            args,
            wait,
        )
        for turn in range(2):
            sources[turn].append(partner(sends[turn], count, turn, level))
    args = [
        a for turn in range(2) for a in sources[turn] + [sources[turn][-1] if joined else edges[turn]]
    ]

    def sums(wait=()):
        return whole_call(
            functools.partial(ring_kernel, [t[1] for t in tables], near, height),
            "ring_sums",
            [jax.ShapeDtypeStruct((2, 2 + 2 * near, FIELDS, height, lanes), jnp.float32)],
            args,
            wait,
        )[0]

    return sums, sends[0]


def per_device(
    density,
    velocity,
    pressure,
    axial_metric,
    azim_metric,
    volume,
    radial_term,
    panel_area,
    observer_ids,
    bin_ids,
    weight_ids,
    bin_weights,
):
    planes, rows, lanes = density.shape
    along = lax.axis_size("axial")
    around = lax.axis_size("azim")
    devices = along * around
    part = planes // 4
    lines = FIELDS * rows * part
    f32 = jnp.float32

    own_d, basis_d, far_d = map(halves, axial_tables(along, lanes, DERIV_ALPHA, "deriv"))
    own_f, basis_f, far_f = map(halves, axial_tables(along, lanes, FILTER_ALPHA, "filter"))
    filter_around = surface_table(around, rows)

    spec = pl.BlockSpec

    def every(k):
        return k

    def kept(k):
        return core_index() * 2 + k

    def sent(k):
        return (1 - core_index()) * 2 + k

    def field(where):
        return spec((part, rows, lanes), lambda k: (where(k), 0, 0))

    def vector(where, size=3):
        return spec((size, part, rows, lanes), lambda k: (0, where(k), 0, 0))

    def inner(where, size=FIELDS, tall=rows):
        return spec((1, size, tall, part, lanes), lambda k: (where(k), 0, 0, 0, 0))

    def inner_one(where, tall=rows):
        return spec((1, tall, part, lanes), lambda k: (where(k), 0, 0, 0))

    def edge(where, width=lines):
        return spec((BASIS, width), lambda k: (0, where(k)))

    def row_half(upper):
        return spec((1, FIELDS, rows, part, lanes), lambda k: (k, 0, upper(), 0, 0))

    def table(array):
        return spec((None,) + array.shape[1:], lambda k: (lax.axis_index("axial"),) + (0,) * (array.ndim - 1))

    def fixed(shape):
        return spec(shape, lambda k: (0,) * len(shape))

    def ring_spec(near):
        return spec((1, 2 + 2 * near, FIELDS, part, lanes), lambda k: (k, 0, 0, 0, 0))

    def shaped(*shape):
        return jax.ShapeDtypeStruct(shape, f32)

    def call(
        kernel, name, steps, ins, outs, shapes, args, wait=(), limit=VMEM_LIMIT, scratch=(), **more
    ):
        return pl.pallas_call(
            waiting(kernel, len(args), wait),
            grid=(steps,),
            in_specs=ins + [spec(memory_space=pl.ANY)] * len(wait),
            out_specs=outs,
            scratch_shapes=scratch,
            out_shape=shapes,
            compiler_params=params(limit),
            cost_estimate=cost(1, 1),
            name=name,
            **more,
        )(*args, *wait)

    tall = 2 * rows
    flux_scratch = pltpu.VMEM((FIELDS, part, rows, lanes), f32)
    half_shape = shaped(2, FIELDS, rows, part, lanes)
    chip_shape = shaped(2, FIELDS, tall, part, lanes)

    def apart(kernel, name, shapes, args, scratch, wait=(), limit=INPUT_LIMIT):
        several = isinstance(shapes, list)
        vmem = spec(memory_space=pltpu.VMEM)
        return pl.pallas_call(
            waiting(kernel, len(args), wait),
            in_specs=[spec(memory_space=pltpu.HBM)] * len(args)
            + [spec(memory_space=pl.ANY)] * len(wait),
            out_specs=[vmem] * len(shapes) if several else vmem,
            out_shape=shapes,
            scratch_shapes=scratch,
            compiler_params=params(limit),
            cost_estimate=cost(1, 1),
            name=name,
        )(*args, *wait)

    def azim_flux(mine, name, limit):
        one, three = (2 * part, rows, lanes), (3, 2 * part, rows, lanes)
        return apart(
            functools.partial(azim_flux_kernel, mine),
            name,
            [half_shape, shaped(2, 3, FIELDS, part, lanes)],
            (density, velocity, pressure, azim_metric, volume),
            [pltpu.VMEM(shape, f32) for shape in (one, three, one, three, one)]
            + [flux_scratch, pltpu.SemaphoreType.DMA((2, 5))],
            limit=limit,
        )

    flux_sent, pack_sent = azim_flux(False, "azim_flux_sent", INPUT_LIMIT)
    pack_in = sibling(pack_sent, around)
    flux_in = sibling(flux_sent, around)
    flux_kept, pack_kept = azim_flux(True, "azim_flux_kept", VMEM_LIMIT)
    *packs, edge_a, edge_b = whole_call(
        functools.partial(chip_moments_kernel, rows),
        "chip_moments",
        [shaped(3 * FIELDS * part, lanes)] * 2 + [shaped(FIELDS * part, lanes)] * 2,
        (pack_kept, pack_in),
    )

    arrived = [partner(packs[turn], around, turn, 0) for turn in range(2)]
    def by_quarter(*refs):
        inputs, (own, basis, base_out, scale_out, edge_out, *scratch) = refs[:6], refs[6:]
        for step in range(4):
            here = slice(step * part, (step + 1) * part)
            pieces = [ref.at[here] if len(ref.shape) == 3 else ref.at[:, here] for ref in inputs]
            section_local_kernel(
                *pieces,
                own.at[lax.axis_index("axial")],
                basis,
                base_out.at[step : step + 1],
                scale_out.at[step : step + 1],
                edge_out.at[:, step * lines : (step + 1) * lines],
                *scratch,
            )

    base, scale, edge_d = whole_call(
        by_quarter,
        "section_local",
        [
            shaped(4, FIELDS, rows, part, lanes),
            shaped(4, rows, part, lanes),
            shaped(BASIS, 4 * lines),
        ],
        (
            density,
            velocity,
            pressure,
            axial_metric,
            volume,
            radial_term,
            jnp.asarray(own_d),
            jnp.asarray(basis_d),
        ),
        wait=(packs[0], flux_in),
        scratch=[flux_scratch] * 2,
    )
    flat = shaped(2 * (FIELDS + 1) * rows * part + 2 * FIELDS * BASIS, lanes)
    base_kept, base_sent = whole_call(
        section_split_kernel, "section_split", [flat, flat], (base, scale, edge_d)
    )
    base_in = sibling(base_sent, around)
    (edge_d,) = whole_call(
        edge_both_kernel, "edge_both", [shaped(BASIS, 4 * lines)], (base_kept, base_in)
    )
    edges_d = [swap(edge_d, "axial", along, mask) for mask in range(1, along)]
    sums_d, sends_d = ring_exchange(
        packs, arrived, [edge_a, edge_b], around, 1, part, DERIV_ROOT ** (2 * rows)
    )

    ring_d = sums_d()
    sectioned, edge_f = whole_call(
        by_chunk(
            section_join_kernel,
            [True] * 2 + [False] * 2 + [True] + [False] * (along + 1) + [True, False],
        ),
        "section_join",
        [chip_shape, shaped(BASIS, 4 * lines)],
        (
            flux_kept,
            flux_in,
            base_kept,
            base_in,
            ring_d,
            jnp.asarray(basis_f),
            jnp.asarray(far_d),
            *edges_d,
        ),
    )
    edges_f = [swap(edge_f, "axial", along, mask) for mask in range(1, along)]
    (axial_local,) = whole_call(
        by_chunk(axial_local_kernel, [True, False, True]),
        "axial_local",
        [chip_shape],
        (sectioned, jnp.asarray(own_f)),
    )
    value, chosen_rows, chosen_bins = whole_call(
        entries_kernel,
        "entries",
        [
            shaped(*weight_ids.shape),
            jax.ShapeDtypeStruct((OBSERVERS, weight_ids.size), jnp.bfloat16),
            jax.ShapeDtypeStruct((TIME_BINS, weight_ids.size), jnp.bfloat16),
        ],
        (bin_weights.reshape(-1, lanes), weight_ids, panel_area, observer_ids, bin_ids),
        wait=(edge_f,),
    )
    chips = around // 2
    height = FIELDS * part
    shapes = [4 * height + tall] * 2 + [2 * height] * 2 + [tall]
    smoothed, *packs, edge_a, edge_b, front = whole_call(
        by_chunk(axial_join_kernel, [True] + [False] * along + [True] + [False] * 5),
        "axial_join",
        [chip_shape] + [shaped(size, lanes) for size in shapes],
        (axial_local, jnp.asarray(far_f), *edges_f),
        wait=(value,),
    )
    arrived = [partner(packs[turn], around, turn, 0) for turn in range(2)]

    masks = list(range(1, chips))
    fronts = [arrived[0], None, arrived[1]] if chips == 4 else [None] * (chips - 1)
    for at, mask in enumerate(masks):
        if fronts[at] is None:
            pairs = [(i, 2 * ((i // 2) ^ mask) + i % 2) for i in range(around)]
            fronts[at] = lax.ppermute(front, "azim", pairs)
    surface, surface_sent = whole_call(
        functools.partial(surface_kernel, masks),
        "surface",
        [shaped(rows, lanes)] * 2,
        (jnp.asarray(filter_around), front, *fronts),
        scratch=[pltpu.VMEM((around * rows, lanes), f32)],
    )
    surface_in = lax.ppermute(surface_sent, "azim", [(i, i + 1) for i in range(0, around, 2)])
    sums_f, sends_f = ring_exchange(
        packs,
        arrived,
        [edge_a, edge_b],
        around,
        2,
        part,
        FILTER_ROOT ** (2 * rows),
        wait=(fronts[1],),
    )
    (partial,) = whole_call(
        signals_kernel,
        "signals",
        [shaped(OBSERVERS, TIME_BINS)],
        (surface, surface_in, value, chosen_rows, chosen_bins),
        wait=(sends_f,),
        scratch=[pltpu.VMEM((2 * TIME_BINS, weight_ids.size), jnp.bfloat16)],
    )
    shares = lax.all_to_all(
        partial.reshape(devices, OBSERVERS // devices, TIME_BINS),
        ("axial", "azim"),
        0,
        0,
        tiled=True,
    )
    (azim_local,) = whole_call(
        by_chunk(azim_local_kernel, [True, True]),
        "azim_local",
        [chip_shape],
        (smoothed,),
        wait=(sends_f,),
    )
    ring_f = sums_f((partial,))
    state_shape = shaped(FIELDS, planes, rows, lanes)
    (rows_sent,) = whole_call(
        by_chunk(azim_send_kernel, [True] * 3),
        "azim_join_sent",
        [half_shape],
        (azim_local, ring_f),
    )
    rows_in = sibling(rows_sent, around)
    mine = call(
        azim_keep_kernel,
        "azim_join_kept",
        2,
        [row_half(core_index), ring_spec(2)],
        vector(kept, FIELDS),
        state_shape,
        (azim_local, ring_f),
    )
    new_state = call(
        place_rows_kernel,
        "place_rows",
        2,
        [inner(every), spec(memory_space=pl.ANY)],
        vector(sent, FIELDS),
        state_shape,
        (rows_in, mine),
        input_output_aliases={1: 0},
    )
    shares, new_state = lax.optimization_barrier((shares, new_state))
    return new_state, jnp.sum(shares, axis=0)


def solution(mesh):
    placed = (
        P(None, "azim", "axial"),
        P(None, None, "azim", "axial"),
        P(None, "azim", "axial"),
        P(None, None, "azim", "axial"),
        P(None, None, "azim", "axial"),
        P(None, "azim", "axial"),
        P(None, None, "azim", "axial"),
        P("azim", "axial"),
        P(None, "azim", "axial"),
        P(None, "azim", "axial"),
        P(None, "azim", "axial"),
        P(),
    )
    return jax.shard_map(
        per_device,
        mesh=mesh,
        in_specs=placed,
        out_specs=(P(None, None, "azim", "axial"), P(("axial", "azim"), None)),
        check_vma=False,
    )
```

```python
import functools
import math

import jax
import jax.numpy as jnp
import numpy as np
from jax import lax
from jax.experimental import pallas as pl
from jax.experimental.pallas import tpu as pltpu
from jax.sharding import PartitionSpec as P

OBSERVERS = 512
TIME_BINS = 128

GAMMA = 1.4
SECTION = 0.25
DERIV_ALPHA = 1.0 / 3.0
FILTER_ALPHA = 0.499
FIELDS = 5
BASIS = 8
VMEM_LIMIT = 16 * 1024 * 1024
INPUT_LIMIT = 60 * 1024 * 1024


def decay_root(alpha):
    return (-1.0 + math.sqrt(1.0 - 4.0 * alpha * alpha)) / (2.0 * alpha)


DERIV_ROOT = decay_root(DERIV_ALPHA)
FILTER_ROOT = decay_root(FILTER_ALPHA)

DERIV_NEAR = 1.0 / 12.0
DERIV_FAR = (
    (25.0 / 36.0) * (DERIV_ROOT - 1.0 / DERIV_ROOT) / (1.0 + 2.0 * DERIV_ALPHA * DERIV_ROOT)
)

_B = FILTER_ALPHA
_EDGE = (1.0 - 2.0 * _B) / 64.0
_Q2 = 1.0 / _B
_Q1 = (-6.0 - _Q2) / _B
_Q0 = (12.0 - _Q1) / _B
_RHO = -8.0 - _Q0
FILTER_MID = _EDGE * (_Q0 + 2.0 * _Q2)
FILTER_ONE = _EDGE * _Q1
FILTER_TWO = _EDGE * _Q2
FILTER_FAR = _EDGE * _RHO / (1.0 + 2.0 * _B * FILTER_ROOT)


def open_operator(length, alpha, side):
    base = decay_root(alpha)
    tri = np.eye(length) + alpha * (np.eye(length, k=1) + np.eye(length, k=-1))
    tri[0, 0] = -alpha / base
    return np.linalg.solve(tri, side)


def deriv_matrix(length):
    return (7.0 / 9.0) * (np.eye(length, k=1) - np.eye(length, k=-1)) + (1.0 / 36.0) * (
        np.eye(length, k=2) - np.eye(length, k=-2)
    )


def filter_matrix(length):
    beta = FILTER_ALPHA
    coeffs = [
        (11.0 + 10.0 * beta) / 16.0,
        (15.0 + 34.0 * beta) / 32.0,
        (-3.0 + 6.0 * beta) / 16.0,
        (1.0 - 2.0 * beta) / 32.0,
    ]
    total = coeffs[0] * np.eye(length)
    for shift in range(1, 4):
        total = total + 0.5 * coeffs[shift] * (np.eye(length, k=shift) + np.eye(length, k=-shift))
    return total


def axial_tables(count, width, alpha, kind):
    length = count * width
    side = deriv_matrix(length) if kind == "deriv" else filter_matrix(length)
    whole = open_operator(length, alpha, side)
    base = decay_root(alpha)
    basis = np.zeros((BASIS, width))
    for edge in range(3):
        basis[edge, edge] = 1.0
        basis[3 + edge, width - 3 + edge] = 1.0
    basis[6] = base ** np.arange(width - 1, -1, -1, dtype=np.float64)
    basis[7] = base ** np.arange(width, dtype=np.float64)
    inverse = np.linalg.pinv(basis)
    own = np.zeros((count, width, width))
    far = np.zeros((count, max(count - 1, 1) * BASIS, width))
    for here in range(count):
        rows = whole[here * width : (here + 1) * width]
        own[here] = rows[:, here * width : (here + 1) * width].T
        if kind == "filter":
            own[here] -= np.eye(width)
        for shift in range(1, count):
            there = here ^ shift
            block = rows[:, there * width : (there + 1) * width]
            far[here, (shift - 1) * BASIS : shift * BASIS] = (block @ inverse).T
    return own, basis, far


def surface_table(around, rows):
    length = around * rows
    turn = np.roll(np.eye(length), 1, axis=1)
    beta = FILTER_ALPHA
    side = (11.0 + 10.0 * beta) / 16.0 * np.eye(length)
    coeffs = [(15.0 + 34.0 * beta) / 64.0, (-3.0 + 6.0 * beta) / 32.0, (1.0 - 2.0 * beta) / 64.0]
    for shift, weight in enumerate(coeffs, start=1):
        step = np.linalg.matrix_power(turn, shift)
        side = side + weight * (step + step.T)
    cycle = np.linalg.solve(np.eye(length) + beta * (turn + turn.T), side)
    return cycle.reshape(around // 2, 2 * rows, length).astype(np.float32)


def halves(table):
    high = np.asarray(table, np.float32).astype(jnp.bfloat16)
    low = (np.asarray(table, np.float64) - high.astype(np.float64)).astype(jnp.bfloat16)
    return np.stack([high, low], axis=-3)


def split(values):
    high = values.astype(jnp.bfloat16)
    return high, (values - high.astype(jnp.float32)).astype(jnp.bfloat16)


def dots(left, right, dims):
    out = None
    for a, b in ((0, 0), (1, 0), (0, 1)):
        part = lax.dot_general(
            left[a], right[b], (dims, ((), ())), preferred_element_type=jnp.float32
        )
        out = part if out is None else out + part
    return out


def outgoing(basis_ref, lines):
    return dots((basis_ref[0], basis_ref[1]), split(lines), ((1,), (1,)))


def incoming(parts, far_ref):
    return dots(split(jnp.concatenate(parts, axis=0)), (far_ref[0], far_ref[1]), ((0,), (0,)))


def own_block(lines, own_ref):
    return dots(split(lines), (own_ref[0], own_ref[1]), ((1,), (0,)))


def tile_energy(density, velocity, pressure):
    return pressure * (1.0 / (GAMMA - 1.0)) + 0.5 * density * (
        velocity[0] * velocity[0] + velocity[1] * velocity[1] + velocity[2] * velocity[2]
    )


def tile_flux(density, velocity, pressure, energy, metric, volume):
    contra = metric[0] * velocity[0] + metric[1] * velocity[1] + metric[2] * velocity[2]
    volume_contra = volume * contra
    mass = density * volume_contra
    push = volume * pressure
    pieces = [mass]
    for comp in range(3):
        pieces.append(mass * velocity[comp] + metric[comp] * push)
    pieces.append((energy + pressure) * volume_contra)
    return pieces


def core_index():
    return lax.rem(lax.axis_index("azim"), 2)


def chip_index():
    return lax.div(lax.axis_index("azim"), 2)


def ring_weights(chips, turn, wide):
    levels = chips.bit_length() - 1
    size = 2 * (levels + 1)
    sends = np.zeros((levels, 2, chips, size))
    sums = np.zeros((2, chips, size))
    unit = np.eye(size)
    for chip in range(chips):
        spot = (chip + turn) % chips
        head, tail = unit[0], unit[1]
        left = right = np.zeros(size)
        for level in range(levels):
            group = 1 << level
            inside = spot % group
            sends[level, :, chip] = head, tail
            head_in, tail_in = unit[2 * level + 2], unit[2 * level + 3]
            if (spot >> level) & 1:
                left = left + wide**inside * head_in
                head, tail = head + wide**group * head_in, tail_in + wide**group * tail
            else:
                right = right + wide ** (group - 1 - inside) * tail_in
                head, tail = head_in + wide**group * head, tail + wide**group * tail_in
        close = 1.0 / (1.0 - wide**chips)
        sums[0, chip] = left + close * wide**spot * head
        sums[1, chip] = right + close * wide ** (chips - 1 - spot) * tail
    return sends, sums


def chosen(index, values):
    if not np.any(values):
        return None
    out = jnp.float32(values[0])
    for at in range(1, len(values)):
        if values[at] != values[at - 1] or np.any(values != values[0]):
            out = jnp.where(index == at, jnp.float32(values[at]), out)
    return out


def slot(value, field, height):
    start = (value * FIELDS + field) * height
    return slice(start, start + height)


def mixed(chip, table, sources, field, height):
    total = None
    for at, source in enumerate(sources):
        for part in range(2):
            weight = chosen(chip, table[:, 2 * at + part])
            if weight is not None:
                term = weight * source[slot(part, field, height)]
                total = term if total is None else total + term
    return total


def moments(tiles, root):
    head = tail = tiles[0]
    for row in range(1, len(tiles)):
        head = tiles[row] + root * head
        tail = tail + (root**row) * tiles[row]
    return head, tail


def fetched(sources, buffers, sem, pieces):
    copies = [
        [
            pltpu.make_async_copy(source.at[where], buffer.at[there], sem.at[at, n])
            for n, (source, buffer, (where, there)) in enumerate(zip(sources, buffers, piece))
        ]
        for at, piece in enumerate(pieces)
    ]
    for group in copies:
        for copy in group:
            copy.start()
    return copies


def azim_flux_kernel(mine, density, velocity, pressure, azim_metric, volume, out, pack, *scratch):
    *buffers, flux, sem = scratch
    chunks, _, rows, planes, _ = out.shape
    core = core_index()
    start = (core if mine else 1 - core) * chunks * planes
    pieces = []
    for chunk in range(chunks):
        here, there = pl.ds(start + chunk * planes, planes), pl.ds(chunk * planes, planes)
        whole = slice(None)
        pieces.append(
            [(here, there), ((whole, here), (whole, there)), (here, there)]
            + [((whole, here), (whole, there)), (here, there)]
        )
    groups = fetched((density, velocity, pressure, azim_metric, volume), buffers, sem, pieces)
    first = core == 0
    for chunk in range(chunks):
        for copy in groups[chunk]:
            copy.wait()
        rho_in, vel_in, pres_in, metric_in, vol_in = buffers
        for plane in range(planes):
            at = chunk * planes + plane
            rho, pres = rho_in[at], pres_in[at]
            vel = [vel_in[c, at] for c in range(3)]
            energy = tile_energy(rho, vel, pres)
            metric = [metric_in[c, at] for c in range(3)]
            for f, piece in enumerate(tile_flux(rho, vel, pres, energy, metric, vol_in[at])):
                flux[f, plane] = piece
        for f in range(FIELDS):
            turned = jnp.swapaxes(flux[f], 0, 1)
            out[chunk, f] = turned
            tiles = [turned[row] for row in range(rows)]
            pack[chunk, 0, f], pack[chunk, 1, f] = moments(tiles, DERIV_ROOT)
            pack[chunk, 2, f] = jnp.where(first, tiles[0], tiles[rows - 1])


def put_moments(step, field, head, tail, low, high, pack, edge):
    on_left = lax.rem(chip_index() + step, 2) == 0
    height = head.shape[0]
    pack[slot(0, field, height)] = head
    pack[slot(1, field, height)] = tail
    for n in range(len(low)):
        pack[slot(2 + n, field, height)] = jnp.where(on_left, high[n], low[n])
        edge[slot(n, field, height)] = jnp.where(on_left, low[n], high[n])


def chip_moments_kernel(rows, keep, other, pack_a, pack_b, edge_a, edge_b):
    first = core_index() == 0
    decay, one = jnp.float32(DERIV_ROOT**rows), jnp.float32(1.0)
    near, away = jnp.where(first, decay, one), jnp.where(first, one, decay)
    height = keep.shape[3]
    for turn, (pack, edge) in enumerate(((pack_a, edge_a), (pack_b, edge_b))):
        on_left = lax.rem(chip_index() + turn, 2) == 0
        mine = first != on_left
        for f in range(FIELDS):
            head, tail, row = (keep[turn, n, f] for n in range(3))
            head_in, tail_in, row_in = (other[turn, n, f] for n in range(3))
            pack[slot(0, f, height)] = near * head + away * head_in
            pack[slot(1, f, height)] = away * tail + near * tail_in
            pack[slot(2, f, height)] = jnp.where(mine, row, row_in)
            edge[slot(0, f, height)] = jnp.where(mine, row_in, row)


def totals_kernel(table, joined, near, height, *refs):
    chip = chip_index()
    *refs, send_a, send_b = refs
    count = len(refs) // 2
    for turn, send in enumerate((send_a, send_b)):
        mine = refs[turn * count : (turn + 1) * count]
        sources = mine[:-1] if joined else mine
        for f in range(FIELDS):
            send[slot(0, f, height)] = mixed(chip, table[turn][0], sources, f, height)
            send[slot(1, f, height)] = mixed(chip, table[turn][1], sources, f, height)
        if joined:
            send[2 * FIELDS * height :] = mine[-1][...]


def ring_kernel(table, near, height, *refs):
    chip = chip_index()
    *refs, out = refs
    count = len(refs) // 2
    for turn in range(2):
        *sources, edge = refs[turn * count : (turn + 1) * count]
        on_left = lax.rem(chip + turn, 2) == 0
        start = 0 if edge.shape[0] == near * FIELDS * height else 2
        for f in range(FIELDS):
            out[turn, 0, f] = mixed(chip, table[turn][0], sources, f, height)
            out[turn, 1, f] = mixed(chip, table[turn][1], sources, f, height)
            for n in range(near):
                paired = sources[1][slot(2 + n, f, height)]
                other = edge[slot(start + n, f, height)]
                out[turn, 2 + n, f] = jnp.where(on_left, other, paired)
                out[turn, 2 + near + n, f] = jnp.where(on_left, paired, other)


def section_local_kernel(
    density,
    velocity,
    pressure,
    axial_metric,
    volume,
    radial,
    own,
    basis,
    base_out,
    scale_out,
    edge_out,
    axial_flux,
    start,
):
    planes, rows, lanes = density.shape
    for plane in range(planes):
        rho = density[plane]
        vel = [velocity[c, plane] for c in range(3)]
        pres = pressure[plane]
        vol = volume[plane]
        energy = tile_energy(rho, vel, pres)
        axial = tile_flux(rho, vel, pres, energy, [axial_metric[c, plane] for c in range(3)], vol)
        state = [rho, rho * vel[0], rho * vel[1], rho * vel[2], energy]
        for f in range(FIELDS):
            axial_flux[f, plane] = axial[f]
            start[f, plane] = state[f] + SECTION * radial[f, plane]
    scale = jnp.swapaxes(SECTION / volume[...], 0, 1)
    scale_out[0] = scale
    for f in range(FIELDS):
        flux = jnp.swapaxes(axial_flux[f], 0, 1).reshape(rows * planes, lanes)
        edge_out[:, f * rows * planes : (f + 1) * rows * planes] = outgoing(basis, flux)
        deriv = own_block(flux, own).reshape(rows, planes, lanes)
        base_out[0, f] = jnp.swapaxes(start[f], 0, 1) - scale * deriv


def section_split_kernel(base, scale, edge, kept, sent):
    fields, rows, planes, lanes = base.shape[1:]
    size = rows * planes
    core = core_index()
    for mine, out in ((core, kept), (1 - core, sent)):
        for chunk in range(2):
            at = 2 * mine + chunk
            for f in range(fields + 1):
                spot = (chunk * (fields + 1) + f) * size
                piece = base[at, f] if f < fields else scale[at]
                out[spot : spot + size] = piece.reshape(size, lanes)
            for f in range(fields):
                from_spot = pl.multiple_of((at * fields + f) * size, 128)
                spot = 2 * (fields + 1) * size + (chunk * fields + f) * BASIS
                out[spot : spot + BASIS] = edge[:, pl.ds(from_spot, size)]


def edge_both_kernel(kept, arrived, edge):
    lanes = kept.shape[1]
    start = kept.shape[0] - 2 * FIELDS * BASIS
    first = core_index() == 0
    for at in range(2 * FIELDS):
        piece = slice(start + at * BASIS, start + (at + 1) * BASIS)
        mine, theirs = kept[piece], arrived[piece]
        spot = 2 * at * lanes
        edge[:, spot : spot + lanes] = jnp.where(first, mine, theirs)
        edge[:, spot + lanes : spot + 2 * lanes] = jnp.where(first, theirs, mine)


def both_row(first, mine, theirs, row):
    rows = mine.shape[0]
    if row < rows:
        return jnp.where(first, mine[row], theirs[row])
    return jnp.where(first, theirs[row - rows], mine[row - rows])


def section_join_kernel(
    step, flux_keep, flux_in, base_keep, base_in, ring, basis, far, *rest
):
    *edges, out, edge = rest
    rows, planes, lanes = flux_keep.shape[2:]
    first = core_index() == 0
    last = 2 * rows - 1
    width = 2 * rows * planes
    size = rows * planes
    weights = far.at[lax.axis_index("axial")]

    def base_rows(f):
        spot = (step * (FIELDS + 1) + f) * size
        halves = [ref[spot : spot + size].reshape(rows, planes, lanes) for ref in (base_keep, base_in)]
        return [both_row(first, *halves, row) for row in range(last + 1)]

    scale = base_rows(FIELDS)
    for f in range(FIELDS):
        spot = (step * FIELDS + f) * width
        axial = incoming([ref[:, spot : spot + width] for ref in edges], weights)
        axial = axial.reshape(2 * rows, planes, lanes)
        base = base_rows(f)
        azim = [both_row(first, flux_keep[0, f], flux_in[0, f], row) for row in range(last + 1)]
        left, right, before, after = (ring[0, n, f] for n in range(4))
        down = [None] * (last + 1)
        down[last] = azim[last] + DERIV_ROOT * right
        for row in range(last - 1, -1, -1):
            down[row] = azim[row] + DERIV_ROOT * down[row + 1]
        up = left
        for row in range(last + 1):
            up = azim[row] + DERIV_ROOT * up
            total = axial[row] + DERIV_FAR * (up - down[row])
            total = total - DERIV_NEAR * (azim[row - 1] if row > 0 else before)
            total = total + DERIV_NEAR * (azim[row + 1] if row < last else after)
            out[0, f, row] = base[row] - scale[row] * total
        edge[:, spot : spot + width] = outgoing(basis, out[0, f].reshape(width, lanes))


def axial_local_kernel(step, values, own, out):
    weights = own.at[lax.axis_index("axial")]
    for f in range(FIELDS):
        lines = values[0, f].reshape(-1, values.shape[-1])
        out[0, f] = (lines + own_block(lines, weights)).reshape(out.shape[2:])


def axial_join_kernel(step, local, far, *rest):
    edges, (out, pack_a, pack_b, edge_a, edge_b, front) = rest[:-6], rest[-6:]
    pack, away = ((pack_a, edge_a), (pack_b, edge_b))[step]
    weights = far.at[lax.axis_index("axial")]
    rows, planes, lanes = local.shape[2:]
    width = rows * planes
    for f in range(FIELDS):
        spot = (step * FIELDS + f) * width
        axial = incoming([ref[:, spot : spot + width] for ref in edges], weights)
        axial = axial.reshape(rows, planes, lanes)
        tiles = [local[0, f, row] + axial[row] for row in range(rows)]
        for row in range(rows):
            out[0, f, row] = tiles[row]
        head, tail = moments(tiles, FILTER_ROOT)
        put_moments(step, f, head, tail, tiles[:2], tiles[rows - 2 :], pack, away)
    if step == 0:
        for row in range(rows):
            front[row : row + 1, :] = out[0, 2, row, 0:1, :] + out[0, 0, row, 0:1, :]
        for other in (pack_a, pack_b):
            other[other.shape[0] - rows :] = front[...]


def azim_local_kernel(step, values, out):
    rows = values.shape[2]
    for f in range(FIELDS):
        down = [None] * rows
        down[rows - 1] = values[0, f, rows - 1]
        for row in range(rows - 2, -1, -1):
            down[row] = values[0, f, row] + FILTER_ROOT * down[row + 1]
        up = None
        for row in range(rows):
            here = values[0, f, row]
            up = here if row == 0 else here + FILTER_ROOT * up
            total = (1.0 + FILTER_MID - FILTER_FAR) * here + FILTER_FAR * (up + down[row])
            for step, weight in ((1, FILTER_ONE), (2, FILTER_TWO)):
                if row >= step:
                    total = total + weight * values[0, f, row - step]
                if row + step < rows:
                    total = total + weight * values[0, f, row + step]
            out[0, f, row] = total


def joined_rows(upper, local, ring, field):
    rows = local.shape[2]
    one, zero = jnp.float32(1.0), jnp.float32(0.0)
    decay = jnp.float32(FILTER_ROOT**rows)
    left = jnp.where(upper, decay, one) * ring[0, 0, field]
    right = jnp.where(upper, one, decay) * ring[0, 1, field]
    low, high = jnp.where(upper, zero, one), jnp.where(upper, one, zero)
    before = [low * ring[0, 2 + n, field] for n in range(2)]
    after = [high * ring[0, 4 + n, field] for n in range(2)]
    tiles = []
    for row in range(rows):
        total = (
            local[0, field, row]
            + (FILTER_FAR * FILTER_ROOT ** (row + 1)) * left
            + (FILTER_FAR * FILTER_ROOT ** (rows - row)) * right
        )
        if row < 2:
            total = total + FILTER_TWO * before[row]
        if row == 0:
            total = total + FILTER_ONE * before[1]
        if row >= rows - 2:
            total = total + FILTER_TWO * after[row - (rows - 2)]
        if row == rows - 1:
            total = total + FILTER_ONE * after[0]
        tiles.append(total)
    return tiles


def azim_send_kernel(step, local, ring, out):
    rows = local.shape[2] // 2
    upper = 1 - core_index()
    there = local.at[:, :, pl.ds(upper * rows, rows)]
    for f in range(FIELDS):
        for row, tile in enumerate(joined_rows(upper == 1, there, ring, f)):
            out[0, f, row] = tile


def azim_keep_kernel(local, ring, out):
    for f in range(FIELDS):
        tiles = joined_rows(core_index() == 1, local, ring, f)
        out[f] = jnp.swapaxes(jnp.stack(tiles), 0, 1)


def place_rows_kernel(values, partial, out):
    for f in range(FIELDS):
        out[f] = jnp.swapaxes(values[0, f], 0, 1)


def entries_kernel(weight_table, weights, area, observers, bins, value, chosen_rows, chosen_bins):
    entries, rows, lanes = weights.shape
    observer_rows = lax.broadcasted_iota(jnp.int32, (chosen_rows.shape[0], lanes), 0)
    bin_rows = lax.broadcasted_iota(jnp.int32, (chosen_bins.shape[0], lanes), 0)
    for entry in range(entries):
        picked = weights[entry]
        found = jnp.zeros(picked.shape, jnp.float32)
        for part in range(weight_table.shape[0]):
            there = picked - part * lanes
            inside = (there >= 0) & (there < lanes)
            columns = jnp.broadcast_to(weight_table[part : part + 1, :], picked.shape)
            part_found = jnp.take_along_axis(columns, jnp.where(inside, there, 0), axis=1)
            found = jnp.where(inside, part_found, found)
        value[entry] = found * area[...]
        for row in range(rows):
            at = (row * entries + entry) * lanes
            hit = observer_rows == observers[entry, row : row + 1, :]
            chosen_rows[:, at : at + lanes] = jnp.where(hit, 1.0, 0.0).astype(jnp.bfloat16)
            hit = bin_rows == bins[entry, row : row + 1, :]
            chosen_bins[:, at : at + lanes] = jnp.where(hit, 1.0, 0.0).astype(jnp.bfloat16)


def surface_kernel(masks, around, front, *rest):
    *arrived, kept, sent, ring = rest
    rows = front.shape[0]
    chip = chip_index()
    for mask, ref in zip((0, *masks), (front, *arrived)):
        spot = pl.multiple_of(jnp.bitwise_xor(chip, mask) * rows, 8)
        ring[pl.ds(spot, rows), :] = ref[ref.shape[0] - rows :]
    surface = -1.0 + jnp.dot(
        around[chip],
        ring[...],
        precision=lax.Precision.HIGHEST,
        preferred_element_type=jnp.float32,
    )
    kept[...] = surface[: rows // 2]
    sent[...] = surface[rows // 2 :]


def signals_kernel(surface, surface_in, value, chosen_rows, chosen_bins, out, placed):
    entries, rows, lanes = value.shape
    height = out.shape[1]
    cells = jnp.where(core_index() == 0, surface[...], surface_in[...])
    for entry in range(entries):
        high, low = split(value[entry] * cells)
        for row in range(rows):
            at = (row * entries + entry) * lanes
            hit = chosen_bins[:, at : at + lanes]
            placed[:height, at : at + lanes] = hit * high[row : row + 1, :]
            placed[height:, at : at + lanes] = hit * low[row : row + 1, :]
    total = lax.dot_general(
        chosen_rows[...],
        placed[...],
        (((1,), (1,)), ((), ())),
        preferred_element_type=jnp.float32,
    )
    out[...] = total[:, :height] + total[:, height:]


def params(limit=VMEM_LIMIT):
    return pltpu.CompilerParams(vmem_limit_bytes=limit)


def cost(flops, moved):
    return pl.CostEstimate(flops=1, bytes_accessed=1, transcendentals=0)


def swap(values, axis, count, mask):
    return lax.ppermute(values, axis, [(i, i ^ mask) for i in range(count)])


def sibling(values, count):
    return lax.ppermute(values, "azim", [(i, i ^ 1) for i in range(count)])


def partner(values, count, turn, level):
    chips = count // 2
    pairs = []
    for i in range(count):
        chip, core = divmod(i, 2)
        there = ((((chip + turn) % chips) ^ ((2 << level) - 1)) - turn) % chips
        pairs.append((i, 2 * there + core))
    return lax.ppermute(values, "azim", pairs)


def waiting(kernel, count, wait):
    if not wait:
        return kernel
    return lambda *refs: kernel(*refs[:count], *refs[count + len(wait) :])


def by_chunk(kernel, blocked):
    def run(*refs):
        for step in range(2):
            pieces = [
                ref.at[step : step + 1] if cut else ref for ref, cut in zip(refs, blocked, strict=True)
            ]
            kernel(step, *pieces)

    return run


def whole_call(kernel, name, shapes, args, wait=(), scratch=()):
    whole = pl.BlockSpec(memory_space=pltpu.VMEM)
    return pl.pallas_call(
        waiting(kernel, len(args), wait),
        in_specs=[whole] * len(args) + [pl.BlockSpec(memory_space=pl.ANY)] * len(wait),
        out_specs=[whole] * len(shapes),
        out_shape=shapes,
        scratch_shapes=scratch,
        compiler_params=params(),
        cost_estimate=cost(1, 1),
        name=name,
    )(*args, *wait)


def ring_exchange(packs, arrived, edges, count, near, height, wide, wait=()):
    chips = count // 2
    levels = chips.bit_length() - 1
    tables = [ring_weights(chips, turn, wide) for turn in range(2)]
    lanes = packs[0].shape[1]
    rows = FIELDS * height
    joined = levels == 2
    sources = [[packs[turn], arrived[turn]] for turn in range(2)]
    if not joined:
        edges = [partner(edges[turn], count, 1 - turn, 0) for turn in range(2)]
    for level in range(1, levels):
        size = (2 + near if joined else 2) * rows
        args = [a for turn in range(2) for a in sources[turn] + ([edges[turn]] if joined else [])]
        sends = whole_call(
            functools.partial(totals_kernel, [t[0][level] for t in tables], joined, near, height),
            "group_totals",
            [jax.ShapeDtypeStruct((size, lanes), jnp.float32)] * 2,
            args,
            wait,
        )
        for turn in range(2):
            sources[turn].append(partner(sends[turn], count, turn, level))
    args = [
        a for turn in range(2) for a in sources[turn] + [sources[turn][-1] if joined else edges[turn]]
    ]

    def sums(wait=()):
        return whole_call(
            functools.partial(ring_kernel, [t[1] for t in tables], near, height),
            "ring_sums",
            [jax.ShapeDtypeStruct((2, 2 + 2 * near, FIELDS, height, lanes), jnp.float32)],
            args,
            wait,
        )[0]

    return sums, sends[0]


def per_device(
    density,
    velocity,
    pressure,
    axial_metric,
    azim_metric,
    volume,
    radial_term,
    panel_area,
    observer_ids,
    bin_ids,
    weight_ids,
    bin_weights,
):
    planes, rows, lanes = density.shape
    along = lax.axis_size("axial")
    around = lax.axis_size("azim")
    devices = along * around
    part = planes // 4
    lines = FIELDS * rows * part
    f32 = jnp.float32

    own_d, basis_d, far_d = map(halves, axial_tables(along, lanes, DERIV_ALPHA, "deriv"))
    own_f, basis_f, far_f = map(halves, axial_tables(along, lanes, FILTER_ALPHA, "filter"))
    filter_around = surface_table(around, rows)

    spec = pl.BlockSpec

    def every(k):
        return k

    def kept(k):
        return core_index() * 2 + k

    def sent(k):
        return (1 - core_index()) * 2 + k

    def field(where):
        return spec((part, rows, lanes), lambda k: (where(k), 0, 0))

    def vector(where, size=3):
        return spec((size, part, rows, lanes), lambda k: (0, where(k), 0, 0))

    def inner(where, size=FIELDS, tall=rows):
        return spec((1, size, tall, part, lanes), lambda k: (where(k), 0, 0, 0, 0))

    def inner_one(where, tall=rows):
        return spec((1, tall, part, lanes), lambda k: (where(k), 0, 0, 0))

    def edge(where, width=lines):
        return spec((BASIS, width), lambda k: (0, where(k)))

    def row_half(upper):
        return spec((1, FIELDS, rows, part, lanes), lambda k: (k, 0, upper(), 0, 0))

    def table(array):
        return spec((None,) + array.shape[1:], lambda k: (lax.axis_index("axial"),) + (0,) * (array.ndim - 1))

    def fixed(shape):
        return spec(shape, lambda k: (0,) * len(shape))

    def ring_spec(near):
        return spec((1, 2 + 2 * near, FIELDS, part, lanes), lambda k: (k, 0, 0, 0, 0))

    def shaped(*shape):
        return jax.ShapeDtypeStruct(shape, f32)

    def call(
        kernel, name, steps, ins, outs, shapes, args, wait=(), limit=VMEM_LIMIT, scratch=(), **more
    ):
        return pl.pallas_call(
            waiting(kernel, len(args), wait),
            grid=(steps,),
            in_specs=ins + [spec(memory_space=pl.ANY)] * len(wait),
            out_specs=outs,
            scratch_shapes=scratch,
            out_shape=shapes,
            compiler_params=params(limit),
            cost_estimate=cost(1, 1),
            name=name,
            **more,
        )(*args, *wait)

    tall = 2 * rows
    flux_scratch = pltpu.VMEM((FIELDS, part, rows, lanes), f32)
    half_shape = shaped(2, FIELDS, rows, part, lanes)
    chip_shape = shaped(2, FIELDS, tall, part, lanes)

    def apart(kernel, name, shapes, args, scratch, wait=(), limit=INPUT_LIMIT):
        several = isinstance(shapes, list)
        vmem = spec(memory_space=pltpu.VMEM)
        return pl.pallas_call(
            waiting(kernel, len(args), wait),
            in_specs=[spec(memory_space=pltpu.HBM)] * len(args)
            + [spec(memory_space=pl.ANY)] * len(wait),
            out_specs=[vmem] * len(shapes) if several else vmem,
            out_shape=shapes,
            scratch_shapes=scratch,
            compiler_params=params(limit),
            cost_estimate=cost(1, 1),
            name=name,
        )(*args, *wait)

    def azim_flux(mine, name, limit):
        one, three = (2 * part, rows, lanes), (3, 2 * part, rows, lanes)
        return apart(
            functools.partial(azim_flux_kernel, mine),
            name,
            [half_shape, shaped(2, 3, FIELDS, part, lanes)],
            (density, velocity, pressure, azim_metric, volume),
            [pltpu.VMEM(shape, f32) for shape in (one, three, one, three, one)]
            + [flux_scratch, pltpu.SemaphoreType.DMA((2, 5))],
            limit=limit,
        )

    flux_sent, pack_sent = azim_flux(False, "azim_flux_sent", INPUT_LIMIT)
    pack_in = sibling(pack_sent, around)
    flux_in = sibling(flux_sent, around)
    flux_kept, pack_kept = azim_flux(True, "azim_flux_kept", VMEM_LIMIT)
    *packs, edge_a, edge_b = whole_call(
        functools.partial(chip_moments_kernel, rows),
        "chip_moments",
        [shaped(3 * FIELDS * part, lanes)] * 2 + [shaped(FIELDS * part, lanes)] * 2,
        (pack_kept, pack_in),
    )

    arrived = [partner(packs[turn], around, turn, 0) for turn in range(2)]
    def by_quarter(*refs):
        inputs, (own, basis, base_out, scale_out, edge_out, *scratch) = refs[:6], refs[6:]
        kept, sent = base_out, scale_out
        base_out, scale_out, edge_out, *scratch = (edge_out, *scratch)
        for step in range(4):
            here = slice(step * part, (step + 1) * part)
            pieces = [ref.at[here] if len(ref.shape) == 3 else ref.at[:, here] for ref in inputs]
            section_local_kernel(
                *pieces,
                own.at[lax.axis_index("axial")],
                basis,
                base_out.at[step : step + 1],
                scale_out.at[step : step + 1],
                edge_out.at[:, step * lines : (step + 1) * lines],
                *scratch,
            )
        section_split_kernel(base_out, scale_out, edge_out, kept, sent)

    flat = shaped(2 * (FIELDS + 1) * rows * part + 2 * FIELDS * BASIS, lanes)
    base_kept, base_sent = whole_call(
        by_quarter,
        "section_local",
        [flat, flat],
        (
            density,
            velocity,
            pressure,
            axial_metric,
            volume,
            radial_term,
            jnp.asarray(own_d),
            jnp.asarray(basis_d),
        ),
        wait=(packs[0], flux_in),
        scratch=[
            pltpu.VMEM((4, FIELDS, rows, part, lanes), f32),
            pltpu.VMEM((4, rows, part, lanes), f32),
            pltpu.VMEM((BASIS, 4 * lines), f32),
            flux_scratch,
            flux_scratch,
        ],
    )
    base_in = sibling(base_sent, around)
    (edge_d,) = whole_call(
        edge_both_kernel, "edge_both", [shaped(BASIS, 4 * lines)], (base_kept, base_in)
    )
    edges_d = [swap(edge_d, "axial", along, mask) for mask in range(1, along)]
    sums_d, sends_d = ring_exchange(
        packs, arrived, [edge_a, edge_b], around, 1, part, DERIV_ROOT ** (2 * rows)
    )

    ring_d = sums_d()
    sectioned, edge_f = whole_call(
        by_chunk(
            section_join_kernel,
            [True] * 2 + [False] * 2 + [True] + [False] * (along + 1) + [True, False],
        ),
        "section_join",
        [chip_shape, shaped(BASIS, 4 * lines)],
        (
            flux_kept,
            flux_in,
            base_kept,
            base_in,
            ring_d,
            jnp.asarray(basis_f),
            jnp.asarray(far_d),
            *edges_d,
        ),
    )
    edges_f = [swap(edge_f, "axial", along, mask) for mask in range(1, along)]
    (axial_local,) = whole_call(
        by_chunk(axial_local_kernel, [True, False, True]),
        "axial_local",
        [chip_shape],
        (sectioned, jnp.asarray(own_f)),
    )
    value, chosen_rows, chosen_bins = whole_call(
        entries_kernel,
        "entries",
        [
            shaped(*weight_ids.shape),
            jax.ShapeDtypeStruct((OBSERVERS, weight_ids.size), jnp.bfloat16),
            jax.ShapeDtypeStruct((TIME_BINS, weight_ids.size), jnp.bfloat16),
        ],
        (bin_weights.reshape(-1, lanes), weight_ids, panel_area, observer_ids, bin_ids),
        wait=(edge_f,),
    )
    chips = around // 2
    height = FIELDS * part
    shapes = [4 * height + tall] * 2 + [2 * height] * 2 + [tall]
    smoothed, *packs, edge_a, edge_b, front = whole_call(
        by_chunk(axial_join_kernel, [True] + [False] * along + [True] + [False] * 5),
        "axial_join",
        [chip_shape] + [shaped(size, lanes) for size in shapes],
        (axial_local, jnp.asarray(far_f), *edges_f),
        wait=(value,),
    )
    arrived = [partner(packs[turn], around, turn, 0) for turn in range(2)]

    masks = list(range(1, chips))
    fronts = [arrived[0], None, arrived[1]] if chips == 4 else [None] * (chips - 1)
    for at, mask in enumerate(masks):
        if fronts[at] is None:
            pairs = [(i, 2 * ((i // 2) ^ mask) + i % 2) for i in range(around)]
            fronts[at] = lax.ppermute(front, "azim", pairs)
    surface, surface_sent = whole_call(
        functools.partial(surface_kernel, masks),
        "surface",
        [shaped(rows, lanes)] * 2,
        (jnp.asarray(filter_around), front, *fronts),
        scratch=[pltpu.VMEM((around * rows, lanes), f32)],
    )
    surface_in = lax.ppermute(surface_sent, "azim", [(i, i + 1) for i in range(0, around, 2)])
    sums_f, sends_f = ring_exchange(
        packs,
        arrived,
        [edge_a, edge_b],
        around,
        2,
        part,
        FILTER_ROOT ** (2 * rows),
        wait=(fronts[1],),
    )
    (partial,) = whole_call(
        signals_kernel,
        "signals",
        [shaped(OBSERVERS, TIME_BINS)],
        (surface, surface_in, value, chosen_rows, chosen_bins),
        wait=(sends_f,),
        scratch=[pltpu.VMEM((2 * TIME_BINS, weight_ids.size), jnp.bfloat16)],
    )
    shares = lax.all_to_all(
        partial.reshape(devices, OBSERVERS // devices, TIME_BINS),
        ("axial", "azim"),
        0,
        0,
        tiled=True,
    )
    (azim_local,) = whole_call(
        by_chunk(azim_local_kernel, [True, True]),
        "azim_local",
        [chip_shape],
        (smoothed,),
        wait=(sends_f,),
    )
    ring_f = sums_f((partial,))
    state_shape = shaped(FIELDS, planes, rows, lanes)
    (rows_sent,) = whole_call(
        by_chunk(azim_send_kernel, [True] * 3),
        "azim_join_sent",
        [half_shape],
        (azim_local, ring_f),
    )
    rows_in = sibling(rows_sent, around)
    mine = call(
        azim_keep_kernel,
        "azim_join_kept",
        2,
        [row_half(core_index), ring_spec(2)],
        vector(kept, FIELDS),
        state_shape,
        (azim_local, ring_f),
    )
    new_state = call(
        place_rows_kernel,
        "place_rows",
        2,
        [inner(every), spec(memory_space=pl.ANY)],
        vector(sent, FIELDS),
        state_shape,
        (rows_in, mine),
        input_output_aliases={1: 0},
    )
    shares, new_state = lax.optimization_barrier((shares, new_state))
    return new_state, jnp.sum(shares, axis=0)


def solution(mesh):
    placed = (
        P(None, "azim", "axial"),
        P(None, None, "azim", "axial"),
        P(None, "azim", "axial"),
        P(None, None, "azim", "axial"),
        P(None, None, "azim", "axial"),
        P(None, "azim", "axial"),
        P(None, None, "azim", "axial"),
        P("azim", "axial"),
        P(None, "azim", "axial"),
        P(None, "azim", "axial"),
        P(None, "azim", "axial"),
        P(),
    )
    return jax.shard_map(
        per_device,
        mesh=mesh,
        in_specs=placed,
        out_specs=(P(None, None, "azim", "axial"), P(("axial", "azim"), None)),
        check_vma=False,
    )
```
